32 devices in a mesh: ctx: 8 (over z, x), tp: 4 (over y, core).
Axes of the slice: x: 2, y: 2, z: 4, core: 2. Of those that a mesh axis runs over, the one named last changes fastest.
Arguments:
- tokens: bfloat16 [2048, 8192], P('ctx', 'tp'), may hold values from -6 to 6
- in_weight: bfloat16 [8192, 8192], P('ctx', 'tp'), may hold values from -0.09375 to 0.09375
- filters: float32 [2048, 8192], P('ctx', 'tp'), may hold values from -1 to 1
- gate: bfloat16 [2048, 8192], P('ctx', 'tp'), may hold values from -6 to 6
- cotangent: bfloat16 [2048, 8192], P('ctx', 'tp'), may hold values from -6 to 6
Outputs:
- gated_output: bfloat16 [2048, 8192], P('ctx', 'tp')
- grad_gate: bfloat16 [2048, 8192], P('ctx', 'tp')
- grad_tokens: bfloat16 [2048, 8192], P('ctx', 'tp')
The draws below stay inside these ranges and needn't reach their ends.
All inputs are finite; a program needn't handle non-finite values.
Results may differ from the reference program's by a relative error of at most 0.028.
Values may be sent and summed in bfloat16 or wider, within the bound.
No kernel may reach another device: no remote copies, remote signals or barrier semaphores. Data moves between devices by JAX's collectives and lax.ppermute only.
A program may use at most 192 MiB of HBM per device.

```python
import math
import jax
import jax.numpy as jnp
from jax import lax

D = 8192
LEN = 2048
CHANNELS = 2048


def draw_filters(key, part):
    key = jax.random.fold_in(key, 11)
    rate_key, rough_key = jax.random.split(key)
    lowest = 8.0
    highest = 4.0 * LEN
    scales = jnp.exp(jax.random.uniform(rate_key, (D,), jnp.float32, math.log(lowest), math.log(highest)))
    rough = jnp.clip(1.5 * jax.random.normal(rough_key, (LEN, D), jnp.float32), -1.0, 1.0)
    positions = jnp.arange(LEN, dtype=jnp.float32)[:, None]
    return jnp.exp(-positions / scales) * rough * jnp.minimum(1.0, 4.0 / jnp.sqrt(scales))


def with_spikes(values, own_key, source, target, parts, factor):
    def block_of(position):
        return (jnp.arange(values.shape[position]) // (values.shape[position] // parts)).reshape((-1,) + (1,) * (values.ndim - 1 - position))

    one_side = jax.random.permutation(own_key, parts)[block_of(target)]
    other_side = (block_of(target) + parts // 2) % parts
    return jnp.where((block_of(source) == one_side) | (block_of(source) == other_side), factor * values, values)


def block_levels(stream_key, extent, cuts, low, high):
    factor_of = 1.0
    for axis_at, parts in cuts:
        heights = jax.random.uniform(jax.random.fold_in(jax.random.fold_in(stream_key, 6), axis_at), (parts,), jnp.float32, low / len(cuts), high / len(cuts))
        factor_of = factor_of * jnp.repeat(jnp.exp(heights), extent[axis_at] // parts).reshape((-1,) + (1,) * (len(extent) - 1 - axis_at))
    return factor_of


def centred(stream_key, shape, deviation, limit, shards=(), kind=jnp.bfloat16):
    values = jax.random.normal(stream_key, shape, jnp.float32) * deviation
    if len(shards) > 0:
        values = block_levels(stream_key, shape, shards, -0.22, 0.18) * values
    return jnp.clip(values, min=-limit, max=limit).astype(kind)


def bell_draw_with(key, dims, scale, reach, cuts, heavy, held_as=jnp.bfloat16):
    values = scale * jax.random.normal(key, dims, jnp.float32)
    if cuts:
        values = values * block_levels(key, dims, cuts, -0.22, 0.18)
    return jnp.clip(with_spikes(values, jax.random.fold_in(key, 3), *heavy), -reach, reach).astype(held_as)


def setup_inputs(seed: int = 0) -> dict:
    arg_keys = jax.random.split(jax.random.key(seed), 6)
    return {
        "tokens": centred(arg_keys[0], (LEN, D), 1.0, 6.0, ((0, 8), (1, 4))),
        "in_weight": bell_draw_with(arg_keys[1], (D, D), D ** -0.5, 0.09375, ((0, 8), (1, 4)), (1, 0, 8, 2.0)),
        "filters": draw_filters(jax.random.fold_in(arg_keys[5], 71), 0),
        "gate": centred(arg_keys[3], (LEN, D), 1.0, 6.0, ((0, 8), (1, 4))),
        "cotangent": centred(arg_keys[4], (LEN, D), 1.0, 6.0, ((0, 8), (1, 4))),
    }


def reference(tokens, in_weight, filters, gate, cotangent):
    values = jnp.dot(tokens, in_weight, preferred_element_type=jnp.float32).astype(jnp.bfloat16)
    gate_wide = gate.astype(jnp.float32)
    cotangent_wide = cotangent.astype(jnp.float32)
    grad_conv = cotangent_wide * gate_wide
    padded_length = 2 * LEN
    block_count = D // CHANNELS

    def channel_blocks(array):
        return array.reshape(LEN, block_count, CHANNELS).transpose(1, 0, 2)

    def merge_blocks(array):
        return array.transpose(1, 0, 2).reshape(LEN, D)

    def convolve_block(inputs):
        values_block, filter_block, grad_block = inputs
        filter_spectrum = jnp.fft.rfft(filter_block, n=padded_length, axis=0)
        forward_spectrum = jnp.fft.rfft(values_block, n=padded_length, axis=0) * filter_spectrum
        backward_spectrum = jnp.fft.rfft(grad_block, n=padded_length, axis=0) * jnp.conj(filter_spectrum)
        convolved_block = jnp.fft.irfft(forward_spectrum, n=padded_length, axis=0)[:LEN]
        backward_block = jnp.fft.irfft(backward_spectrum, n=padded_length, axis=0)[:LEN]
        return convolved_block.astype(jnp.float32), backward_block.astype(jnp.float32)

    convolved, backward = lax.map(convolve_block, (channel_blocks(values.astype(jnp.float32)), channel_blocks(filters), channel_blocks(grad_conv)))
    convolved = merge_blocks(convolved)
    backward = merge_blocks(backward)
    gated_output = (gate_wide * convolved).astype(jnp.bfloat16)
    grad_gate = (cotangent_wide * convolved).astype(jnp.bfloat16)
    grad_values = backward.astype(jnp.bfloat16)
    weight_blocks = in_weight.reshape(D, block_count, CHANNELS).transpose(1, 0, 2)

    def accumulate(running, pieces):
        grad_block, weight_block = pieces
        product_term = lax.dot_general(grad_block, weight_block, (((1,), (1,)), ((), ())), preferred_element_type=jnp.float32)
        rounded_term = lax.optimization_barrier(product_term.astype(jnp.bfloat16))
        return running + rounded_term.astype(jnp.float32), None

    starting = jnp.zeros((LEN, D), jnp.float32)
    summed, _ = lax.scan(accumulate, starting, (channel_blocks(grad_values), weight_blocks))
    return gated_output, grad_gate, summed.astype(jnp.bfloat16)
```

```python
import functools
import math

import jax
import jax.numpy as jnp
import numpy as np
from jax import lax
from jax.experimental import pallas as pl
from jax.experimental.pallas import tpu as pltpu
from jax.sharding import Mesh, PartitionSpec as P

TWO_PI = 2.0 * math.pi
WIDE = jnp.float32
SHORT = jnp.bfloat16
LAST_TWO = (((1,), (1,)), ((), ()))


def transform_table(length):
    period = 16 * length
    fine_count = 32
    fine = jnp.arange(fine_count, dtype=jnp.int32)[:, None]
    coarse = jnp.arange(length // fine_count, dtype=jnp.int32)[:, None]
    time = 4 * jnp.arange(length, dtype=jnp.int32)[None, :] + 1
    scale = TWO_PI / period
    fine_angle = ((4 * fine + 1) * time % period).astype(WIDE) * scale
    coarse_angle = (4 * fine_count * coarse * time % period).astype(WIDE) * scale
    fine_cos, fine_sin, coarse_cos, coarse_sin = lax.optimization_barrier(
        (jnp.cos(fine_angle), jnp.sin(fine_angle), jnp.cos(coarse_angle), jnp.sin(coarse_angle))
    )
    fine_cos, fine_sin = fine_cos[None], fine_sin[None]
    coarse_cos, coarse_sin = coarse_cos[:, None], coarse_sin[:, None]
    cos_part = (coarse_cos * fine_cos - coarse_sin * fine_sin).astype(SHORT)
    sin_part = (coarse_sin * fine_cos + coarse_cos * fine_sin).astype(SHORT)
    return cos_part.reshape(length, length), sin_part.reshape(length, length)


def table_block(length):
    return min(512, length // 2)


def rotation(length):
    angle = (4 * jnp.arange(length, dtype=jnp.int32) + 1).astype(WIDE) * (TWO_PI / (16 * length))
    return jnp.stack([jnp.cos(angle), jnp.sin(angle)], axis=1)


def wide_dot(left, right):
    return jnp.dot(left, right, preferred_element_type=WIDE)


def wide_dot_turned(left, right):
    return lax.dot_general(left, right, LAST_TWO, preferred_element_type=WIDE)


def kernel_params(axes):
    return pltpu.CompilerParams(
        dimension_semantics=("arbitrary",) * axes, vmem_limit_bytes=48 * 1024 * 1024
    )


def cost(flops, bytes_accessed):
    return pl.CostEstimate(flops=flops, bytes_accessed=bytes_accessed, transcendentals=0)


ANYWHERE = pl.BlockSpec(memory_space=pl.ANY)


def waiting(kernel, count):
    return lambda index_ref, *refs: kernel(index_ref, *refs[count:])


def aligned(index, size):
    return pl.ds(pl.multiple_of(index * size, size), size)


def correlate_kernel(cos_ref, sin_ref, turn_ref, both_ref, out_ref, spectrum_ref, signal_ref, mix_ref):
    phase, step = pl.program_id(0), pl.program_id(1)
    block = cos_ref.shape[0]
    length, channels = mix_ref.shape[1:]
    rows = aligned(step, block)

    @pl.when((phase == 0) & (step == 0))
    def _():
        for which in range(2):
            signal_ref[:, which * channels : (which + 1) * channels] = both_ref[:, which].reshape(length, channels)

    @pl.when(phase == 0)
    def _():
        turn_cos, turn_sin = turn_ref[:, 0:1], turn_ref[:, 1:2]
        cos_sums = wide_dot(cos_ref[...], signal_ref[...])
        sin_sums = wide_dot(sin_ref[...], signal_ref[...])
        raw_cos, signal_cos = cos_sums[:, :channels], cos_sums[:, channels:]
        raw_sin, signal_sin = sin_sums[:, :channels], sin_sums[:, channels:]
        filter_cos = raw_cos * turn_cos + raw_sin * turn_sin
        filter_sin = raw_sin * turn_cos - raw_cos * turn_sin
        spectrum_ref[0] = filter_cos.astype(SHORT)
        spectrum_ref[1] = filter_sin.astype(SHORT)
        mix_ref[0, rows] = (signal_cos * filter_cos + signal_sin * filter_sin).astype(SHORT)
        mix_ref[1, rows] = (signal_sin * filter_cos - signal_cos * filter_sin).astype(SHORT)

    @pl.when(phase == 1)
    def _():
        total = wide_dot(cos_ref[...], mix_ref[0]) + wide_dot(sin_ref[...], mix_ref[1])
        out_ref[...] = (total * (1.0 / length)).astype(out_ref.dtype)


def correlate(table, turn, both):
    parts, _, rows, channels = both.shape
    length = parts * rows
    block = table_block(length)
    steps = length // block
    table_spec = pl.BlockSpec((block, length), lambda p, s: (s, 0))
    return pl.pallas_call(
        correlate_kernel,
        grid=(2, steps),
        in_specs=[
            table_spec,
            table_spec,
            pl.BlockSpec((block, 2), lambda p, s: (s, 0)),
            pl.BlockSpec((parts, 2, rows, channels), lambda p, s: (0, 0, 0, 0)),
        ],
        out_specs=[
            pl.BlockSpec((block, channels), lambda p, s: (p * s, 0)),
            pl.BlockSpec((2, block, channels), lambda p, s: (0, s + p * (steps - 1 - s), 0)),
        ],
        out_shape=[
            jax.ShapeDtypeStruct((length, channels), SHORT),
            jax.ShapeDtypeStruct((2, length, channels), SHORT),
        ],
        scratch_shapes=[pltpu.VMEM((length, 2 * channels), SHORT), pltpu.VMEM((2, length, channels), SHORT)],
        compiler_params=kernel_params(2),
        cost_estimate=cost(12 * length * length * channels, 8 * length * length),
    )(table[0], table[1], turn, both)


def convolve_kernel(inner, places_ref, cos_ref, sin_ref, spectrum_ref, *refs):
    part_refs, (out_ref, signal_ref, mix_ref) = refs[:inner], refs[inner:]
    phase, step = pl.program_id(0), pl.program_id(1)
    block = cos_ref.shape[0]
    length = signal_ref.shape[0]
    rows = aligned(step, block)
    pieces = places_ref.shape[1]
    size = part_refs[0].shape[0] // pieces

    @pl.when((phase == 0) & (step == 0))
    def _():
        for s in range(inner):
            for p in range(pieces):
                signal_ref[aligned(places_ref[s, p], size)] = part_refs[s][p * size : (p + 1) * size]

    @pl.when(phase == 0)
    def _():
        filter_cos, filter_sin = spectrum_ref[0].astype(WIDE), spectrum_ref[1].astype(WIDE)
        signal_cos = wide_dot(cos_ref[...], signal_ref[...])
        signal_sin = wide_dot(sin_ref[...], signal_ref[...])
        mix_ref[0, rows] = (signal_cos * filter_cos - signal_sin * filter_sin).astype(SHORT)
        mix_ref[1, rows] = (signal_cos * filter_sin + signal_sin * filter_cos).astype(SHORT)

    @pl.when(phase == 1)
    def _():
        total = wide_dot(cos_ref[...], mix_ref[0]) + wide_dot(sin_ref[...], mix_ref[1])
        out_ref[...] = (total * (1.0 / length)).astype(out_ref.dtype)


def convolve(table, spectrum, parts, places):
    length, channels = spectrum.shape[1:]
    block = table_block(length)
    steps = length // block
    table_spec = pl.BlockSpec((block, length), lambda p, s, _: (s, 0))
    return pl.pallas_call(
        functools.partial(convolve_kernel, len(parts)),
        grid_spec=pltpu.PrefetchScalarGridSpec(
            num_scalar_prefetch=1,
            grid=(2, steps),
            in_specs=[
                table_spec,
                table_spec,
                pl.BlockSpec((2, block, channels), lambda p, s, _: (0, s + p * (steps - 1 - s), 0)),
            ]
            + [pl.BlockSpec(part.shape, lambda p, s, _: (0, 0)) for part in parts],
            out_specs=pl.BlockSpec((block, channels), lambda p, s, _: (p * s, 0)),
            scratch_shapes=[pltpu.VMEM((length, channels), SHORT), pltpu.VMEM((2, length, channels), SHORT)],
        ),
        out_shape=jax.ShapeDtypeStruct((length, channels), SHORT),
        compiler_params=kernel_params(2),
        cost_estimate=cost(8 * length * length * channels, 8 * length * length),
    )(places, table[0], table[1], spectrum, *parts)


def prepare_kernel(index_ref, filters_ref, gate_ref, cotangent_ref, out_ref):
    out_ref[0, 0] = filters_ref[...].astype(SHORT)
    out_ref[0, 1] = (cotangent_ref[...].astype(WIDE) * gate_ref[...].astype(WIDE)).astype(SHORT)


def prepare(filters, gate, cotangent, groups, waits):
    rows, width = filters.shape
    channels = width // groups
    if channels % 128:
        both = jnp.stack([filters, cotangent.astype(WIDE) * gate.astype(WIDE)]).astype(SHORT)
        return both.reshape(2, rows, groups, channels).transpose(2, 0, 1, 3)
    spec = pl.BlockSpec((rows, channels), lambda g: (0, g))
    return pl.pallas_call(
        waiting(prepare_kernel, len(waits)),
        grid=(groups,),
        in_specs=[pl.BlockSpec(memory_space=pltpu.SMEM)] + [ANYWHERE] * len(waits) + [spec] * 3,
        out_specs=pl.BlockSpec((1, 2, rows, channels), lambda g: (g, 0, 0, 0)),
        out_shape=jax.ShapeDtypeStruct((groups, 2, rows, channels), SHORT),
        compiler_params=kernel_params(1),
        cost_estimate=cost(2 * rows * width, 12 * rows * width),
    )(jnp.zeros((1,), jnp.int32), *waits, filters, gate, cotangent)


def finish_kernel(convolved_ref, gate_ref, cotangent_ref, output_ref, grad_ref):
    convolved = convolved_ref[0].astype(WIDE)
    output_ref[...] = (gate_ref[...].astype(WIDE) * convolved).astype(SHORT)
    grad_ref[...] = (cotangent_ref[...].astype(WIDE) * convolved).astype(SHORT)


def finish(convolved, gate, cotangent):
    groups, rows, channels = convolved.shape
    width = groups * channels
    if channels % 128:
        wide = convolved.swapaxes(0, 1).reshape(rows, width).astype(WIDE)
        return [(other.astype(WIDE) * wide).astype(SHORT) for other in (gate, cotangent)]
    spec = pl.BlockSpec((rows, channels), lambda g: (0, g))
    return pl.pallas_call(
        finish_kernel,
        grid=(groups,),
        in_specs=[pl.BlockSpec((1, rows, channels), lambda g: (g, 0, 0)), spec, spec],
        out_specs=[spec, spec],
        out_shape=[jax.ShapeDtypeStruct((rows, width), SHORT)] * 2,
        compiler_params=kernel_params(1),
        cost_estimate=cost(2 * rows * width, 10 * rows * width),
    )(convolved, gate, cotangent)


def arrange_kernel(dims, index_ref, *refs):
    outer, inner, far, near, halves, half_rows = dims
    part_refs, out_refs = refs[:inner], refs[inner:]
    channels = part_refs[0].shape[-1]
    tp = far * near
    for s in range(inner):
        lanes = aligned(index_ref[s], channels)
        for ahead in range(tp):
            source = index_ref[inner + ahead]
            for o in range(outer):
                for h in range(halves):
                    place = (ahead * outer + o) * half_rows
                    piece = part_refs[s][o, aligned(source * halves + h, half_rows)]
                    out_refs[h][place : place + half_rows, lanes] = piece


def arrange(parts, inner_places, sources, dims, waits):
    outer, inner, far, near, halves, half_rows = dims
    channels = parts[0].shape[-1]
    tp = far * near
    shape = (tp * outer * half_rows, inner * channels)
    if channels % 128:
        slots = jnp.zeros((inner, *parts[0].shape), SHORT)
        for s in range(inner):
            slots = lax.dynamic_update_index_in_dim(slots, parts[s], inner_places[s], 0)
        slots = slots.reshape(inner, outer, tp, halves, half_rows, channels).transpose(2, 3, 1, 4, 0, 5)
        slots = jnp.stack([pick(slots, sources[a]) for a in range(tp)])
        return [slots[:, h].reshape(shape) for h in range(halves)]
    index = jnp.concatenate([inner_places, sources]).astype(jnp.int32)
    size = math.prod(shape) * 2
    return pl.pallas_call(
        waiting(functools.partial(arrange_kernel, dims), len(waits)),
        in_specs=[pl.BlockSpec(memory_space=pltpu.SMEM)]
        + [ANYWHERE] * len(waits)
        + [pl.BlockSpec(memory_space=pltpu.VMEM)] * inner,
        out_specs=[pl.BlockSpec(memory_space=pltpu.VMEM)] * halves,
        out_shape=[jax.ShapeDtypeStruct(shape, SHORT)] * halves,
        compiler_params=kernel_params(0),
        cost_estimate=cost(0, 2 * halves * size),
    )(index, *waits, *parts)


def assemble_kernel(dims, index_ref, *refs):
    halves, steps, blocks, half_rows, depth = dims
    out_ref = refs[-1]
    for h in range(halves):
        for s in range(steps):
            rows = aligned(index_ref[s] * halves + h, half_rows)
            for b in range(blocks):
                out_ref[rows, aligned(index_ref[steps + b], depth)] = refs[h * steps + s][b]


def assemble(pieces, row_places, block_places, columns):
    halves, steps = len(pieces), len(pieces[0])
    blocks, half_rows, depth = pieces[0][0].shape
    flat = [piece for half in pieces for piece in half]
    rows = halves * steps * half_rows
    return pl.pallas_call(
        functools.partial(assemble_kernel, (halves, steps, blocks, half_rows, depth)),
        in_specs=[pl.BlockSpec(memory_space=pltpu.SMEM)] + [pl.BlockSpec(memory_space=pltpu.VMEM)] * len(flat),
        out_specs=pl.BlockSpec(memory_space=pltpu.VMEM),
        out_shape=jax.ShapeDtypeStruct((rows, columns), SHORT),
        compiler_params=kernel_params(0),
        cost_estimate=cost(0, 4 * rows * columns),
    )(jnp.concatenate([row_places, block_places]).astype(jnp.int32), *flat)


def chunk_kernel(index_ref, in_ref, out_ref):
    out_ref[...] = in_ref[...]


def chunk_of(array, index, count):
    rows, width = array.shape
    chunk = width // count
    block = min(rows, 256)
    if chunk % 128:
        return lax.dynamic_slice_in_dim(array, index * chunk, chunk, 1)
    return pl.pallas_call(
        chunk_kernel,
        grid_spec=pltpu.PrefetchScalarGridSpec(
            num_scalar_prefetch=1,
            grid=(rows // block,),
            in_specs=[pl.BlockSpec((block, chunk), lambda r, index: (r, index[0]))],
            out_specs=pl.BlockSpec((block, chunk), lambda r, _: (r, 0)),
        ),
        out_shape=jax.ShapeDtypeStruct((rows, chunk), array.dtype),
        compiler_params=kernel_params(1),
        cost_estimate=cost(0, 4 * rows * chunk),
    )(index[None].astype(jnp.int32), array)


def join_kernel(index_ref, *refs):
    size = refs[0].shape[0]
    for p, ref in enumerate(refs[:-1]):
        refs[-1][p * size : (p + 1) * size] = ref[...]


def join(parts, waits):
    size, width = parts[0].shape
    rows = len(parts) * size
    if size % 16:
        return jnp.concatenate(parts, axis=0)
    return pl.pallas_call(
        waiting(join_kernel, len(waits)),
        in_specs=[pl.BlockSpec(memory_space=pltpu.SMEM)]
        + [ANYWHERE] * len(waits)
        + [pl.BlockSpec(memory_space=pltpu.VMEM)] * len(parts),
        out_specs=pl.BlockSpec(memory_space=pltpu.VMEM),
        out_shape=jax.ShapeDtypeStruct((rows, width), parts[0].dtype),
        compiler_params=kernel_params(0),
        cost_estimate=cost(0, 4 * rows * width),
    )(jnp.zeros((1,), jnp.int32), *waits, *parts)


def product_kernel(dims, index_ref, *refs):
    inner, outer, pieces, depth, add = dims
    token_refs, weight_refs, out_ref = refs[:pieces], refs[pieces : pieces + inner], refs[-1]
    size = token_refs[0].shape[0] // outer
    parts = [aligned(index_ref[2 + inner + s], size) for s in range(outer)]
    total = refs[-2][...].astype(WIDE) if add else 0.0
    for i in range(inner):
        columns = aligned(index_ref[2 + i], depth)
        tokens = jnp.concatenate([ref[rows, columns] for ref in token_refs for rows in parts], axis=0)
        total = total + wide_dot(tokens, weight_refs[i][...])
    out_ref[...] = total.astype(SHORT).reshape(out_ref.shape)


def product(pieces, in_weight, chunk_index, received, inner_blocks, row_order, running, last, waits):
    inner = len(received) + 1
    outer = row_order.shape[0]
    depth, width = in_weight.shape
    chunk = width // outer
    channels = chunk // inner
    size, whole_depth = pieces[0].shape
    rows = len(pieces) * size
    at_inner = inner_blocks[0]
    if channels % 128:
        tokens = jnp.stack(pieces).reshape(len(pieces), outer, size // outer, whole_depth)
        tokens = jnp.concatenate([pick(tokens, row_order[s], 1)[:, None] for s in range(outer)], axis=1)
        tokens = tokens.reshape(rows, whole_depth)
        weights = [chunk_of(in_weight, chunk_index, outer)] + received
        total = sum(
            wide_dot(lax.dynamic_slice_in_dim(tokens, inner_blocks[i] * depth, depth, 1), weights[i])
            for i in range(inner)
        )
        if running is not None:
            total = total + running.astype(WIDE)
        total = total.astype(SHORT)
        if last:
            total = total.reshape(rows, inner, channels)
            total = jnp.stack([pick(total, (at_inner + i) % inner, 1) for i in range(inner)])
        return total
    if last:
        out_spec = pl.BlockSpec((1, rows, channels), lambda g, index: ((g + inner - index[2]) % inner, 0, 0))
        out_shape = (inner, rows, channels)
    else:
        out_spec = pl.BlockSpec((rows, channels), lambda g, _: (0, g))
        out_shape = (rows, chunk)
    block = pl.BlockSpec((depth, channels), lambda g, _: (0, g))
    index = jnp.concatenate([chunk_index[None], at_inner[None], inner_blocks, row_order]).astype(jnp.int32)
    return pl.pallas_call(
        waiting(
            functools.partial(product_kernel, (inner, outer, len(pieces), depth, running is not None)), len(waits)
        ),
        grid_spec=pltpu.PrefetchScalarGridSpec(
            num_scalar_prefetch=1,
            grid=(inner,),
            in_specs=[ANYWHERE] * len(waits)
            + [pl.BlockSpec((size, whole_depth), lambda g, _: (0, 0)) for _ in pieces]
            + [pl.BlockSpec((depth, channels), lambda g, index: (0, index[0] * inner + g))]
            + [block for _ in received]
            + ([] if running is None else [pl.BlockSpec((rows, channels), lambda g, _: (0, g))]),
            out_specs=out_spec,
        ),
        out_shape=jax.ShapeDtypeStruct(out_shape, SHORT),
        compiler_params=kernel_params(1),
        cost_estimate=cost(2 * rows * whole_depth * chunk, 2 * (rows + chunk) * whole_depth + 4 * rows * chunk),
    )(index, *waits, *pieces, in_weight, *received, *([] if running is None else [running]))


def shares_kernel(dims, index_ref, grad_ref, *refs):
    outer, inner, near, chunk = dims
    own_ref, received_refs = refs[0], refs[1 : 1 + (inner - 1) * outer]
    out_refs, plain_ref = refs[1 + (inner - 1) * outer : -1], refs[-1]
    size = out_refs[0].shape[1]

    @pl.when(pl.program_id(0) == 0)
    def _():
        for o in range(outer):
            plain_ref[:, o * chunk : (o + 1) * chunk] = grad_ref[o]

    for i in range(inner):
        if i == 0:
            total = wide_dot_turned(plain_ref[...], own_ref[...])
        else:
            total = sum(
                wide_dot_turned(grad_ref[index_ref[s]], received_refs[(i - 1) * outer + s][...]) for s in range(outer)
            )
        total = total.astype(SHORT)
        for n in range(near):
            out_refs[n][i] = total[n * size : (n + 1) * size]


def shares(grad_values, in_weight, received, chunks, near, waits):
    outer, rows, chunk = grad_values.shape
    inner = len(received) + 1
    depth, width = in_weight.shape
    if chunk // inner % 128:
        plain = grad_values.swapaxes(0, 1).reshape(rows, width)
        totals = [wide_dot_turned(plain, in_weight)] + [
            sum(wide_dot_turned(pick(grad_values, chunks[s]), held[s]) for s in range(outer)) for held in received
        ]
        total = jnp.stack(totals).astype(SHORT).reshape(inner, near, rows // near, depth)
        return [total[:, n] for n in range(near)]
    block = min(depth, 256)
    flat = [w for held in received for w in held]
    out_spec = pl.BlockSpec((inner, rows // near, block), lambda k, _: (0, 0, k))
    return pl.pallas_call(
        waiting(functools.partial(shares_kernel, (outer, inner, near, chunk)), len(waits)),
        grid_spec=pltpu.PrefetchScalarGridSpec(
            num_scalar_prefetch=1,
            grid=(depth // block,),
            in_specs=[ANYWHERE] * len(waits)
            + [pl.BlockSpec((outer, rows, chunk), lambda k, _: (0, 0, 0))]
            + [pl.BlockSpec((block, width), lambda k, _: (k, 0))]
            + [pl.BlockSpec((block, chunk), lambda k, _: (k, 0)) for _ in flat],
            out_specs=[out_spec] * near,
            scratch_shapes=[pltpu.VMEM((rows, width), SHORT)],
        ),
        out_shape=[jax.ShapeDtypeStruct((inner, rows // near, depth), SHORT)] * near,
        compiler_params=kernel_params(1),
        cost_estimate=cost(
            2 * rows * width * inner * depth, 2 * (inner * depth + rows) * width + 2 * rows * inner * depth
        ),
    )(chunks.astype(jnp.int32), *waits, grad_values, in_weight, *flat)


def shifted(array, axis, shift):
    size = lax.axis_size(axis)
    return lax.ppermute(array, axis, [(at, (at + shift) % size) for at in range(size)])


def pick(array, index, axis=0):
    return lax.dynamic_index_in_dim(array, index, axis, keepdims=False)


def turned(parts, start):
    count = len(parts)
    backwards = jnp.stack(parts[::-1])
    doubled = jnp.concatenate([backwards, backwards], axis=0)
    return lax.dynamic_slice_in_dim(doubled, (count - 1 - start) % count, count, 0)


def per_device(tokens, in_weight, filters, gate, cotangent):
    outer, inner, far, near = (lax.axis_size(a) for a in ("outer", "inner", "far", "near"))
    at_outer, at_inner, at_far, at_near = (lax.axis_index(a) for a in ("outer", "inner", "far", "near"))
    tp = far * near
    at_tp = at_far * near + at_near
    rows, columns = tokens.shape
    fine_rows = rows // tp
    halves = 2 if fine_rows >= 32 else 1
    half_rows = fine_rows // halves
    ctx = ("outer", "inner")
    ctx_size = outer * inner
    cell = ("outer", "far", "near")
    split = tp // outer
    depth, width = in_weight.shape
    channels = width // ctx_size
    tile_blocks = columns // depth
    length = ctx_size * rows
    back_inner = [(at_inner - i) % inner for i in range(inner)]

    def destination(source_outer, source_tp, step):
        part = (source_outer * split + source_tp % split + step) % tp
        return (source_tp // split) * tp + part

    chunks = [(at_outer - s) % outer for s in range(outer)]
    order = [s % outer for s in range(1, outer + 1)]
    received = [[None] * outer for _ in range(1, inner)]
    for s in order:
        sent = chunk_of(in_weight, chunks[s], outer)
        for i in range(1, inner):
            received[i - 1][s] = shifted(sent, "inner", i)

    moved = []
    if split == 1:
        by_far = tokens.reshape(far, near * fine_rows, columns)
        held = [pick(by_far, at_far)] + [shifted(pick(by_far, (at_far + f) % far), "far", f) for f in range(1, far)]
        held = jnp.stack(held).reshape(far, near, fine_rows, columns)
        for step in range(tp):
            pairs = []
            for o in range(outer):
                for g in range(far):
                    for c in range(near):
                        tile, part = (o + step) % tp // near, (o + step) % tp % near
                        pairs.append(((o * far + g) * near + c, ((tile * near + c) * far + g) * near + part))
            number = (at_outer + step) % tp
            part = lax.dynamic_slice(
                held, ((at_far - number // near) % far, number % near, 0, 0), (1, 1, fine_rows, columns)
            )
            moved.append(lax.ppermute(part.reshape(fine_rows, columns), cell, pairs))
        token_part = join(moved, [held[s] for held in received for s in order[:2]])
    else:
        row_parts = tokens.reshape(tp, fine_rows, columns)
        for step in range(tp):
            pairs = [(o * tp + t, destination(o, t, step)) for o in range(outer) for t in range(tp)]
            part = (at_outer * split + at_tp % split + step) % tp
            moved.append(lax.ppermute(pick(row_parts, part), cell, pairs))
        token_part = turned(moved, at_tp).reshape(outer, split, fine_rows, columns).swapaxes(1, 2)
        token_part = token_part.reshape(outer * fine_rows, split * columns)

    prepared = prepare(filters, gate, cotangent, ctx_size, [token_part])
    channel_rows = lax.all_to_all(prepared, ctx, split_axis=0, concat_axis=0, tiled=True)
    table = transform_table(length)

    pieces = [token_part] + [shifted(token_part, "far", f) for f in range(1, far)]
    pieces = pieces + [shifted(piece, "near", n) for n in range(1, near) for piece in pieces]
    places = []
    for n in range(near):
        for f in range(far):
            source_near = (at_near - n) % near
            source = (at_far - f) % far * near + source_near
            for s in range(outer):
                source_outer = (source_near - s) % outer if split == 1 else s
                places.append(source_outer * (inner * tp) + source)
    places = jnp.stack(places).astype(jnp.int32)
    places = jnp.stack([places + back_inner[s] * tp for s in range(inner)])

    grad_values, spectrum = correlate(table, rotation(length), channel_rows)
    by_inner = grad_values.reshape(outer, inner, rows, channels)
    grad_parts = [pick(by_inner, at_inner, 1)]
    for i in range(1, inner):
        grad_parts.append(shifted(pick(by_inner, (at_inner + i) % inner, 1), "inner", i))
    blocks = jnp.stack(back_inner)
    turn = at_outer // near * near if split == 1 else 0
    row_order = jnp.stack([(s + turn) % outer + at_outer * 0 for s in range(outer)])
    running = None
    for s in order:
        if running is not None:
            running = shifted(running, "outer", 1)
        held = [chunk[s] for chunk in received]
        waits = [chunk[(s + 1) % outer] for chunk in received if s != 0]
        if s == 1:
            waits = waits + list(table)
        if s == outer - 1:
            waits = waits + [spectrum]
        if s == 0:
            waits = waits + grad_parts
        running = product(pieces, in_weight, chunks[s], held, blocks, row_order, running, s == 0, waits)
    value_parts = [running[0]] + [shifted(running[i], "inner", i) for i in range(1, inner)]

    sources = [(at_far + f) % far * near + (at_near + n) % near for n in range(near) for f in range(far)]
    arranged = arrange(
        grad_parts, jnp.stack(back_inner), jnp.stack(sources), (outer, inner, far, near, halves, half_rows), [running]
    )

    convolved = convolve(table, spectrum, value_parts, places).reshape(ctx_size, rows, channels)

    sent_back = []
    waits = [convolved]
    for half in arranged:
        gathered = lax.all_gather(half, "outer", axis=0, tiled=False)
        by_near = shares(gathered, in_weight, received, jnp.stack(chunks), near, waits)
        total = by_near[0].astype(WIDE) + sum(shifted(by_near[n], "near", n).astype(WIDE) for n in range(1, near))
        total = total.astype(SHORT).reshape(inner, far, outer * half_rows, depth)
        total = total[:, 0].astype(WIDE) + sum(shifted(total[:, f], "far", f).astype(WIDE) for f in range(1, far))
        total = total.astype(SHORT).reshape(inner, outer, half_rows, depth)
        if split == 1:
            total = total.swapaxes(0, 1)
        else:
            total = turned(list(total), at_inner).reshape(split, tile_blocks, outer, half_rows, depth)
            total = total.transpose(2, 0, 1, 3, 4).reshape(tp, tile_blocks, half_rows, depth)
        back = []
        for step in range(tp):
            pairs = [(destination(o, t, step), o * tp + t) for o in range(outer) for t in range(tp)]
            back.append(lax.ppermute(pick(total, (at_tp - step) % tp), cell, pairs))
        sent_back.append(back)
        waits = back
    row_places = [(at_outer * split + at_tp % split + step) % tp for step in range(tp)]
    block_places = back_inner if split == 1 else [jnp.int32(b) for b in range(tile_blocks)]
    grad_tokens = assemble(sent_back, jnp.stack(row_places), jnp.stack(block_places), columns)

    convolved = lax.all_to_all(convolved, ctx, split_axis=0, concat_axis=0, tiled=True)
    gated_output, grad_gate = finish(convolved, gate, cotangent)
    return (gated_output, grad_gate, grad_tokens)


def solution(mesh):
    ctx_size, tp_size = mesh.shape["ctx"], mesh.shape["tp"]
    inner, near = 1, 2
    while inner * inner * 4 <= ctx_size:
        inner *= 2
    fine_mesh = Mesh(
        np.asarray(mesh.devices).reshape(ctx_size // inner, inner, tp_size // near, near),
        ("outer", "inner", "far", "near"),
    )
    placed = P(("outer", "inner"), ("far", "near"))
    return jax.shard_map(
        per_device,
        mesh=fine_mesh,
        in_specs=(placed,) * 5,
        out_specs=(placed,) * 3,
        check_vma=False,
    )
```

```python
import functools
import math

import jax
import jax.numpy as jnp
import numpy as np
from jax import lax
from jax.experimental import pallas as pl
from jax.experimental.pallas import tpu as pltpu
from jax.sharding import Mesh, PartitionSpec as P

TWO_PI = 2.0 * math.pi
WIDE = jnp.float32
SHORT = jnp.bfloat16
LAST_TWO = (((1,), (1,)), ((), ()))


def transform_table(length):
    period = 16 * length
    if length > 2048:
        points = 4 * jnp.arange(length, dtype=jnp.int32) + 1
        angles = (points[:, None] * points[None, :] % period).astype(WIDE) * (TWO_PI / period)
        return [jnp.cos(angles).astype(SHORT), jnp.sin(angles).astype(SHORT)]
    points = 4 * np.arange(length, dtype=np.int64) + 1
    turns = points[:, None] * points[None, :] % period
    angles = np.arange(period) * (TWO_PI / period)
    return [jnp.asarray(wave(angles).astype(SHORT)[turns]) for wave in (np.cos, np.sin)]


def table_block(length):
    return min(512, length // 2)


def rotation(length):
    angle = (4 * jnp.arange(length, dtype=jnp.int32) + 1).astype(WIDE) * (TWO_PI / (16 * length))
    return jnp.stack([jnp.cos(angle), jnp.sin(angle)], axis=1)


def wide_dot(left, right):
    return jnp.dot(left, right, preferred_element_type=WIDE)


def wide_dot_turned(left, right):
    return lax.dot_general(left, right, LAST_TWO, preferred_element_type=WIDE)


def kernel_params(axes):
    return pltpu.CompilerParams(
        dimension_semantics=("arbitrary",) * axes, vmem_limit_bytes=48 * 1024 * 1024
    )


NO_COST = pl.CostEstimate(flops=0, bytes_accessed=0, transcendentals=0)


ANYWHERE = pl.BlockSpec(memory_space=pl.ANY)


def waiting(kernel, count):
    return lambda index_ref, *refs: kernel(index_ref, *refs[count:])


def release_kernel(index_ref, in_ref, out_ref):
    pass


def release(array, waits):
    return pl.pallas_call(
        waiting(release_kernel, len(waits)),
        in_specs=[pl.BlockSpec(memory_space=pltpu.SMEM)] + [ANYWHERE] * (len(waits) + 1),
        out_specs=ANYWHERE,
        out_shape=jax.ShapeDtypeStruct(array.shape, array.dtype),
        input_output_aliases={1 + len(waits): 0},
        compiler_params=kernel_params(0),
        cost_estimate=NO_COST,
    )(jnp.zeros((1,), jnp.int32), *waits, array)


def aligned(index, size):
    return pl.ds(pl.multiple_of(index * size, size), size)


def correlate_kernel(index_ref, cos_ref, sin_ref, turn_ref, both_ref, out_ref, spectrum_ref, signal_ref, mix_ref):
    phase, step = pl.program_id(0), pl.program_id(1)
    block = cos_ref.shape[0]
    length, channels = mix_ref.shape[1:]
    rows = aligned(step, block)

    @pl.when((phase == 0) & (step == 0))
    def _():
        for which in range(2):
            signal_ref[:, which * channels : (which + 1) * channels] = both_ref[:, which].reshape(length, channels)

    @pl.when(phase == 0)
    def _():
        turn_cos, turn_sin = turn_ref[:, 0:1], turn_ref[:, 1:2]
        cos_sums = wide_dot(cos_ref[...], signal_ref[...])
        sin_sums = wide_dot(sin_ref[...], signal_ref[...])
        raw_cos, signal_cos = cos_sums[:, :channels], cos_sums[:, channels:]
        raw_sin, signal_sin = sin_sums[:, :channels], sin_sums[:, channels:]
        filter_cos = raw_cos * turn_cos + raw_sin * turn_sin
        filter_sin = raw_sin * turn_cos - raw_cos * turn_sin
        spectrum_ref[0] = filter_cos.astype(SHORT)
        spectrum_ref[1] = filter_sin.astype(SHORT)
        mix_ref[0, rows] = (signal_cos * filter_cos + signal_sin * filter_sin).astype(SHORT)
        mix_ref[1, rows] = (signal_sin * filter_cos - signal_cos * filter_sin).astype(SHORT)

    @pl.when(phase == 1)
    def _():
        total = wide_dot(cos_ref[...], mix_ref[0]) + wide_dot(sin_ref[...], mix_ref[1])
        out_ref[...] = (total * (1.0 / length)).astype(out_ref.dtype)


def correlate(table, turn, both, waits):
    parts, _, rows, channels = both.shape
    length = parts * rows
    block = table_block(length)
    steps = length // block
    table_spec = pl.BlockSpec((block, length), lambda p, s: (s, 0))
    return pl.pallas_call(
        waiting(correlate_kernel, len(waits)),
        grid=(2, steps),
        in_specs=[
            pl.BlockSpec(memory_space=pltpu.SMEM),
            *[ANYWHERE] * len(waits),
            table_spec,
            table_spec,
            pl.BlockSpec((block, 2), lambda p, s: (s, 0)),
            pl.BlockSpec((parts, 2, rows, channels), lambda p, s: (0, 0, 0, 0)),
        ],
        out_specs=[
            pl.BlockSpec((block, channels), lambda p, s: (p * s, 0)),
            pl.BlockSpec((2, block, channels), lambda p, s: (0, s + p * (steps - 1 - s), 0)),
        ],
        out_shape=[
            jax.ShapeDtypeStruct((length, channels), SHORT),
            jax.ShapeDtypeStruct((2, length, channels), SHORT),
        ],
        scratch_shapes=[pltpu.VMEM((length, 2 * channels), SHORT), pltpu.VMEM((2, length, channels), SHORT)],
        compiler_params=kernel_params(2),
        cost_estimate=NO_COST,
    )(jnp.zeros((1,), jnp.int32), *waits, table[0], table[1], turn, both)


def convolve_kernel(inner, places_ref, cos_ref, sin_ref, spectrum_ref, *refs):
    part_refs, (out_ref, signal_ref, mix_ref) = refs[:inner], refs[inner:]
    phase, step = pl.program_id(0), pl.program_id(1)
    block = cos_ref.shape[0]
    length = signal_ref.shape[0]
    rows = aligned(step, block)
    pieces = places_ref.shape[1]
    size = part_refs[0].shape[0] // pieces

    @pl.when((phase == 0) & (step == 0))
    def _():
        for s in range(inner):
            for p in range(pieces):
                signal_ref[aligned(places_ref[s, p], size)] = part_refs[s][p * size : (p + 1) * size]

    @pl.when(phase == 0)
    def _():
        filter_cos, filter_sin = spectrum_ref[0].astype(WIDE), spectrum_ref[1].astype(WIDE)
        signal_cos = wide_dot(cos_ref[...], signal_ref[...])
        signal_sin = wide_dot(sin_ref[...], signal_ref[...])
        mix_ref[0, rows] = (signal_cos * filter_cos - signal_sin * filter_sin).astype(SHORT)
        mix_ref[1, rows] = (signal_cos * filter_sin + signal_sin * filter_cos).astype(SHORT)

    @pl.when(phase == 1)
    def _():
        total = wide_dot(cos_ref[...], mix_ref[0]) + wide_dot(sin_ref[...], mix_ref[1])
        out_ref[...] = (total * (1.0 / length)).astype(out_ref.dtype)


def convolve(table, spectrum, parts, places):
    length, channels = spectrum.shape[1:]
    block = table_block(length)
    steps = length // block
    table_spec = pl.BlockSpec((block, length), lambda p, s, _: (s, 0))
    return pl.pallas_call(
        functools.partial(convolve_kernel, len(parts)),
        grid_spec=pltpu.PrefetchScalarGridSpec(
            num_scalar_prefetch=1,
            grid=(2, steps),
            in_specs=[
                table_spec,
                table_spec,
                pl.BlockSpec((2, block, channels), lambda p, s, _: (0, s + p * (steps - 1 - s), 0)),
            ]
            + [pl.BlockSpec(part.shape, lambda p, s, _: (0, 0)) for part in parts],
            out_specs=pl.BlockSpec((block, channels), lambda p, s, _: (p * s, 0)),
            scratch_shapes=[pltpu.VMEM((length, channels), SHORT), pltpu.VMEM((2, length, channels), SHORT)],
        ),
        out_shape=jax.ShapeDtypeStruct((length, channels), SHORT),
        compiler_params=kernel_params(2),
        cost_estimate=NO_COST,
    )(places, table[0], table[1], spectrum, *parts)


def prepare_kernel(index_ref, filters_ref, gate_ref, cotangent_ref, out_ref):
    out_ref[0, 0] = filters_ref[...].astype(SHORT)
    out_ref[0, 1] = (cotangent_ref[...].astype(WIDE) * gate_ref[...].astype(WIDE)).astype(SHORT)


def prepare(filters, gate, cotangent, groups, waits):
    rows, width = filters.shape
    channels = width // groups
    if channels % 128:
        both = jnp.stack([filters, cotangent.astype(WIDE) * gate.astype(WIDE)]).astype(SHORT)
        return both.reshape(2, rows, groups, channels).transpose(2, 0, 1, 3)
    spec = pl.BlockSpec((rows, channels), lambda g: (0, g))
    return pl.pallas_call(
        waiting(prepare_kernel, len(waits)),
        grid=(groups,),
        in_specs=[pl.BlockSpec(memory_space=pltpu.SMEM)] + [ANYWHERE] * len(waits) + [spec] * 3,
        out_specs=pl.BlockSpec((1, 2, rows, channels), lambda g: (g, 0, 0, 0)),
        out_shape=jax.ShapeDtypeStruct((groups, 2, rows, channels), SHORT),
        compiler_params=kernel_params(1),
        cost_estimate=NO_COST,
    )(jnp.zeros((1,), jnp.int32), *waits, filters, gate, cotangent)


def finish_kernel(convolved_ref, gate_ref, cotangent_ref, output_ref, grad_ref):
    convolved = convolved_ref[0].astype(WIDE)
    output_ref[...] = (gate_ref[...].astype(WIDE) * convolved).astype(SHORT)
    grad_ref[...] = (cotangent_ref[...].astype(WIDE) * convolved).astype(SHORT)


def finish(convolved, gate, cotangent):
    groups, rows, channels = convolved.shape
    width = groups * channels
    if channels % 128:
        wide = convolved.swapaxes(0, 1).reshape(rows, width).astype(WIDE)
        return [(other.astype(WIDE) * wide).astype(SHORT) for other in (gate, cotangent)]
    spec = pl.BlockSpec((rows, channels), lambda g: (0, g))
    return pl.pallas_call(
        finish_kernel,
        grid=(groups,),
        in_specs=[pl.BlockSpec((1, rows, channels), lambda g: (g, 0, 0)), spec, spec],
        out_specs=[spec, spec],
        out_shape=[jax.ShapeDtypeStruct((rows, width), SHORT)] * 2,
        compiler_params=kernel_params(1),
        cost_estimate=NO_COST,
    )(convolved, gate, cotangent)


def arrange_kernel(dims, index_ref, *refs):
    outer, inner, far, near, halves, half_rows = dims
    part_refs, out_refs = refs[:inner], refs[inner:]
    channels = part_refs[0].shape[-1]
    tp = far * near
    for s in range(inner):
        lanes = aligned(index_ref[s], channels)
        for ahead in range(tp):
            source = index_ref[inner + ahead]
            for o in range(outer):
                for h in range(halves):
                    place = (ahead * outer + o) * half_rows
                    piece = part_refs[s][o, aligned(source * halves + h, half_rows)]
                    out_refs[h][place : place + half_rows, lanes] = piece


def arrange(parts, inner_places, sources, dims, waits):
    outer, inner, far, near, halves, half_rows = dims
    channels = parts[0].shape[-1]
    tp = far * near
    shape = (tp * outer * half_rows, inner * channels)
    if channels % 128:
        slots = jnp.zeros((inner, *parts[0].shape), SHORT)
        for s in range(inner):
            slots = lax.dynamic_update_index_in_dim(slots, parts[s], inner_places[s], 0)
        slots = slots.reshape(inner, outer, tp, halves, half_rows, channels).transpose(2, 3, 1, 4, 0, 5)
        slots = jnp.stack([pick(slots, sources[a]) for a in range(tp)])
        return [slots[:, h].reshape(shape) for h in range(halves)]
    index = jnp.concatenate([inner_places, sources]).astype(jnp.int32)
    size = math.prod(shape) * 2
    return pl.pallas_call(
        waiting(functools.partial(arrange_kernel, dims), len(waits)),
        in_specs=[pl.BlockSpec(memory_space=pltpu.SMEM)]
        + [ANYWHERE] * len(waits)
        + [pl.BlockSpec(memory_space=pltpu.VMEM)] * inner,
        out_specs=[pl.BlockSpec(memory_space=pltpu.VMEM)] * halves,
        out_shape=[jax.ShapeDtypeStruct(shape, SHORT)] * halves,
        compiler_params=kernel_params(0),
        cost_estimate=NO_COST,
    )(index, *waits, *parts)


def assemble_kernel(dims, index_ref, *refs):
    halves, steps, blocks, half_rows, depth = dims
    out_ref = refs[-1]
    for h in range(halves):
        for s in range(steps):
            rows = aligned(index_ref[s] * halves + h, half_rows)
            for b in range(blocks):
                out_ref[rows, aligned(index_ref[steps + b], depth)] = refs[h * steps + s][b]


def assemble(pieces, row_places, block_places, columns):
    halves, steps = len(pieces), len(pieces[0])
    blocks, half_rows, depth = pieces[0][0].shape
    flat = [piece for half in pieces for piece in half]
    rows = halves * steps * half_rows
    return pl.pallas_call(
        functools.partial(assemble_kernel, (halves, steps, blocks, half_rows, depth)),
        in_specs=[pl.BlockSpec(memory_space=pltpu.SMEM)] + [pl.BlockSpec(memory_space=pltpu.VMEM)] * len(flat),
        out_specs=pl.BlockSpec(memory_space=pltpu.VMEM),
        out_shape=jax.ShapeDtypeStruct((rows, columns), SHORT),
        compiler_params=kernel_params(0),
        cost_estimate=NO_COST,
    )(jnp.concatenate([row_places, block_places]).astype(jnp.int32), *flat)


def chunk_kernel(index_ref, in_ref, out_ref):
    out_ref[...] = in_ref[...]


def chunks_of(array, indices, count, waits=()):
    rows, width = array.shape
    chunk = width // count
    block = min(rows, 256)
    if chunk % 128:
        return jnp.concatenate([lax.dynamic_slice_in_dim(array, i * chunk, chunk, 1) for i in indices], axis=1)
    return pl.pallas_call(
        waiting(chunk_kernel, len(waits)),
        grid_spec=pltpu.PrefetchScalarGridSpec(
            num_scalar_prefetch=1,
            grid=(rows // block, len(indices)),
            in_specs=[ANYWHERE] * len(waits) + [pl.BlockSpec((block, chunk), lambda r, c, index: (r, index[c]))],
            out_specs=pl.BlockSpec((block, chunk), lambda r, c, _: (r, c)),
        ),
        out_shape=jax.ShapeDtypeStruct((rows, len(indices) * chunk), array.dtype),
        compiler_params=kernel_params(2),
        cost_estimate=NO_COST,
    )(jnp.stack(indices).astype(jnp.int32), *waits, array)


def row_part(array, index, count, waits):
    rows, width = array.shape
    size = rows // count
    if size % 16 or width % 128:
        return lax.dynamic_slice_in_dim(array, index * size, size, 0)
    return pl.pallas_call(
        waiting(chunk_kernel, len(waits)),
        grid_spec=pltpu.PrefetchScalarGridSpec(
            num_scalar_prefetch=1,
            grid=(1,),
            in_specs=[ANYWHERE] * len(waits) + [pl.BlockSpec((size, width), lambda r, index: (index[0], 0))],
            out_specs=pl.BlockSpec((size, width), lambda r, _: (0, 0)),
        ),
        out_shape=jax.ShapeDtypeStruct((size, width), array.dtype),
        compiler_params=kernel_params(1),
        cost_estimate=NO_COST,
    )(index[None].astype(jnp.int32), *waits, array)


def join_kernel(index_ref, *refs):
    size = refs[0].shape[0]
    for p, ref in enumerate(refs[:-1]):
        refs[-1][p * size : (p + 1) * size] = ref[...]


def join(parts, waits):
    size, width = parts[0].shape
    rows = len(parts) * size
    if size % 16:
        return jnp.concatenate(parts, axis=0)
    return pl.pallas_call(
        waiting(join_kernel, len(waits)),
        in_specs=[pl.BlockSpec(memory_space=pltpu.SMEM)]
        + [ANYWHERE] * len(waits)
        + [pl.BlockSpec(memory_space=pltpu.VMEM)] * len(parts),
        out_specs=pl.BlockSpec(memory_space=pltpu.VMEM),
        out_shape=jax.ShapeDtypeStruct((rows, width), parts[0].dtype),
        compiler_params=kernel_params(0),
        cost_estimate=NO_COST,
    )(jnp.zeros((1,), jnp.int32), *waits, *parts)


def product_kernel(dims, index_ref, *refs):
    inner, outer, pieces, depth, add = dims
    token_refs, weight_refs, out_ref = refs[:pieces], refs[pieces : pieces + inner], refs[-1]
    size = token_refs[0].shape[0] // outer
    parts = [aligned(index_ref[2 + inner + s], size) for s in range(outer)]
    total = refs[-2][...].astype(WIDE) if add else 0.0
    for i in range(inner):
        columns = aligned(index_ref[2 + i], depth)
        tokens = jnp.concatenate([ref[rows, columns] for ref in token_refs for rows in parts], axis=0)
        total = total + wide_dot(tokens, weight_refs[i][...])
    out_ref[...] = total.astype(SHORT).reshape(out_ref.shape)


def product(pieces, in_weight, chunk_index, received, inner_blocks, row_order, running, last, waits):
    inner = len(received) + 1
    outer = row_order.shape[0]
    depth, width = in_weight.shape
    chunk = width // outer
    channels = chunk // inner
    size, whole_depth = pieces[0].shape
    rows = len(pieces) * size
    at_inner = inner_blocks[0]
    if channels % 128:
        tokens = jnp.stack(pieces).reshape(len(pieces), outer, size // outer, whole_depth)
        tokens = jnp.concatenate([pick(tokens, row_order[s], 1)[:, None] for s in range(outer)], axis=1)
        tokens = tokens.reshape(rows, whole_depth)
        weights = [chunks_of(in_weight, [chunk_index], outer)]
        weights += [held[:, at * chunk : (at + 1) * chunk] for held, at in received]
        total = sum(
            wide_dot(lax.dynamic_slice_in_dim(tokens, inner_blocks[i] * depth, depth, 1), weights[i])
            for i in range(inner)
        )
        if running is not None:
            total = total + running.astype(WIDE)
        total = total.astype(SHORT)
        if last:
            total = total.reshape(rows, inner, channels)
            total = jnp.stack([pick(total, (at_inner + i) % inner, 1) for i in range(inner)])
        return total
    if last:
        out_spec = pl.BlockSpec((1, rows, channels), lambda g, index: ((g + inner - index[2]) % inner, 0, 0))
        out_shape = (inner, rows, channels)
    else:
        out_spec = pl.BlockSpec((rows, channels), lambda g, _: (0, g))
        out_shape = (rows, chunk)
    index = jnp.concatenate([chunk_index[None], at_inner[None], inner_blocks, row_order]).astype(jnp.int32)
    return pl.pallas_call(
        waiting(
            functools.partial(product_kernel, (inner, outer, len(pieces), depth, running is not None)), len(waits)
        ),
        grid_spec=pltpu.PrefetchScalarGridSpec(
            num_scalar_prefetch=1,
            grid=(inner,),
            in_specs=[ANYWHERE] * len(waits)
            + [pl.BlockSpec((size, whole_depth), lambda g, _: (0, 0)) for _ in pieces]
            + [pl.BlockSpec((depth, channels), lambda g, index: (0, index[0] * inner + g))]
            + [
                pl.BlockSpec((depth, channels), lambda g, _, at=at: (0, at * inner + g)) for _, at in received
            ]
            + ([] if running is None else [pl.BlockSpec((rows, channels), lambda g, _: (0, g))]),
            out_specs=out_spec,
        ),
        out_shape=jax.ShapeDtypeStruct(out_shape, SHORT),
        compiler_params=kernel_params(1),
        cost_estimate=NO_COST,
    )(index, *waits, *pieces, in_weight, *[held for held, _ in received], *([] if running is None else [running]))


def shares_kernel(dims, index_ref, grad_ref, *refs):
    outer, inner, near, chunk = dims
    own_ref, received_refs = refs[0], refs[1 : 1 + (inner - 1) * outer]
    out_refs, plain_ref = refs[1 + (inner - 1) * outer : -1], refs[-1]
    size = out_refs[0].shape[1]

    @pl.when(pl.program_id(0) == 0)
    def _():
        for o in range(outer):
            plain_ref[:, o * chunk : (o + 1) * chunk] = grad_ref[o]

    for i in range(inner):
        if i == 0:
            total = wide_dot_turned(plain_ref[...], own_ref[...])
        else:
            total = sum(
                wide_dot_turned(grad_ref[index_ref[s]], received_refs[(i - 1) * outer + s][...]) for s in range(outer)
            )
        total = total.astype(SHORT)
        for n in range(near):
            out_refs[n][i] = total[n * size : (n + 1) * size]


def shares(grad_values, in_weight, received, chunks, near, waits):
    outer, rows, chunk = grad_values.shape
    inner = len(received) + 1
    depth, width = in_weight.shape
    if chunk // inner % 128:
        plain = grad_values.swapaxes(0, 1).reshape(rows, width)
        totals = [wide_dot_turned(plain, in_weight)] + [
            sum(
                wide_dot_turned(pick(grad_values, chunks[s]), held[s][0][:, held[s][1] * chunk : (held[s][1] + 1) * chunk])
                for s in range(outer)
            )
            for held in received
        ]
        total = jnp.stack(totals).astype(SHORT).reshape(inner, near, rows // near, depth)
        return [total[:, n] for n in range(near)]
    block = min(depth, 256)
    flat = [w for held in received for w in held]
    out_spec = pl.BlockSpec((inner, rows // near, block), lambda k, _: (0, 0, k))
    return pl.pallas_call(
        waiting(functools.partial(shares_kernel, (outer, inner, near, chunk)), len(waits)),
        grid_spec=pltpu.PrefetchScalarGridSpec(
            num_scalar_prefetch=1,
            grid=(depth // block,),
            in_specs=[ANYWHERE] * len(waits)
            + [pl.BlockSpec((outer, rows, chunk), lambda k, _: (0, 0, 0))]
            + [pl.BlockSpec((block, width), lambda k, _: (k, 0))]
            + [pl.BlockSpec((block, chunk), lambda k, _, at=at: (k, at)) for _, at in flat],
            out_specs=[out_spec] * near,
            scratch_shapes=[pltpu.VMEM((rows, width), SHORT)],
        ),
        out_shape=[jax.ShapeDtypeStruct((inner, rows // near, depth), SHORT)] * near,
        compiler_params=kernel_params(1),
        cost_estimate=NO_COST,
    )(chunks.astype(jnp.int32), *waits, grad_values, in_weight, *[held for held, _ in flat])


def shifted(array, axis, shift):
    size = lax.axis_size(axis)
    return lax.ppermute(array, axis, [(at, (at + shift) % size) for at in range(size)])


def pick(array, index, axis=0):
    return lax.dynamic_index_in_dim(array, index, axis, keepdims=False)


def turned(parts, start):
    count = len(parts)
    backwards = jnp.stack(parts[::-1])
    doubled = jnp.concatenate([backwards, backwards], axis=0)
    return lax.dynamic_slice_in_dim(doubled, (count - 1 - start) % count, count, 0)


def per_device(tokens, in_weight, filters, gate, cotangent):
    outer, inner, far, near = (lax.axis_size(a) for a in ("outer", "inner", "far", "near"))
    at_outer, at_inner, at_far, at_near = (lax.axis_index(a) for a in ("outer", "inner", "far", "near"))
    tp = far * near
    at_tp = at_far * near + at_near
    rows, columns = tokens.shape
    fine_rows = rows // tp
    halves = 2 if fine_rows >= 32 else 1
    half_rows = fine_rows // halves
    ctx = ("outer", "inner")
    ctx_size = outer * inner
    cell = ("outer", "far", "near")
    split = tp // outer
    depth, width = in_weight.shape
    channels = width // ctx_size
    tile_blocks = columns // depth
    length = ctx_size * rows
    back_inner = [(at_inner - i) % inner for i in range(inner)]

    def destination(source_outer, source_tp, step):
        part = (source_outer * split + source_tp % split + step) % tp
        return (source_tp // split) * tp + part

    chunks = [(at_outer - s) % outer for s in range(outer)]
    order = [s % outer for s in range(1, outer + 1)]
    received = [[None] * outer for _ in range(1, inner)]
    arrivals = []

    def send_pair(waits):
        pair = order[2 * len(arrivals) : 2 * len(arrivals) + 2]
        sent = chunks_of(in_weight, [chunks[s] for s in pair], outer, waits)
        arrivals.append([shifted(sent, "inner", i) for i in range(1, inner)])
        for i in range(1, inner):
            for at, s in enumerate(pair):
                received[i - 1][s] = (arrivals[-1][i - 1], at)
        return sent

    moved = []
    if split == 1:
        by_far = [row_part(tokens, (at_far + f) % far, far, []) for f in range(far)]
        sent = send_pair(by_far)
        prepared = prepare(filters, gate, cotangent, ctx_size, [sent])
        held = [by_far[0]] + [shifted(by_far[f], "far", f) for f in range(1, far)]
        held = jnp.stack(held).reshape(far, near, fine_rows, columns)
        for step in range(tp):
            pairs = []
            for o in range(outer):
                for g in range(far):
                    for c in range(near):
                        tile, part = (o + step) % tp // near, (o + step) % tp % near
                        pairs.append(((o * far + g) * near + c, ((tile * near + c) * far + g) * near + part))
            number = (at_outer + step) % tp
            part = lax.dynamic_slice(
                held, ((at_far - number // near) % far, number % near, 0, 0), (1, 1, fine_rows, columns)
            )
            moved.append(lax.ppermute(part.reshape(fine_rows, columns), cell, pairs))
        token_part = join(moved, arrivals[0] + [prepared])
    else:
        prepared = prepare(filters, gate, cotangent, ctx_size, [send_pair([tokens])])
        row_parts = tokens.reshape(tp, fine_rows, columns)
        for step in range(tp):
            pairs = [(o * tp + t, destination(o, t, step)) for o in range(outer) for t in range(tp)]
            part = (at_outer * split + at_tp % split + step) % tp
            moved.append(lax.ppermute(pick(row_parts, part), cell, pairs))
        token_part = turned(moved, at_tp).reshape(outer, split, fine_rows, columns).swapaxes(1, 2)
        token_part = token_part.reshape(outer * fine_rows, split * columns)

    channel_rows = lax.all_to_all(release(prepared, [token_part]), ctx, split_axis=0, concat_axis=0, tiled=True)
    sent = token_part
    while len(arrivals) < outer // 2:
        sent = send_pair([sent, *arrivals[-1]])
    table = transform_table(length)

    pieces = [token_part] + [shifted(token_part, "far", f) for f in range(1, far)]
    pieces = pieces + [shifted(piece, "near", n) for n in range(1, near) for piece in pieces]
    places = []
    for n in range(near):
        for f in range(far):
            source_near = (at_near - n) % near
            source = (at_far - f) % far * near + source_near
            for s in range(outer):
                source_outer = (source_near - s) % outer if split == 1 else s
                places.append(source_outer * (inner * tp) + source)
    places = jnp.stack(places).astype(jnp.int32)
    places = jnp.stack([places + back_inner[s] * tp for s in range(inner)])

    blocks = jnp.stack(back_inner)
    turn = at_outer // near * near if split == 1 else 0
    row_order = jnp.stack([(s + turn) % outer + at_outer * 0 for s in range(outer)])
    running = None
    waits = [sent]
    for s in order:
        if running is not None:
            running = shifted(running, "outer", 1)
        held = [chunk[s] for chunk in received]
        running = product(pieces, in_weight, chunks[s], held, blocks, row_order, running, s == 0, waits)
        waits = []
        if s == outer - 2:
            grad_values, spectrum = correlate(table, rotation(length), channel_rows, [running])
            by_inner = grad_values.reshape(outer, inner, rows, channels)
            grad_parts = [pick(by_inner, at_inner, 1)]
            for i in range(1, inner):
                grad_parts.append(shifted(pick(by_inner, (at_inner + i) % inner, 1), "inner", i))
            waits = [spectrum]
        if s == outer - 1:
            sources = [(at_far + f) % far * near + (at_near + n) % near for n in range(near) for f in range(far)]
            arranged = arrange(
                grad_parts, jnp.stack(back_inner), jnp.stack(sources), (outer, inner, far, near, halves, half_rows), [running]
            )
            gathered = [lax.all_gather(half, "outer", axis=0, tiled=False) for half in arranged]
            waits = list(arranged)
    value_parts = [running[0]] + [shifted(running[i], "inner", i) for i in range(1, inner)]

    convolved = convolve(table, spectrum, value_parts, places).reshape(ctx_size, rows, channels)

    sent_back = []
    waits = [convolved]
    for half in gathered:
        by_near = shares(half, in_weight, received, jnp.stack(chunks), near, waits)
        total = by_near[0].astype(WIDE) + sum(shifted(by_near[n], "near", n).astype(WIDE) for n in range(1, near))
        total = total.astype(SHORT).reshape(inner, far, outer * half_rows, depth)
        waits = [total]
        total = total[:, 0].astype(WIDE) + sum(shifted(total[:, f], "far", f).astype(WIDE) for f in range(1, far))
        total = total.astype(SHORT).reshape(inner, outer, half_rows, depth)
        if split == 1:
            total = total.swapaxes(0, 1)
        else:
            total = turned(list(total), at_inner).reshape(split, tile_blocks, outer, half_rows, depth)
            total = total.transpose(2, 0, 1, 3, 4).reshape(tp, tile_blocks, half_rows, depth)
        back = []
        for step in range(tp):
            pairs = [(destination(o, t, step), o * tp + t) for o in range(outer) for t in range(tp)]
            back.append(lax.ppermute(pick(total, (at_tp - step) % tp), cell, pairs))
        sent_back.append(back)
    row_places = [(at_outer * split + at_tp % split + step) % tp for step in range(tp)]
    block_places = back_inner if split == 1 else [jnp.int32(b) for b in range(tile_blocks)]
    grad_tokens = assemble(sent_back, jnp.stack(row_places), jnp.stack(block_places), columns)

    exchanged = lax.all_to_all(convolved, ctx, split_axis=0, concat_axis=0, tiled=True)
    gated_output, grad_gate = finish(exchanged, gate, cotangent)
    return (gated_output, grad_gate, grad_tokens)


def solution(mesh):
    ctx_size, tp_size = mesh.shape["ctx"], mesh.shape["tp"]
    inner, near = 1, 2
    while inner * inner * 4 <= ctx_size:
        inner *= 2
    fine_mesh = Mesh(
        np.asarray(mesh.devices).reshape(ctx_size // inner, inner, tp_size // near, near),
        ("outer", "inner", "far", "near"),
    )
    placed = P(("outer", "inner"), ("far", "near"))
    return jax.shard_map(
        per_device,
        mesh=fine_mesh,
        in_specs=(placed,) * 5,
        out_specs=(placed,) * 3,
        check_vma=False,
    )
```

```python
import functools
import math

import jax
import jax.numpy as jnp
import numpy as np
from jax import lax
from jax.experimental import pallas as pl
from jax.experimental.pallas import tpu as pltpu
from jax.sharding import Mesh, PartitionSpec as P

TWO_PI = 2.0 * math.pi
WIDE = jnp.float32
SHORT = jnp.bfloat16
LAST_TWO = (((1,), (1,)), ((), ()))


def transform_table(length):
    period = 16 * length
    if length > 2048:
        points = 4 * jnp.arange(length, dtype=jnp.int32) + 1
        angles = (points[:, None] * points[None, :] % period).astype(WIDE) * (TWO_PI / period)
        return [jnp.cos(angles).astype(SHORT), jnp.sin(angles).astype(SHORT)]
    points = 4 * np.arange(length, dtype=np.int64) + 1
    turns = points[:, None] * points[None, :] % period
    angles = np.arange(period) * (TWO_PI / period)
    return [jnp.asarray(wave(angles).astype(SHORT)[turns]) for wave in (np.cos, np.sin)]


def table_block(length):
    return min(512, length // 2)


def rotation(length):
    angle = (4 * jnp.arange(length, dtype=jnp.int32) + 1).astype(WIDE) * (TWO_PI / (16 * length))
    return jnp.stack([jnp.cos(angle), jnp.sin(angle)], axis=1)


def wide_dot(left, right):
    return jnp.dot(left, right, preferred_element_type=WIDE)


def wide_dot_turned(left, right):
    return lax.dot_general(left, right, LAST_TWO, preferred_element_type=WIDE)


def kernel_params(axes):
    return pltpu.CompilerParams(
        dimension_semantics=("arbitrary",) * axes, vmem_limit_bytes=48 * 1024 * 1024
    )


NO_COST = pl.CostEstimate(flops=0, bytes_accessed=0, transcendentals=0)


ANYWHERE = pl.BlockSpec(memory_space=pl.ANY)


def waiting(kernel, count):
    return lambda index_ref, *refs: kernel(index_ref, *refs[count:])


def release_kernel(index_ref, in_ref, out_ref):
    pass


def release(array, waits):
    return pl.pallas_call(
        waiting(release_kernel, len(waits)),
        in_specs=[pl.BlockSpec(memory_space=pltpu.SMEM)] + [ANYWHERE] * (len(waits) + 1),
        out_specs=ANYWHERE,
        out_shape=jax.ShapeDtypeStruct(array.shape, array.dtype),
        input_output_aliases={1 + len(waits): 0},
        compiler_params=kernel_params(0),
        cost_estimate=NO_COST,
    )(jnp.zeros((1,), jnp.int32), *waits, array)


def aligned(index, size):
    return pl.ds(pl.multiple_of(index * size, size), size)


def correlate_kernel(index_ref, cos_ref, sin_ref, turn_ref, both_ref, out_ref, spectrum_ref, signal_ref, mix_ref):
    phase, step = pl.program_id(0), pl.program_id(1)
    block = cos_ref.shape[0]
    length, channels = mix_ref.shape[1:]
    rows = aligned(step, block)

    @pl.when((phase == 0) & (step == 0))
    def _():
        for which in range(2):
            signal_ref[:, which * channels : (which + 1) * channels] = both_ref[:, which].reshape(length, channels)

    @pl.when(phase == 0)
    def _():
        turn_cos, turn_sin = turn_ref[:, 0:1], turn_ref[:, 1:2]
        cos_sums = wide_dot(cos_ref[...], signal_ref[...])
        sin_sums = wide_dot(sin_ref[...], signal_ref[...])
        raw_cos, signal_cos = cos_sums[:, :channels], cos_sums[:, channels:]
        raw_sin, signal_sin = sin_sums[:, :channels], sin_sums[:, channels:]
        filter_cos = raw_cos * turn_cos + raw_sin * turn_sin
        filter_sin = raw_sin * turn_cos - raw_cos * turn_sin
        spectrum_ref[0] = filter_cos.astype(SHORT)
        spectrum_ref[1] = filter_sin.astype(SHORT)
        mix_ref[0, rows] = (signal_cos * filter_cos + signal_sin * filter_sin).astype(SHORT)
        mix_ref[1, rows] = (signal_sin * filter_cos - signal_cos * filter_sin).astype(SHORT)

    @pl.when(phase == 1)
    def _():
        total = wide_dot(cos_ref[...], mix_ref[0]) + wide_dot(sin_ref[...], mix_ref[1])
        out_ref[...] = (total * (1.0 / length)).astype(out_ref.dtype)


def correlate(table, turn, both, waits):
    parts, _, rows, channels = both.shape
    length = parts * rows
    block = table_block(length)
    steps = length // block
    table_spec = pl.BlockSpec((block, length), lambda p, s: (s, 0))
    return pl.pallas_call(
        waiting(correlate_kernel, len(waits)),
        grid=(2, steps),
        in_specs=[
            pl.BlockSpec(memory_space=pltpu.SMEM),
            *[ANYWHERE] * len(waits),
            table_spec,
            table_spec,
            pl.BlockSpec((block, 2), lambda p, s: (s, 0)),
            pl.BlockSpec((parts, 2, rows, channels), lambda p, s: (0, 0, 0, 0)),
        ],
        out_specs=[
            pl.BlockSpec((block, channels), lambda p, s: (p * s, 0)),
            pl.BlockSpec((2, block, channels), lambda p, s: (0, s + p * (steps - 1 - s), 0)),
        ],
        out_shape=[
            jax.ShapeDtypeStruct((length, channels), SHORT),
            jax.ShapeDtypeStruct((2, length, channels), SHORT),
        ],
        scratch_shapes=[pltpu.VMEM((length, 2 * channels), SHORT), pltpu.VMEM((2, length, channels), SHORT)],
        compiler_params=kernel_params(2),
        cost_estimate=NO_COST,
    )(jnp.zeros((1,), jnp.int32), *waits, table[0], table[1], turn, both)


def convolve_kernel(inner, places_ref, cos_ref, sin_ref, spectrum_ref, *refs):
    part_refs, (out_ref, signal_ref, mix_ref) = refs[:inner], refs[inner:]
    phase, step = pl.program_id(0), pl.program_id(1)
    block = cos_ref.shape[0]
    length = signal_ref.shape[0]
    rows = aligned(step, block)
    pieces = places_ref.shape[1]
    size = part_refs[0].shape[0] // pieces

    @pl.when((phase == 0) & (step == 0))
    def _():
        for s in range(inner):
            for p in range(pieces):
                signal_ref[aligned(places_ref[s, p], size)] = part_refs[s][p * size : (p + 1) * size]

    @pl.when(phase == 0)
    def _():
        filter_cos, filter_sin = spectrum_ref[0].astype(WIDE), spectrum_ref[1].astype(WIDE)
        signal_cos = wide_dot(cos_ref[...], signal_ref[...])
        signal_sin = wide_dot(sin_ref[...], signal_ref[...])
        mix_ref[0, rows] = (signal_cos * filter_cos - signal_sin * filter_sin).astype(SHORT)
        mix_ref[1, rows] = (signal_cos * filter_sin + signal_sin * filter_cos).astype(SHORT)

    @pl.when(phase == 1)
    def _():
        total = wide_dot(cos_ref[...], mix_ref[0]) + wide_dot(sin_ref[...], mix_ref[1])
        out_ref[...] = (total * (1.0 / length)).astype(out_ref.dtype)


def convolve(table, spectrum, parts, places, waits):
    length, channels = spectrum.shape[1:]
    block = table_block(length)
    steps = length // block
    table_spec = pl.BlockSpec((block, length), lambda p, s, _: (s, 0))
    return pl.pallas_call(
        waiting(functools.partial(convolve_kernel, len(parts)), len(waits)),
        grid_spec=pltpu.PrefetchScalarGridSpec(
            num_scalar_prefetch=1,
            grid=(2, steps),
            in_specs=[
                *[ANYWHERE] * len(waits),
                table_spec,
                table_spec,
                pl.BlockSpec((2, block, channels), lambda p, s, _: (0, s + p * (steps - 1 - s), 0)),
            ]
            + [pl.BlockSpec(part.shape, lambda p, s, _: (0, 0)) for part in parts],
            out_specs=pl.BlockSpec((block, channels), lambda p, s, _: (p * s, 0)),
            scratch_shapes=[pltpu.VMEM((length, channels), SHORT), pltpu.VMEM((2, length, channels), SHORT)],
        ),
        out_shape=jax.ShapeDtypeStruct((length, channels), SHORT),
        compiler_params=kernel_params(2),
        cost_estimate=NO_COST,
    )(places, *waits, table[0], table[1], spectrum, *parts)


def prepare_kernel(index_ref, filters_ref, gate_ref, cotangent_ref, out_ref):
    out_ref[0, 0] = filters_ref[...].astype(SHORT)
    out_ref[0, 1] = (cotangent_ref[...].astype(WIDE) * gate_ref[...].astype(WIDE)).astype(SHORT)


def prepare(filters, gate, cotangent, groups, waits):
    rows, width = filters.shape
    channels = width // groups
    if channels % 128:
        both = jnp.stack([filters, cotangent.astype(WIDE) * gate.astype(WIDE)]).astype(SHORT)
        return both.reshape(2, rows, groups, channels).transpose(2, 0, 1, 3)
    spec = pl.BlockSpec((rows, channels), lambda g: (0, g))
    return pl.pallas_call(
        waiting(prepare_kernel, len(waits)),
        grid=(groups,),
        in_specs=[pl.BlockSpec(memory_space=pltpu.SMEM)] + [ANYWHERE] * len(waits) + [spec] * 3,
        out_specs=pl.BlockSpec((1, 2, rows, channels), lambda g: (g, 0, 0, 0)),
        out_shape=jax.ShapeDtypeStruct((groups, 2, rows, channels), SHORT),
        compiler_params=kernel_params(1),
        cost_estimate=NO_COST,
    )(jnp.zeros((1,), jnp.int32), *waits, filters, gate, cotangent)


def finish_kernel(convolved_ref, gate_ref, cotangent_ref, output_ref, grad_ref):
    convolved = convolved_ref[0].astype(WIDE)
    output_ref[...] = (gate_ref[...].astype(WIDE) * convolved).astype(SHORT)
    grad_ref[...] = (cotangent_ref[...].astype(WIDE) * convolved).astype(SHORT)


def finish(convolved, gate, cotangent):
    groups, rows, channels = convolved.shape
    width = groups * channels
    if channels % 128:
        wide = convolved.swapaxes(0, 1).reshape(rows, width).astype(WIDE)
        return [(other.astype(WIDE) * wide).astype(SHORT) for other in (gate, cotangent)]
    spec = pl.BlockSpec((rows, channels), lambda g: (0, g))
    return pl.pallas_call(
        finish_kernel,
        grid=(groups,),
        in_specs=[pl.BlockSpec((1, rows, channels), lambda g: (g, 0, 0)), spec, spec],
        out_specs=[spec, spec],
        out_shape=[jax.ShapeDtypeStruct((rows, width), SHORT)] * 2,
        compiler_params=kernel_params(1),
        cost_estimate=NO_COST,
    )(convolved, gate, cotangent)


def arrange_kernel(dims, index_ref, *refs):
    outer, inner, far, near, halves, half_rows = dims
    part_refs, out_refs = refs[:inner], refs[inner:]
    channels = part_refs[0].shape[-1]
    tp = far * near
    for s in range(inner):
        lanes = aligned(index_ref[s], channels)
        for ahead in range(tp):
            source = index_ref[inner + ahead]
            for o in range(outer):
                for h in range(halves):
                    place = (ahead * outer + o) * half_rows
                    piece = part_refs[s][o, aligned(source * halves + h, half_rows)]
                    out_refs[h][place : place + half_rows, lanes] = piece


def arrange(parts, inner_places, sources, dims, waits):
    outer, inner, far, near, halves, half_rows = dims
    channels = parts[0].shape[-1]
    tp = far * near
    shape = (tp * outer * half_rows, inner * channels)
    if channels % 128:
        slots = jnp.zeros((inner, *parts[0].shape), SHORT)
        for s in range(inner):
            slots = lax.dynamic_update_index_in_dim(slots, parts[s], inner_places[s], 0)
        slots = slots.reshape(inner, outer, tp, halves, half_rows, channels).transpose(2, 3, 1, 4, 0, 5)
        slots = jnp.stack([pick(slots, sources[a]) for a in range(tp)])
        return [slots[:, h].reshape(shape) for h in range(halves)]
    index = jnp.concatenate([inner_places, sources]).astype(jnp.int32)
    size = math.prod(shape) * 2
    return pl.pallas_call(
        waiting(functools.partial(arrange_kernel, dims), len(waits)),
        in_specs=[pl.BlockSpec(memory_space=pltpu.SMEM)]
        + [ANYWHERE] * len(waits)
        + [pl.BlockSpec(memory_space=pltpu.VMEM)] * inner,
        out_specs=[pl.BlockSpec(memory_space=pltpu.VMEM)] * halves,
        out_shape=[jax.ShapeDtypeStruct(shape, SHORT)] * halves,
        compiler_params=kernel_params(0),
        cost_estimate=NO_COST,
    )(index, *waits, *parts)


def assemble_kernel(dims, index_ref, *refs):
    halves, steps, blocks, half_rows, depth = dims
    out_ref = refs[-1]
    for h in range(halves):
        for s in range(steps):
            rows = aligned(index_ref[s] * halves + h, half_rows)
            for b in range(blocks):
                out_ref[rows, aligned(index_ref[steps + b], depth)] = refs[h * steps + s][b]


def assemble(pieces, row_places, block_places, columns):
    halves, steps = len(pieces), len(pieces[0])
    blocks, half_rows, depth = pieces[0][0].shape
    flat = [piece for half in pieces for piece in half]
    rows = halves * steps * half_rows
    return pl.pallas_call(
        functools.partial(assemble_kernel, (halves, steps, blocks, half_rows, depth)),
        in_specs=[pl.BlockSpec(memory_space=pltpu.SMEM)] + [pl.BlockSpec(memory_space=pltpu.VMEM)] * len(flat),
        out_specs=pl.BlockSpec(memory_space=pltpu.VMEM),
        out_shape=jax.ShapeDtypeStruct((rows, columns), SHORT),
        compiler_params=kernel_params(0),
        cost_estimate=NO_COST,
    )(jnp.concatenate([row_places, block_places]).astype(jnp.int32), *flat)


def chunk_kernel(index_ref, in_ref, out_ref):
    out_ref[...] = in_ref[...]


def chunks_of(array, indices, count, waits=()):
    rows, width = array.shape
    chunk = width // count
    block = min(rows, 1024)
    if chunk % 128:
        return jnp.concatenate([lax.dynamic_slice_in_dim(array, i * chunk, chunk, 1) for i in indices], axis=1)
    return pl.pallas_call(
        waiting(chunk_kernel, len(waits)),
        grid_spec=pltpu.PrefetchScalarGridSpec(
            num_scalar_prefetch=1,
            grid=(rows // block, len(indices)),
            in_specs=[ANYWHERE] * len(waits) + [pl.BlockSpec((block, chunk), lambda r, c, index: (r, index[c]))],
            out_specs=pl.BlockSpec((block, chunk), lambda r, c, _: (r, c)),
        ),
        out_shape=jax.ShapeDtypeStruct((rows, len(indices) * chunk), array.dtype),
        compiler_params=kernel_params(2),
        cost_estimate=NO_COST,
    )(jnp.stack(indices).astype(jnp.int32), *waits, array)


def join_kernel(index_ref, *refs):
    size = refs[0].shape[0]
    for p, ref in enumerate(refs[:-1]):
        refs[-1][p * size : (p + 1) * size] = ref[...]


def join(parts, waits):
    size, width = parts[0].shape
    rows = len(parts) * size
    if size % 16:
        return jnp.concatenate(parts, axis=0)
    return pl.pallas_call(
        waiting(join_kernel, len(waits)),
        in_specs=[pl.BlockSpec(memory_space=pltpu.SMEM)]
        + [ANYWHERE] * len(waits)
        + [pl.BlockSpec(memory_space=pltpu.VMEM)] * len(parts),
        out_specs=pl.BlockSpec(memory_space=pltpu.VMEM),
        out_shape=jax.ShapeDtypeStruct((rows, width), parts[0].dtype),
        compiler_params=kernel_params(0),
        cost_estimate=NO_COST,
    )(jnp.zeros((1,), jnp.int32), *waits, *parts)


def product_kernel(dims, index_ref, *refs):
    inner, outer, pieces, depth, add = dims
    token_refs, weight_refs, (out_ref, joined_ref) = refs[:pieces], refs[pieces : pieces + inner], refs[-2:]
    size = token_refs[0].shape[0] // outer

    @pl.when(pl.program_id(0) == 0)
    def _():
        for p in range(pieces):
            for o in range(outer):
                rows = aligned(index_ref[2 + inner + o], size)
                place = (p * outer + o) * size
                joined_ref[place : place + size] = token_refs[p][rows]

    total = refs[-3][...].astype(WIDE) if add else 0.0
    for i in range(inner):
        columns = aligned(index_ref[2 + i], depth)
        total = total + wide_dot(joined_ref[:, columns], weight_refs[i][...])
    out_ref[...] = total.astype(SHORT).reshape(out_ref.shape)


def product(pieces, in_weight, chunk_index, received, inner_blocks, row_order, running, last, waits):
    inner = len(received) + 1
    outer = row_order.shape[0]
    depth, width = in_weight.shape
    chunk = width // outer
    channels = chunk // inner
    size, whole_depth = pieces[0].shape
    rows = len(pieces) * size
    at_inner = inner_blocks[0]
    if channels % 128:
        tokens = jnp.stack(pieces).reshape(len(pieces), outer, size // outer, whole_depth)
        tokens = jnp.concatenate([pick(tokens, row_order[s], 1)[:, None] for s in range(outer)], axis=1)
        tokens = tokens.reshape(rows, whole_depth)
        weights = [chunks_of(in_weight, [chunk_index], outer)]
        weights += [held[:, at * chunk : (at + 1) * chunk] for held, at in received]
        total = sum(
            wide_dot(lax.dynamic_slice_in_dim(tokens, inner_blocks[i] * depth, depth, 1), weights[i])
            for i in range(inner)
        )
        if running is not None:
            total = total + running.astype(WIDE)
        total = total.astype(SHORT)
        if last:
            total = total.reshape(rows, inner, channels)
            total = jnp.stack([pick(total, (at_inner + i) % inner, 1) for i in range(inner)])
        return total
    if last:
        out_spec = pl.BlockSpec((1, rows, channels), lambda g, index: ((g + inner - index[2]) % inner, 0, 0))
        out_shape = (inner, rows, channels)
    else:
        out_spec = pl.BlockSpec((rows, channels), lambda g, _: (0, g))
        out_shape = (rows, chunk)
    index = jnp.concatenate([chunk_index[None], at_inner[None], inner_blocks, row_order]).astype(jnp.int32)
    return pl.pallas_call(
        waiting(
            functools.partial(product_kernel, (inner, outer, len(pieces), depth, running is not None)), len(waits)
        ),
        grid_spec=pltpu.PrefetchScalarGridSpec(
            num_scalar_prefetch=1,
            grid=(inner,),
            in_specs=[ANYWHERE] * len(waits)
            + [pl.BlockSpec((size, whole_depth), lambda g, _: (0, 0)) for _ in pieces]
            + [pl.BlockSpec((depth, channels), lambda g, index: (0, index[0] * inner + g))]
            + [
                pl.BlockSpec((depth, channels), lambda g, _, at=at: (0, at * inner + g)) for _, at in received
            ]
            + ([] if running is None else [pl.BlockSpec((rows, channels), lambda g, _: (0, g))]),
            out_specs=out_spec,
            scratch_shapes=[pltpu.VMEM((rows, whole_depth), SHORT)],
        ),
        out_shape=jax.ShapeDtypeStruct(out_shape, SHORT),
        compiler_params=kernel_params(1),
        cost_estimate=NO_COST,
    )(index, *waits, *pieces, in_weight, *[held for held, _ in received], *([] if running is None else [running]))


def shares_kernel(dims, index_ref, grad_ref, *refs):
    outer, inner, near, chunk = dims
    own_ref, received_refs = refs[0], refs[1 : 1 + (inner - 1) * outer]
    out_refs, plain_ref = refs[1 + (inner - 1) * outer : -1], refs[-1]
    size = out_refs[0].shape[1]

    @pl.when(pl.program_id(0) == 0)
    def _():
        for o in range(outer):
            plain_ref[:, o * chunk : (o + 1) * chunk] = grad_ref[o]

    for i in range(inner):
        if i == 0:
            total = wide_dot_turned(plain_ref[...], own_ref[...])
        else:
            total = sum(
                wide_dot_turned(grad_ref[index_ref[s]], received_refs[(i - 1) * outer + s][...]) for s in range(outer)
            )
        total = total.astype(SHORT)
        for n in range(near):
            out_refs[n][i] = total[n * size : (n + 1) * size]


def shares(grad_values, in_weight, received, chunks, near, waits):
    outer, rows, chunk = grad_values.shape
    inner = len(received) + 1
    depth, width = in_weight.shape
    if chunk // inner % 128:
        plain = grad_values.swapaxes(0, 1).reshape(rows, width)
        totals = [wide_dot_turned(plain, in_weight)] + [
            sum(
                wide_dot_turned(pick(grad_values, chunks[s]), held[s][0][:, held[s][1] * chunk : (held[s][1] + 1) * chunk])
                for s in range(outer)
            )
            for held in received
        ]
        total = jnp.stack(totals).astype(SHORT).reshape(inner, near, rows // near, depth)
        return [total[:, n] for n in range(near)]
    block = min(depth, 256)
    flat = [w for held in received for w in held]
    out_spec = pl.BlockSpec((inner, rows // near, block), lambda k, _: (0, 0, k))
    return pl.pallas_call(
        waiting(functools.partial(shares_kernel, (outer, inner, near, chunk)), len(waits)),
        grid_spec=pltpu.PrefetchScalarGridSpec(
            num_scalar_prefetch=1,
            grid=(depth // block,),
            in_specs=[ANYWHERE] * len(waits)
            + [pl.BlockSpec((outer, rows, chunk), lambda k, _: (0, 0, 0))]
            + [pl.BlockSpec((block, width), lambda k, _: (k, 0))]
            + [pl.BlockSpec((block, chunk), lambda k, _, at=at: (k, at)) for _, at in flat],
            out_specs=[out_spec] * near,
            scratch_shapes=[pltpu.VMEM((rows, width), SHORT)],
        ),
        out_shape=[jax.ShapeDtypeStruct((inner, rows // near, depth), SHORT)] * near,
        compiler_params=kernel_params(1),
        cost_estimate=NO_COST,
    )(chunks.astype(jnp.int32), *waits, grad_values, in_weight, *[held for held, _ in flat])


def shifted(array, axis, shift):
    size = lax.axis_size(axis)
    return lax.ppermute(array, axis, [(at, (at + shift) % size) for at in range(size)])


def pick(array, index, axis=0):
    return lax.dynamic_index_in_dim(array, index, axis, keepdims=False)


def turned(parts, start):
    count = len(parts)
    backwards = jnp.stack(parts[::-1])
    doubled = jnp.concatenate([backwards, backwards], axis=0)
    return lax.dynamic_slice_in_dim(doubled, (count - 1 - start) % count, count, 0)


def per_device(tokens, in_weight, filters, gate, cotangent):
    outer, inner, far, near = (lax.axis_size(a) for a in ("outer", "inner", "far", "near"))
    at_outer, at_inner, at_far, at_near = (lax.axis_index(a) for a in ("outer", "inner", "far", "near"))
    tp = far * near
    at_tp = at_far * near + at_near
    rows, columns = tokens.shape
    fine_rows = rows // tp
    halves = 2 if fine_rows >= 32 else 1
    half_rows = fine_rows // halves
    ctx = ("outer", "inner")
    ctx_size = outer * inner
    cell = ("outer", "far", "near")
    split = tp // outer
    depth, width = in_weight.shape
    channels = width // ctx_size
    tile_blocks = columns // depth
    length = ctx_size * rows
    back_inner = [(at_inner - i) % inner for i in range(inner)]

    def destination(source_outer, source_tp, step):
        part = (source_outer * split + source_tp % split + step) % tp
        return (source_tp // split) * tp + part

    chunks = [(at_outer - s) % outer for s in range(outer)]
    order = [s % outer for s in range(1, outer + 1)]
    received = [[None] * outer for _ in range(1, inner)]
    arrivals = []

    def send_chunks(some, waits):
        sent = chunks_of(in_weight, [chunks[s] for s in some], outer, waits)
        arrivals.append([shifted(sent, "inner", i) for i in range(1, inner)])
        for i in range(1, inner):
            for at, s in enumerate(some):
                received[i - 1][s] = (arrivals[-1][i - 1], at)
        return sent

    moved = []
    if split == 1:
        by_far = tokens.reshape(far, near * fine_rows, columns)
        by_far = [pick(by_far, (at_far + f) % far) for f in range(far)]
        sent = send_chunks(order[:2], by_far[1:])
        prepared = prepare(filters, gate, cotangent, ctx_size, [sent])
        held = [by_far[0]] + [shifted(by_far[f], "far", f) for f in range(1, far)]
        held = jnp.stack(held).reshape(far, near, fine_rows, columns)
        for step in range(tp):
            pairs = []
            for o in range(outer):
                for g in range(far):
                    for c in range(near):
                        tile, part = (o + step) % tp // near, (o + step) % tp % near
                        pairs.append(((o * far + g) * near + c, ((tile * near + c) * far + g) * near + part))
            number = (at_outer + step) % tp
            part = lax.dynamic_slice(
                held, ((at_far - number // near) % far, number % near, 0, 0), (1, 1, fine_rows, columns)
            )
            moved.append(lax.ppermute(part.reshape(fine_rows, columns), cell, pairs))
        token_part = join(moved, [prepared, *arrivals[0]])
    else:
        sent = send_chunks(order[:2], [])
        prepared = prepare(filters, gate, cotangent, ctx_size, [sent])
        row_parts = tokens.reshape(tp, fine_rows, columns)
        for step in range(tp):
            pairs = [(o * tp + t, destination(o, t, step)) for o in range(outer) for t in range(tp)]
            part = (at_outer * split + at_tp % split + step) % tp
            moved.append(lax.ppermute(pick(row_parts, part), cell, pairs))
        token_part = turned(moved, at_tp).reshape(outer, split, fine_rows, columns).swapaxes(1, 2)
        token_part = token_part.reshape(outer * fine_rows, split * columns)

    channel_rows = lax.all_to_all(release(prepared, [token_part]), ctx, split_axis=0, concat_axis=0, tiled=True)
    sent = send_chunks(order[2:], [token_part, *arrivals[0]])
    table = transform_table(length)

    pieces = [token_part] + [shifted(token_part, "far", f) for f in range(1, far)]
    pieces = pieces + [shifted(piece, "near", n) for n in range(1, near) for piece in pieces]
    places = []
    for n in range(near):
        for f in range(far):
            source_near = (at_near - n) % near
            source = (at_far - f) % far * near + source_near
            for s in range(outer):
                source_outer = (source_near - s) % outer if split == 1 else s
                places.append(source_outer * (inner * tp) + source)
    places = jnp.stack(places).astype(jnp.int32)
    places = jnp.stack([places + back_inner[s] * tp for s in range(inner)])

    blocks = jnp.stack(back_inner)
    turn = at_outer // near * near if split == 1 else 0
    row_order = jnp.stack([(s + turn) % outer + at_outer * 0 for s in range(outer)])
    running = None
    waits = [sent]
    for s in order:
        if running is not None:
            running = shifted(running, "outer", 1)
        held = [chunk[s] for chunk in received]
        running = product(pieces, in_weight, chunks[s], held, blocks, row_order, running, s == 0, waits)
        waits = []
        if s == outer - 2:
            grad_values, spectrum = correlate(table, rotation(length), channel_rows, [running])
            by_inner = grad_values.reshape(outer, inner, rows, channels)
            grad_parts = [pick(by_inner, at_inner, 1)]
            for i in range(1, inner):
                grad_parts.append(shifted(pick(by_inner, (at_inner + i) % inner, 1), "inner", i))
            waits = [spectrum]
        if s == outer - 1:
            sources = [(at_far + f) % far * near + (at_near + n) % near for n in range(near) for f in range(far)]
            arranged = arrange(
                grad_parts, jnp.stack(back_inner), jnp.stack(sources), (outer, inner, far, near, halves, half_rows), [running]
            )
            gathered = [lax.all_gather(half, "outer", axis=0, tiled=False) for half in arranged]
            waits = list(arranged)
    value_parts = [running[0]] + [shifted(running[i], "inner", i) for i in range(1, inner)]

    sent_back = []
    waits = [running]
    for at, half in enumerate(gathered):
        by_near = shares(half, in_weight, received, jnp.stack(chunks), near, waits)
        total = by_near[0].astype(WIDE) + sum(shifted(by_near[n], "near", n).astype(WIDE) for n in range(1, near))
        total = total.astype(SHORT).reshape(inner, far, outer * half_rows, depth)
        if at == 0:
            convolved = convolve(table, spectrum, value_parts, places, [total])
            convolved = convolved.reshape(ctx_size, rows, channels)
            exchanged = lax.all_to_all(convolved, ctx, split_axis=0, concat_axis=0, tiled=True)
        others = [shifted(total[:, f], "far", f) for f in range(1, far)]
        total = total[:, 0].astype(WIDE) + sum(other.astype(WIDE) for other in others)
        total = total.astype(SHORT).reshape(inner, outer, half_rows, depth)
        waits = [convolved, total]
        if split == 1:
            total = total.swapaxes(0, 1)
        else:
            total = turned(list(total), at_inner).reshape(split, tile_blocks, outer, half_rows, depth)
            total = total.transpose(2, 0, 1, 3, 4).reshape(tp, tile_blocks, half_rows, depth)
        back = []
        for step in range(tp):
            pairs = [(destination(o, t, step), o * tp + t) for o in range(outer) for t in range(tp)]
            back.append(lax.ppermute(pick(total, (at_tp - step) % tp), cell, pairs))
        sent_back.append(back)
    row_places = [(at_outer * split + at_tp % split + step) % tp for step in range(tp)]
    block_places = back_inner if split == 1 else [jnp.int32(b) for b in range(tile_blocks)]
    grad_tokens = assemble(sent_back, jnp.stack(row_places), jnp.stack(block_places), columns)

    gated_output, grad_gate = finish(exchanged, gate, cotangent)
    return (gated_output, grad_gate, grad_tokens)


def solution(mesh):
    ctx_size, tp_size = mesh.shape["ctx"], mesh.shape["tp"]
    inner, near = 1, 2
    while inner * inner * 4 <= ctx_size:
        inner *= 2
    fine_mesh = Mesh(
        np.asarray(mesh.devices).reshape(ctx_size // inner, inner, tp_size // near, near),
        ("outer", "inner", "far", "near"),
    )
    placed = P(("outer", "inner"), ("far", "near"))
    return jax.shard_map(
        per_device,
        mesh=fine_mesh,
        in_specs=(placed,) * 5,
        out_specs=(placed,) * 3,
        check_vma=False,
    )
```

```python
import functools
import math

import jax
import jax.numpy as jnp
import numpy as np
from jax import lax
from jax.experimental import pallas as pl
from jax.experimental.pallas import tpu as pltpu
from jax.sharding import Mesh, PartitionSpec as P

TWO_PI = 2.0 * math.pi
WIDE = jnp.float32
SHORT = jnp.bfloat16
LAST_TWO = (((1,), (1,)), ((), ()))


def transform_table(length):
    period = 16 * length
    if length > 2048:
        points = 4 * jnp.arange(length, dtype=jnp.int32) + 1
        angles = (points[:, None] * points[None, :] % period).astype(WIDE) * (TWO_PI / period)
        return [jnp.cos(angles).astype(SHORT), jnp.sin(angles).astype(SHORT)]
    points = 4 * np.arange(length, dtype=np.int64) + 1
    turns = points[:, None] * points[None, :] % period
    angles = np.arange(period) * (TWO_PI / period)
    return [jnp.asarray(wave(angles).astype(SHORT)[turns]) for wave in (np.cos, np.sin)]


def table_block(length):
    return min(512, length // 2)


def rotation(length):
    angle = (4 * jnp.arange(length, dtype=jnp.int32) + 1).astype(WIDE) * (TWO_PI / (16 * length))
    return jnp.stack([jnp.cos(angle), jnp.sin(angle)], axis=1)


def wide_dot(left, right):
    return jnp.dot(left, right, preferred_element_type=WIDE)


def wide_dot_turned(left, right):
    return lax.dot_general(left, right, LAST_TWO, preferred_element_type=WIDE)


def kernel_params(axes):
    return pltpu.CompilerParams(
        dimension_semantics=("arbitrary",) * axes, vmem_limit_bytes=48 * 1024 * 1024
    )


NO_COST = pl.CostEstimate(flops=0, bytes_accessed=0, transcendentals=0)


ANYWHERE = pl.BlockSpec(memory_space=pl.ANY)


def waiting(kernel, count):
    return lambda index_ref, *refs: kernel(index_ref, *refs[count:])


def release_kernel(index_ref, in_ref, out_ref):
    pass


def release(array, waits):
    return pl.pallas_call(
        waiting(release_kernel, len(waits)),
        in_specs=[pl.BlockSpec(memory_space=pltpu.SMEM)] + [ANYWHERE] * (len(waits) + 1),
        out_specs=ANYWHERE,
        out_shape=jax.ShapeDtypeStruct(array.shape, array.dtype),
        input_output_aliases={1 + len(waits): 0},
        compiler_params=kernel_params(0),
        cost_estimate=NO_COST,
    )(jnp.zeros((1,), jnp.int32), *waits, array)


def aligned(index, size):
    return pl.ds(pl.multiple_of(index * size, size), size)


def correlate_kernel(index_ref, cos_ref, sin_ref, turn_ref, *refs):
    both_refs, (out_ref, spectrum_ref, signal_ref, mix_ref) = refs[:2], refs[2:]
    phase, step = pl.program_id(0), pl.program_id(1)
    block = cos_ref.shape[0]
    length, channels = mix_ref.shape[1:]
    rows = aligned(step, block)

    @pl.when((phase == 0) & (step == 0))
    def _():
        for which in range(2):
            signal_ref[:, which * channels : (which + 1) * channels] = both_refs[which][...].reshape(length, channels)

    @pl.when(phase == 0)
    def _():
        turn_cos, turn_sin = turn_ref[:, 0:1], turn_ref[:, 1:2]
        cos_sums = wide_dot(cos_ref[...], signal_ref[...])
        sin_sums = wide_dot(sin_ref[...], signal_ref[...])
        raw_cos, signal_cos = cos_sums[:, :channels], cos_sums[:, channels:]
        raw_sin, signal_sin = sin_sums[:, :channels], sin_sums[:, channels:]
        filter_cos = raw_cos * turn_cos + raw_sin * turn_sin
        filter_sin = raw_sin * turn_cos - raw_cos * turn_sin
        spectrum_ref[0] = filter_cos.astype(SHORT)
        spectrum_ref[1] = filter_sin.astype(SHORT)
        mix_ref[0, rows] = (signal_cos * filter_cos + signal_sin * filter_sin).astype(SHORT)
        mix_ref[1, rows] = (signal_sin * filter_cos - signal_cos * filter_sin).astype(SHORT)

    @pl.when(phase == 1)
    def _():
        total = wide_dot(cos_ref[...], mix_ref[0]) + wide_dot(sin_ref[...], mix_ref[1])
        out_ref[...] = (total * (1.0 / length)).astype(out_ref.dtype)


def correlate(table, turn, filters, signal, waits):
    parts, rows, channels = filters.shape
    length = parts * rows
    block = table_block(length)
    steps = length // block
    table_spec = pl.BlockSpec((block, length), lambda p, s: (s, 0))
    return pl.pallas_call(
        waiting(correlate_kernel, len(waits)),
        grid=(2, steps),
        in_specs=[
            pl.BlockSpec(memory_space=pltpu.SMEM),
            *[ANYWHERE] * len(waits),
            table_spec,
            table_spec,
            pl.BlockSpec((block, 2), lambda p, s: (s, 0)),
            pl.BlockSpec((parts, rows, channels), lambda p, s: (0, 0, 0)),
            pl.BlockSpec((parts, rows, channels), lambda p, s: (0, 0, 0)),
        ],
        out_specs=[
            pl.BlockSpec((block, channels), lambda p, s: (p * s, 0)),
            pl.BlockSpec((2, block, channels), lambda p, s: (0, s + p * (steps - 1 - s), 0)),
        ],
        out_shape=[
            jax.ShapeDtypeStruct((length, channels), SHORT),
            jax.ShapeDtypeStruct((2, length, channels), SHORT),
        ],
        scratch_shapes=[pltpu.VMEM((length, 2 * channels), SHORT), pltpu.VMEM((2, length, channels), SHORT)],
        compiler_params=kernel_params(2),
        cost_estimate=NO_COST,
    )(jnp.zeros((1,), jnp.int32), *waits, table[0], table[1], turn, filters, signal)


def convolve_kernel(inner, places_ref, cos_ref, sin_ref, spectrum_ref, *refs):
    part_refs, (out_ref, signal_ref, mix_ref) = refs[:inner], refs[inner:]
    phase, step = pl.program_id(0), pl.program_id(1)
    block = cos_ref.shape[0]
    length = signal_ref.shape[0]
    rows = aligned(step, block)
    pieces = places_ref.shape[1]
    size = part_refs[0].shape[0] // pieces

    @pl.when((phase == 0) & (step == 0))
    def _():
        for s in range(inner):
            for p in range(pieces):
                signal_ref[aligned(places_ref[s, p], size)] = part_refs[s][p * size : (p + 1) * size]

    @pl.when(phase == 0)
    def _():
        filter_cos, filter_sin = spectrum_ref[0].astype(WIDE), spectrum_ref[1].astype(WIDE)
        signal_cos = wide_dot(cos_ref[...], signal_ref[...])
        signal_sin = wide_dot(sin_ref[...], signal_ref[...])
        mix_ref[0, rows] = (signal_cos * filter_cos - signal_sin * filter_sin).astype(SHORT)
        mix_ref[1, rows] = (signal_cos * filter_sin + signal_sin * filter_cos).astype(SHORT)

    @pl.when(phase == 1)
    def _():
        total = wide_dot(cos_ref[...], mix_ref[0]) + wide_dot(sin_ref[...], mix_ref[1])
        out_ref[...] = (total * (1.0 / length)).astype(out_ref.dtype)


def convolve(table, spectrum, parts, places, waits):
    length, channels = spectrum.shape[1:]
    block = table_block(length)
    steps = length // block
    table_spec = pl.BlockSpec((block, length), lambda p, s, _: (s, 0))
    return pl.pallas_call(
        waiting(functools.partial(convolve_kernel, len(parts)), len(waits)),
        grid_spec=pltpu.PrefetchScalarGridSpec(
            num_scalar_prefetch=1,
            grid=(2, steps),
            in_specs=[
                *[ANYWHERE] * len(waits),
                table_spec,
                table_spec,
                pl.BlockSpec((2, block, channels), lambda p, s, _: (0, s + p * (steps - 1 - s), 0)),
            ]
            + [pl.BlockSpec(part.shape, lambda p, s, _: (0, 0)) for part in parts],
            out_specs=pl.BlockSpec((block, channels), lambda p, s, _: (p * s, 0)),
            scratch_shapes=[pltpu.VMEM((length, channels), SHORT), pltpu.VMEM((2, length, channels), SHORT)],
        ),
        out_shape=jax.ShapeDtypeStruct((length, channels), SHORT),
        compiler_params=kernel_params(2),
        cost_estimate=NO_COST,
    )(places, *waits, table[0], table[1], spectrum, *parts)


def prepare_kernel(index_ref, *refs):
    total = refs[0][...].astype(WIDE)
    for ref in refs[1:-1]:
        total = total * ref[...].astype(WIDE)
    refs[-1][0] = total.astype(SHORT)


def prepare(factors, groups, waits):
    rows, width = factors[0].shape
    channels = width // groups
    if channels % 128:
        total = functools.reduce(lambda x, y: x * y, [factor.astype(WIDE) for factor in factors])
        return total.astype(SHORT).reshape(rows, groups, channels).swapaxes(0, 1)
    spec = pl.BlockSpec((rows, channels), lambda g: (0, g))
    return pl.pallas_call(
        waiting(prepare_kernel, len(waits)),
        grid=(groups,),
        in_specs=[pl.BlockSpec(memory_space=pltpu.SMEM)] + [ANYWHERE] * len(waits) + [spec] * len(factors),
        out_specs=pl.BlockSpec((1, rows, channels), lambda g: (g, 0, 0)),
        out_shape=jax.ShapeDtypeStruct((groups, rows, channels), SHORT),
        compiler_params=kernel_params(1),
        cost_estimate=NO_COST,
    )(jnp.zeros((1,), jnp.int32), *waits, *factors)


def finish_kernel(convolved_ref, gate_ref, cotangent_ref, output_ref, grad_ref):
    convolved = convolved_ref[0].astype(WIDE)
    output_ref[...] = (gate_ref[...].astype(WIDE) * convolved).astype(SHORT)
    grad_ref[...] = (cotangent_ref[...].astype(WIDE) * convolved).astype(SHORT)


def finish(convolved, gate, cotangent):
    groups, rows, channels = convolved.shape
    width = groups * channels
    if channels % 128:
        wide = convolved.swapaxes(0, 1).reshape(rows, width).astype(WIDE)
        return [(other.astype(WIDE) * wide).astype(SHORT) for other in (gate, cotangent)]
    spec = pl.BlockSpec((rows, channels), lambda g: (0, g))
    return pl.pallas_call(
        finish_kernel,
        grid=(groups,),
        in_specs=[pl.BlockSpec((1, rows, channels), lambda g: (g, 0, 0)), spec, spec],
        out_specs=[spec, spec],
        out_shape=[jax.ShapeDtypeStruct((rows, width), SHORT)] * 2,
        compiler_params=kernel_params(1),
        cost_estimate=NO_COST,
    )(convolved, gate, cotangent)


def arrange_kernel(dims, index_ref, *refs):
    outer, inner, far, near, halves, half_rows = dims
    part_refs, out_refs = refs[:inner], refs[inner:]
    channels = part_refs[0].shape[-1]
    tp = far * near
    for s in range(inner):
        lanes = aligned(index_ref[s], channels)
        for ahead in range(tp):
            source = index_ref[inner + ahead]
            for o in range(outer):
                for h in range(halves):
                    place = (ahead * outer + o) * half_rows
                    piece = part_refs[s][o, aligned(source * halves + h, half_rows)]
                    out_refs[h][place : place + half_rows, lanes] = piece


def arrange(parts, inner_places, sources, dims, waits):
    outer, inner, far, near, halves, half_rows = dims
    channels = parts[0].shape[-1]
    tp = far * near
    shape = (tp * outer * half_rows, inner * channels)
    if channels % 128:
        slots = jnp.zeros((inner, *parts[0].shape), SHORT)
        for s in range(inner):
            slots = lax.dynamic_update_index_in_dim(slots, parts[s], inner_places[s], 0)
        slots = slots.reshape(inner, outer, tp, halves, half_rows, channels).transpose(2, 3, 1, 4, 0, 5)
        slots = jnp.stack([pick(slots, sources[a]) for a in range(tp)])
        return [slots[:, h].reshape(shape) for h in range(halves)]
    index = jnp.concatenate([inner_places, sources]).astype(jnp.int32)
    size = math.prod(shape) * 2
    return pl.pallas_call(
        waiting(functools.partial(arrange_kernel, dims), len(waits)),
        in_specs=[pl.BlockSpec(memory_space=pltpu.SMEM)]
        + [ANYWHERE] * len(waits)
        + [pl.BlockSpec(memory_space=pltpu.VMEM)] * inner,
        out_specs=[pl.BlockSpec(memory_space=pltpu.VMEM)] * halves,
        out_shape=[jax.ShapeDtypeStruct(shape, SHORT)] * halves,
        compiler_params=kernel_params(0),
        cost_estimate=NO_COST,
    )(index, *waits, *parts)


def assemble_kernel(dims, index_ref, *refs):
    halves, steps, blocks, half_rows, depth = dims
    out_ref = refs[-1]
    for h in range(halves):
        for s in range(steps):
            rows = aligned(index_ref[s] * halves + h, half_rows)
            for b in range(blocks):
                out_ref[rows, aligned(index_ref[steps + b], depth)] = refs[h * steps + s][b]


def assemble(pieces, row_places, block_places, columns):
    halves, steps = len(pieces), len(pieces[0])
    blocks, half_rows, depth = pieces[0][0].shape
    flat = [piece for half in pieces for piece in half]
    rows = halves * steps * half_rows
    return pl.pallas_call(
        functools.partial(assemble_kernel, (halves, steps, blocks, half_rows, depth)),
        in_specs=[pl.BlockSpec(memory_space=pltpu.SMEM)] + [pl.BlockSpec(memory_space=pltpu.VMEM)] * len(flat),
        out_specs=pl.BlockSpec(memory_space=pltpu.VMEM),
        out_shape=jax.ShapeDtypeStruct((rows, columns), SHORT),
        compiler_params=kernel_params(0),
        cost_estimate=NO_COST,
    )(jnp.concatenate([row_places, block_places]).astype(jnp.int32), *flat)


def chunk_kernel(index_ref, in_ref, out_ref):
    out_ref[...] = in_ref[...]


def chunks_of(array, indices, count, waits=()):
    rows, width = array.shape
    chunk = width // count
    block = min(rows, 1024)
    if chunk % 128:
        return jnp.concatenate([lax.dynamic_slice_in_dim(array, i * chunk, chunk, 1) for i in indices], axis=1)
    return pl.pallas_call(
        waiting(chunk_kernel, len(waits)),
        grid_spec=pltpu.PrefetchScalarGridSpec(
            num_scalar_prefetch=1,
            grid=(rows // block, len(indices)),
            in_specs=[ANYWHERE] * len(waits) + [pl.BlockSpec((block, chunk), lambda r, c, index: (r, index[c]))],
            out_specs=pl.BlockSpec((block, chunk), lambda r, c, _: (r, c)),
        ),
        out_shape=jax.ShapeDtypeStruct((rows, len(indices) * chunk), array.dtype),
        compiler_params=kernel_params(2),
        cost_estimate=NO_COST,
    )(jnp.stack(indices).astype(jnp.int32), *waits, array)


def join_kernel(index_ref, *refs):
    size = refs[0].shape[0]
    for p, ref in enumerate(refs[:-1]):
        refs[-1][p * size : (p + 1) * size] = ref[...]


def join(parts, waits):
    size, width = parts[0].shape
    rows = len(parts) * size
    if size % 16:
        return jnp.concatenate(parts, axis=0)
    return pl.pallas_call(
        waiting(join_kernel, len(waits)),
        in_specs=[pl.BlockSpec(memory_space=pltpu.SMEM)]
        + [ANYWHERE] * len(waits)
        + [pl.BlockSpec(memory_space=pltpu.VMEM)] * len(parts),
        out_specs=pl.BlockSpec(memory_space=pltpu.VMEM),
        out_shape=jax.ShapeDtypeStruct((rows, width), parts[0].dtype),
        compiler_params=kernel_params(0),
        cost_estimate=NO_COST,
    )(jnp.zeros((1,), jnp.int32), *waits, *parts)


def product_kernel(dims, index_ref, *refs):
    inner, outer, pieces, depth, add = dims
    token_refs, weight_refs, (out_ref, joined_ref) = refs[:pieces], refs[pieces : pieces + inner], refs[-2:]
    size = token_refs[0].shape[0] // outer

    @pl.when(pl.program_id(0) == 0)
    def _():
        for p in range(pieces):
            for o in range(outer):
                rows = aligned(index_ref[2 + inner + o], size)
                place = (p * outer + o) * size
                joined_ref[place : place + size] = token_refs[p][rows]

    total = refs[-3][...].astype(WIDE) if add else 0.0
    for i in range(inner):
        columns = aligned(index_ref[2 + i], depth)
        total = total + wide_dot(joined_ref[:, columns], weight_refs[i][...])
    out_ref[...] = total.astype(SHORT).reshape(out_ref.shape)


def product(pieces, in_weight, chunk_index, received, inner_blocks, row_order, running, last, waits):
    inner = len(received) + 1
    outer = row_order.shape[0]
    depth, width = in_weight.shape
    chunk = width // outer
    channels = chunk // inner
    size, whole_depth = pieces[0].shape
    rows = len(pieces) * size
    at_inner = inner_blocks[0]
    if channels % 128:
        tokens = jnp.stack(pieces).reshape(len(pieces), outer, size // outer, whole_depth)
        tokens = jnp.concatenate([pick(tokens, row_order[s], 1)[:, None] for s in range(outer)], axis=1)
        tokens = tokens.reshape(rows, whole_depth)
        weights = [chunks_of(in_weight, [chunk_index], outer)]
        weights += [held[:, at * chunk : (at + 1) * chunk] for held, at in received]
        total = sum(
            wide_dot(lax.dynamic_slice_in_dim(tokens, inner_blocks[i] * depth, depth, 1), weights[i])
            for i in range(inner)
        )
        if running is not None:
            total = total + running.astype(WIDE)
        total = total.astype(SHORT)
        if last:
            total = total.reshape(rows, inner, channels)
            total = jnp.stack([pick(total, (at_inner + i) % inner, 1) for i in range(inner)])
        return total
    if last:
        out_spec = pl.BlockSpec((1, rows, channels), lambda g, index: ((g + inner - index[2]) % inner, 0, 0))
        out_shape = (inner, rows, channels)
    else:
        out_spec = pl.BlockSpec((rows, channels), lambda g, _: (0, g))
        out_shape = (rows, chunk)
    index = jnp.concatenate([chunk_index[None], at_inner[None], inner_blocks, row_order]).astype(jnp.int32)
    return pl.pallas_call(
        waiting(
            functools.partial(product_kernel, (inner, outer, len(pieces), depth, running is not None)), len(waits)
        ),
        grid_spec=pltpu.PrefetchScalarGridSpec(
            num_scalar_prefetch=1,
            grid=(inner,),
            in_specs=[ANYWHERE] * len(waits)
            + [pl.BlockSpec((size, whole_depth), lambda g, _: (0, 0)) for _ in pieces]
            + [pl.BlockSpec((depth, channels), lambda g, index: (0, index[0] * inner + g))]
            + [
                pl.BlockSpec((depth, channels), lambda g, _, at=at: (0, at * inner + g)) for _, at in received
            ]
            + ([] if running is None else [pl.BlockSpec((rows, channels), lambda g, _: (0, g))]),
            out_specs=out_spec,
            scratch_shapes=[pltpu.VMEM((rows, whole_depth), SHORT)],
        ),
        out_shape=jax.ShapeDtypeStruct(out_shape, SHORT),
        compiler_params=kernel_params(1),
        cost_estimate=NO_COST,
    )(index, *waits, *pieces, in_weight, *[held for held, _ in received], *([] if running is None else [running]))


def shares_kernel(dims, index_ref, grad_ref, *refs):
    outer, inner, near, chunk = dims
    own_ref, received_refs = refs[0], refs[1 : 1 + (inner - 1) * outer]
    out_refs, plain_ref = refs[1 + (inner - 1) * outer : -1], refs[-1]
    size = out_refs[0].shape[1]

    @pl.when(pl.program_id(0) == 0)
    def _():
        for o in range(outer):
            plain_ref[:, o * chunk : (o + 1) * chunk] = grad_ref[o]

    for i in range(inner):
        if i == 0:
            total = wide_dot_turned(plain_ref[...], own_ref[...])
        else:
            total = sum(
                wide_dot_turned(grad_ref[index_ref[s]], received_refs[(i - 1) * outer + s][...]) for s in range(outer)
            )
        total = total.astype(SHORT)
        for n in range(near):
            out_refs[n][i] = total[n * size : (n + 1) * size]


def shares(grad_values, in_weight, received, chunks, near, waits):
    outer, rows, chunk = grad_values.shape
    inner = len(received) + 1
    depth, width = in_weight.shape
    if chunk // inner % 128:
        plain = grad_values.swapaxes(0, 1).reshape(rows, width)
        totals = [wide_dot_turned(plain, in_weight)] + [
            sum(
                wide_dot_turned(pick(grad_values, chunks[s]), held[s][0][:, held[s][1] * chunk : (held[s][1] + 1) * chunk])
                for s in range(outer)
            )
            for held in received
        ]
        total = jnp.stack(totals).astype(SHORT).reshape(inner, near, rows // near, depth)
        return [total[:, n] for n in range(near)]
    block = min(depth, 256)
    flat = [w for held in received for w in held]
    out_spec = pl.BlockSpec((inner, rows // near, block), lambda k, _: (0, 0, k))
    return pl.pallas_call(
        waiting(functools.partial(shares_kernel, (outer, inner, near, chunk)), len(waits)),
        grid_spec=pltpu.PrefetchScalarGridSpec(
            num_scalar_prefetch=1,
            grid=(depth // block,),
            in_specs=[ANYWHERE] * len(waits)
            + [pl.BlockSpec((outer, rows, chunk), lambda k, _: (0, 0, 0))]
            + [pl.BlockSpec((block, width), lambda k, _: (k, 0))]
            + [pl.BlockSpec((block, chunk), lambda k, _, at=at: (k, at)) for _, at in flat],
            out_specs=[out_spec] * near,
            scratch_shapes=[pltpu.VMEM((rows, width), SHORT)],
        ),
        out_shape=[jax.ShapeDtypeStruct((inner, rows // near, depth), SHORT)] * near,
        compiler_params=kernel_params(1),
        cost_estimate=NO_COST,
    )(chunks.astype(jnp.int32), *waits, grad_values, in_weight, *[held for held, _ in flat])


def shifted(array, axis, shift):
    size = lax.axis_size(axis)
    return lax.ppermute(array, axis, [(at, (at + shift) % size) for at in range(size)])


def pick(array, index, axis=0):
    return lax.dynamic_index_in_dim(array, index, axis, keepdims=False)


def turned(parts, start):
    count = len(parts)
    backwards = jnp.stack(parts[::-1])
    doubled = jnp.concatenate([backwards, backwards], axis=0)
    return lax.dynamic_slice_in_dim(doubled, (count - 1 - start) % count, count, 0)


def per_device(tokens, in_weight, filters, gate, cotangent):
    outer, inner, far, near = (lax.axis_size(a) for a in ("outer", "inner", "far", "near"))
    at_outer, at_inner, at_far, at_near = (lax.axis_index(a) for a in ("outer", "inner", "far", "near"))
    tp = far * near
    at_tp = at_far * near + at_near
    rows, columns = tokens.shape
    fine_rows = rows // tp
    halves = 2 if fine_rows >= 32 else 1
    half_rows = fine_rows // halves
    ctx = ("outer", "inner")
    ctx_size = outer * inner
    cell = ("outer", "far", "near")
    split = tp // outer
    depth, width = in_weight.shape
    channels = width // ctx_size
    tile_blocks = columns // depth
    length = ctx_size * rows
    back_inner = [(at_inner - i) % inner for i in range(inner)]

    def destination(source_outer, source_tp, step):
        part = (source_outer * split + source_tp % split + step) % tp
        return (source_tp // split) * tp + part

    chunks = [(at_outer - s) % outer for s in range(outer)]
    order = [s % outer for s in range(1, outer + 1)]
    received = [[None] * outer for _ in range(1, inner)]
    arrivals = []

    def send_chunks(some, waits):
        sent = chunks_of(in_weight, [chunks[s] for s in some], outer, waits)
        arrivals.append([shifted(sent, "inner", i) for i in range(1, inner)])
        for i in range(1, inner):
            for at, s in enumerate(some):
                received[i - 1][s] = (arrivals[-1][i - 1], at)
        return sent

    moved = []
    if split == 1:
        by_far = tokens.reshape(far, near * fine_rows, columns)
        by_far = [pick(by_far, (at_far + f) % far) for f in range(far)]
        own_filters = prepare([filters], ctx_size, by_far[1:])
        all_filters = lax.all_to_all(own_filters, ctx, split_axis=0, concat_axis=0, tiled=True)
        sent = send_chunks(order[:2], [own_filters])
        prepared = prepare([cotangent, gate], ctx_size, [sent])
        held = [by_far[0]] + [shifted(by_far[f], "far", f) for f in range(1, far)]
        held = jnp.stack(held).reshape(far, near, fine_rows, columns)
        for step in range(tp):
            pairs = []
            for o in range(outer):
                for g in range(far):
                    for c in range(near):
                        tile, part = (o + step) % tp // near, (o + step) % tp % near
                        pairs.append(((o * far + g) * near + c, ((tile * near + c) * far + g) * near + part))
            number = (at_outer + step) % tp
            part = lax.dynamic_slice(
                held, ((at_far - number // near) % far, number % near, 0, 0), (1, 1, fine_rows, columns)
            )
            moved.append(lax.ppermute(part.reshape(fine_rows, columns), cell, pairs))
        token_part = join(moved, [prepared, all_filters, *arrivals[0]])
    else:
        own_filters = prepare([filters], ctx_size, [])
        all_filters = lax.all_to_all(own_filters, ctx, split_axis=0, concat_axis=0, tiled=True)
        sent = send_chunks(order[:2], [own_filters])
        prepared = prepare([cotangent, gate], ctx_size, [sent])
        row_parts = tokens.reshape(tp, fine_rows, columns)
        for step in range(tp):
            pairs = [(o * tp + t, destination(o, t, step)) for o in range(outer) for t in range(tp)]
            part = (at_outer * split + at_tp % split + step) % tp
            moved.append(lax.ppermute(pick(row_parts, part), cell, pairs))
        token_part = turned(moved, at_tp).reshape(outer, split, fine_rows, columns).swapaxes(1, 2)
        token_part = token_part.reshape(outer * fine_rows, split * columns)

    signal_rows = lax.all_to_all(release(prepared, [token_part]), ctx, split_axis=0, concat_axis=0, tiled=True)
    sent = token_part
    for s in order[2:]:
        sent = send_chunks([s], [sent, *arrivals[0]])
    table = transform_table(length)

    pieces = [token_part] + [shifted(token_part, "far", f) for f in range(1, far)]
    pieces = pieces + [shifted(piece, "near", n) for n in range(1, near) for piece in pieces]
    places = []
    for n in range(near):
        for f in range(far):
            source_near = (at_near - n) % near
            source = (at_far - f) % far * near + source_near
            for s in range(outer):
                source_outer = (source_near - s) % outer if split == 1 else s
                places.append(source_outer * (inner * tp) + source)
    places = jnp.stack(places).astype(jnp.int32)
    places = jnp.stack([places + back_inner[s] * tp for s in range(inner)])

    blocks = jnp.stack(back_inner)
    turn = at_outer // near * near if split == 1 else 0
    row_order = jnp.stack([(s + turn) % outer + at_outer * 0 for s in range(outer)])
    running = None
    waits = [sent]
    for s in order:
        if running is not None:
            running = shifted(running, "outer", 1)
        held = [chunk[s] for chunk in received]
        running = product(pieces, in_weight, chunks[s], held, blocks, row_order, running, s == 0, waits)
        waits = []
        if s == 1:
            grad_values, spectrum = correlate(table, rotation(length), all_filters, signal_rows, [running])
            by_inner = grad_values.reshape(outer, inner, rows, channels)
            grad_parts = [pick(by_inner, at_inner, 1)]
            for i in range(1, inner):
                grad_parts.append(shifted(pick(by_inner, (at_inner + i) % inner, 1), "inner", i))
            waits = [spectrum, *arrivals[1]]
        if s == 2:
            sources = [(at_far + f) % far * near + (at_near + n) % near for n in range(near) for f in range(far)]
            arranged = arrange(
                grad_parts, jnp.stack(back_inner), jnp.stack(sources), (outer, inner, far, near, halves, half_rows), [running]
            )
            gathered = [lax.all_gather(half, "outer", axis=0, tiled=False) for half in arranged]
            waits = list(arranged) + arrivals[-1]
    value_parts = [running[0]] + [shifted(running[i], "inner", i) for i in range(1, inner)]

    sent_back = []
    waits = [running]
    for at, half in enumerate(gathered):
        by_near = shares(half, in_weight, received, jnp.stack(chunks), near, waits)
        total = by_near[0].astype(WIDE) + sum(shifted(by_near[n], "near", n).astype(WIDE) for n in range(1, near))
        total = total.astype(SHORT).reshape(inner, far, outer * half_rows, depth)
        if at == 0:
            convolved = convolve(table, spectrum, value_parts, places, [total])
            convolved = convolved.reshape(ctx_size, rows, channels)
            exchanged = lax.all_to_all(convolved, ctx, split_axis=0, concat_axis=0, tiled=True)
        others = [shifted(total[:, f], "far", f) for f in range(1, far)]
        total = total[:, 0].astype(WIDE) + sum(other.astype(WIDE) for other in others)
        total = total.astype(SHORT).reshape(inner, outer, half_rows, depth)
        waits = [convolved, total]
        if split == 1:
            total = total.swapaxes(0, 1)
        else:
            total = turned(list(total), at_inner).reshape(split, tile_blocks, outer, half_rows, depth)
            total = total.transpose(2, 0, 1, 3, 4).reshape(tp, tile_blocks, half_rows, depth)
        back = []
        for step in range(tp):
            pairs = [(destination(o, t, step), o * tp + t) for o in range(outer) for t in range(tp)]
            back.append(lax.ppermute(pick(total, (at_tp - step) % tp), cell, pairs))
        sent_back.append(back)
    row_places = [(at_outer * split + at_tp % split + step) % tp for step in range(tp)]
    block_places = back_inner if split == 1 else [jnp.int32(b) for b in range(tile_blocks)]
    grad_tokens = assemble(sent_back, jnp.stack(row_places), jnp.stack(block_places), columns)

    gated_output, grad_gate = finish(exchanged, gate, cotangent)
    return (gated_output, grad_gate, grad_tokens)


def solution(mesh):
    ctx_size, tp_size = mesh.shape["ctx"], mesh.shape["tp"]
    inner, near = 1, 2
    while inner * inner * 4 <= ctx_size:
        inner *= 2
    fine_mesh = Mesh(
        np.asarray(mesh.devices).reshape(ctx_size // inner, inner, tp_size // near, near),
        ("outer", "inner", "far", "near"),
    )
    placed = P(("outer", "inner"), ("far", "near"))
    return jax.shard_map(
        per_device,
        mesh=fine_mesh,
        in_specs=(placed,) * 5,
        out_specs=(placed,) * 3,
        check_vma=False,
    )
```

```python
import functools
import math

import jax
import jax.numpy as jnp
import numpy as np
from jax import lax
from jax.experimental import pallas as pl
from jax.experimental.pallas import tpu as pltpu
from jax.sharding import Mesh, PartitionSpec as P

TWO_PI = 2.0 * math.pi
WIDE = jnp.float32
SHORT = jnp.bfloat16
LAST_TWO = (((1,), (1,)), ((), ()))


def transform_table(length):
    period = 16 * length
    if length > 2048:
        points = 4 * jnp.arange(length, dtype=jnp.int32) + 1
        angles = (points[:, None] * points[None, :] % period).astype(WIDE) * (TWO_PI / period)
        return [jnp.cos(angles).astype(SHORT), jnp.sin(angles).astype(SHORT)]
    points = 4 * np.arange(length, dtype=np.int64) + 1
    turns = points[:, None] * points[None, :] % period
    angles = np.arange(period) * (TWO_PI / period)
    return [jnp.asarray(wave(angles).astype(SHORT)[turns]) for wave in (np.cos, np.sin)]


def table_block(length):
    return min(512, length // 2)


def rotation(length):
    angle = (4 * jnp.arange(length, dtype=jnp.int32) + 1).astype(WIDE) * (TWO_PI / (16 * length))
    return jnp.stack([jnp.cos(angle), jnp.sin(angle)], axis=1)


def wide_dot(left, right):
    return jnp.dot(left, right, preferred_element_type=WIDE)


def wide_dot_turned(left, right):
    return lax.dot_general(left, right, LAST_TWO, preferred_element_type=WIDE)


def kernel_params(axes):
    return pltpu.CompilerParams(
        dimension_semantics=("arbitrary",) * axes, vmem_limit_bytes=48 * 1024 * 1024
    )


NO_COST = pl.CostEstimate(flops=0, bytes_accessed=0, transcendentals=0)


ANYWHERE = pl.BlockSpec(memory_space=pl.ANY)


def waiting(kernel, count):
    return lambda index_ref, *refs: kernel(index_ref, *refs[count:])


def release_kernel(index_ref, in_ref, out_ref):
    pass


def release(array, waits):
    return pl.pallas_call(
        waiting(release_kernel, len(waits)),
        in_specs=[pl.BlockSpec(memory_space=pltpu.SMEM)] + [ANYWHERE] * (len(waits) + 1),
        out_specs=ANYWHERE,
        out_shape=jax.ShapeDtypeStruct(array.shape, array.dtype),
        input_output_aliases={1 + len(waits): 0},
        compiler_params=kernel_params(0),
        cost_estimate=NO_COST,
    )(jnp.zeros((1,), jnp.int32), *waits, array)


def aligned(index, size):
    return pl.ds(pl.multiple_of(index * size, size), size)


def correlate_kernel(index_ref, cos_ref, sin_ref, turn_ref, *refs):
    both_refs, (out_ref, spectrum_ref, signal_ref, mix_ref) = refs[:2], refs[2:]
    phase, step = pl.program_id(0), pl.program_id(1)
    block = cos_ref.shape[0]
    length, channels = mix_ref.shape[1:]
    rows = aligned(step, block)

    @pl.when((phase == 0) & (step == 0))
    def _():
        for which in range(2):
            signal_ref[:, which * channels : (which + 1) * channels] = both_refs[which][...].reshape(length, channels)

    @pl.when(phase == 0)
    def _():
        turn_cos, turn_sin = turn_ref[:, 0:1], turn_ref[:, 1:2]
        cos_sums = wide_dot(cos_ref[...], signal_ref[...])
        sin_sums = wide_dot(sin_ref[...], signal_ref[...])
        raw_cos, signal_cos = cos_sums[:, :channels], cos_sums[:, channels:]
        raw_sin, signal_sin = sin_sums[:, :channels], sin_sums[:, channels:]
        filter_cos = raw_cos * turn_cos + raw_sin * turn_sin
        filter_sin = raw_sin * turn_cos - raw_cos * turn_sin
        spectrum_ref[0] = filter_cos.astype(SHORT)
        spectrum_ref[1] = filter_sin.astype(SHORT)
        mix_ref[0, rows] = (signal_cos * filter_cos + signal_sin * filter_sin).astype(SHORT)
        mix_ref[1, rows] = (signal_sin * filter_cos - signal_cos * filter_sin).astype(SHORT)

    @pl.when(phase == 1)
    def _():
        total = wide_dot(cos_ref[...], mix_ref[0]) + wide_dot(sin_ref[...], mix_ref[1])
        out_ref[...] = (total * (1.0 / length)).astype(out_ref.dtype)


def correlate(table, turn, filters, signal, waits):
    parts, rows, channels = filters.shape
    length = parts * rows
    block = table_block(length)
    steps = length // block
    table_spec = pl.BlockSpec((block, length), lambda p, s: (s, 0))
    return pl.pallas_call(
        waiting(correlate_kernel, len(waits)),
        grid=(2, steps),
        in_specs=[
            pl.BlockSpec(memory_space=pltpu.SMEM),
            *[ANYWHERE] * len(waits),
            table_spec,
            table_spec,
            pl.BlockSpec((block, 2), lambda p, s: (s, 0)),
            pl.BlockSpec((parts, rows, channels), lambda p, s: (0, 0, 0)),
            pl.BlockSpec((parts, rows, channels), lambda p, s: (0, 0, 0)),
        ],
        out_specs=[
            pl.BlockSpec((block, channels), lambda p, s: (p * s, 0)),
            pl.BlockSpec((2, block, channels), lambda p, s: (0, s + p * (steps - 1 - s), 0)),
        ],
        out_shape=[
            jax.ShapeDtypeStruct((length, channels), SHORT),
            jax.ShapeDtypeStruct((2, length, channels), SHORT),
        ],
        scratch_shapes=[pltpu.VMEM((length, 2 * channels), SHORT), pltpu.VMEM((2, length, channels), SHORT)],
        compiler_params=kernel_params(2),
        cost_estimate=NO_COST,
    )(jnp.zeros((1,), jnp.int32), *waits, table[0], table[1], turn, filters, signal)


def convolve_kernel(inner, places_ref, cos_ref, sin_ref, spectrum_ref, *refs):
    part_refs, (out_ref, signal_ref, mix_ref) = refs[:inner], refs[inner:]
    phase, step = pl.program_id(0), pl.program_id(1)
    block = cos_ref.shape[0]
    length = signal_ref.shape[0]
    rows = aligned(step, block)
    pieces = places_ref.shape[1]
    size = part_refs[0].shape[0] // pieces

    @pl.when((phase == 0) & (step == 0))
    def _():
        for s in range(inner):
            for p in range(pieces):
                signal_ref[aligned(places_ref[s, p], size)] = part_refs[s][p * size : (p + 1) * size]

    @pl.when(phase == 0)
    def _():
        filter_cos, filter_sin = spectrum_ref[0].astype(WIDE), spectrum_ref[1].astype(WIDE)
        signal_cos = wide_dot(cos_ref[...], signal_ref[...])
        signal_sin = wide_dot(sin_ref[...], signal_ref[...])
        mix_ref[0, rows] = (signal_cos * filter_cos - signal_sin * filter_sin).astype(SHORT)
        mix_ref[1, rows] = (signal_cos * filter_sin + signal_sin * filter_cos).astype(SHORT)

    @pl.when(phase == 1)
    def _():
        total = wide_dot(cos_ref[...], mix_ref[0]) + wide_dot(sin_ref[...], mix_ref[1])
        out_ref[...] = (total * (1.0 / length)).astype(out_ref.dtype)


def convolve(table, spectrum, parts, places, waits):
    length, channels = spectrum.shape[1:]
    block = table_block(length)
    steps = length // block
    table_spec = pl.BlockSpec((block, length), lambda p, s, _: (s, 0))
    return pl.pallas_call(
        waiting(functools.partial(convolve_kernel, len(parts)), len(waits)),
        grid_spec=pltpu.PrefetchScalarGridSpec(
            num_scalar_prefetch=1,
            grid=(2, steps),
            in_specs=[
                *[ANYWHERE] * len(waits),
                table_spec,
                table_spec,
                pl.BlockSpec((2, block, channels), lambda p, s, _: (0, s + p * (steps - 1 - s), 0)),
            ]
            + [pl.BlockSpec(part.shape, lambda p, s, _: (0, 0)) for part in parts],
            out_specs=pl.BlockSpec((block, channels), lambda p, s, _: (p * s, 0)),
            scratch_shapes=[pltpu.VMEM((length, channels), SHORT), pltpu.VMEM((2, length, channels), SHORT)],
        ),
        out_shape=jax.ShapeDtypeStruct((length, channels), SHORT),
        compiler_params=kernel_params(2),
        cost_estimate=NO_COST,
    )(places, *waits, table[0], table[1], spectrum, *parts)


def prepare_kernel(index_ref, *refs):
    total = refs[0][...].astype(WIDE)
    for ref in refs[1:-1]:
        total = total * ref[...].astype(WIDE)
    refs[-1][0] = total.astype(SHORT)


def prepare(factors, groups, waits):
    rows, width = factors[0].shape
    channels = width // groups
    if channels % 128:
        total = functools.reduce(lambda x, y: x * y, [factor.astype(WIDE) for factor in factors])
        return total.astype(SHORT).reshape(rows, groups, channels).swapaxes(0, 1)
    spec = pl.BlockSpec((rows, channels), lambda g: (0, g))
    return pl.pallas_call(
        waiting(prepare_kernel, len(waits)),
        grid=(groups,),
        in_specs=[pl.BlockSpec(memory_space=pltpu.SMEM)] + [ANYWHERE] * len(waits) + [spec] * len(factors),
        out_specs=pl.BlockSpec((1, rows, channels), lambda g: (g, 0, 0)),
        out_shape=jax.ShapeDtypeStruct((groups, rows, channels), SHORT),
        compiler_params=kernel_params(1),
        cost_estimate=NO_COST,
    )(jnp.zeros((1,), jnp.int32), *waits, *factors)


def finish_kernel(convolved_ref, gate_ref, cotangent_ref, output_ref, grad_ref):
    convolved = convolved_ref[0].astype(WIDE)
    output_ref[...] = (gate_ref[...].astype(WIDE) * convolved).astype(SHORT)
    grad_ref[...] = (cotangent_ref[...].astype(WIDE) * convolved).astype(SHORT)


def finish(convolved, gate, cotangent):
    groups, rows, channels = convolved.shape
    width = groups * channels
    if channels % 128:
        wide = convolved.swapaxes(0, 1).reshape(rows, width).astype(WIDE)
        return [(other.astype(WIDE) * wide).astype(SHORT) for other in (gate, cotangent)]
    spec = pl.BlockSpec((rows, channels), lambda g: (0, g))
    return pl.pallas_call(
        finish_kernel,
        grid=(groups,),
        in_specs=[pl.BlockSpec((1, rows, channels), lambda g: (g, 0, 0)), spec, spec],
        out_specs=[spec, spec],
        out_shape=[jax.ShapeDtypeStruct((rows, width), SHORT)] * 2,
        compiler_params=kernel_params(1),
        cost_estimate=NO_COST,
    )(convolved, gate, cotangent)


def arrange_kernel(dims, index_ref, *refs):
    outer, inner, far, near, halves, half_rows = dims
    part_refs, out_refs = refs[:inner], refs[inner:]
    channels = part_refs[0].shape[-1]
    tp = far * near
    for s in range(inner):
        lanes = aligned(index_ref[s], channels)
        for ahead in range(tp):
            source = index_ref[inner + ahead]
            for o in range(outer):
                for h in range(halves):
                    place = (ahead * outer + o) * half_rows
                    piece = part_refs[s][o, aligned(source * halves + h, half_rows)]
                    out_refs[h][place : place + half_rows, lanes] = piece


def arrange(parts, inner_places, sources, dims, waits):
    outer, inner, far, near, halves, half_rows = dims
    channels = parts[0].shape[-1]
    tp = far * near
    shape = (tp * outer * half_rows, inner * channels)
    if channels % 128:
        slots = jnp.zeros((inner, *parts[0].shape), SHORT)
        for s in range(inner):
            slots = lax.dynamic_update_index_in_dim(slots, parts[s], inner_places[s], 0)
        slots = slots.reshape(inner, outer, tp, halves, half_rows, channels).transpose(2, 3, 1, 4, 0, 5)
        slots = jnp.stack([pick(slots, sources[a]) for a in range(tp)])
        return [slots[:, h].reshape(shape) for h in range(halves)]
    index = jnp.concatenate([inner_places, sources]).astype(jnp.int32)
    size = math.prod(shape) * 2
    return pl.pallas_call(
        waiting(functools.partial(arrange_kernel, dims), len(waits)),
        in_specs=[pl.BlockSpec(memory_space=pltpu.SMEM)]
        + [ANYWHERE] * len(waits)
        + [pl.BlockSpec(memory_space=pltpu.VMEM)] * inner,
        out_specs=[pl.BlockSpec(memory_space=pltpu.VMEM)] * halves,
        out_shape=[jax.ShapeDtypeStruct(shape, SHORT)] * halves,
        compiler_params=kernel_params(0),
        cost_estimate=NO_COST,
    )(index, *waits, *parts)


def assemble_kernel(dims, index_ref, *refs):
    halves, steps, blocks, half_rows, depth = dims
    out_ref = refs[-1]
    for h in range(halves):
        for s in range(steps):
            rows = aligned(index_ref[s] * halves + h, half_rows)
            for b in range(blocks):
                out_ref[rows, aligned(index_ref[steps + b], depth)] = refs[h * steps + s][b]


def assemble(pieces, row_places, block_places, columns):
    halves, steps = len(pieces), len(pieces[0])
    blocks, half_rows, depth = pieces[0][0].shape
    flat = [piece for half in pieces for piece in half]
    rows = halves * steps * half_rows
    return pl.pallas_call(
        functools.partial(assemble_kernel, (halves, steps, blocks, half_rows, depth)),
        in_specs=[pl.BlockSpec(memory_space=pltpu.SMEM)] + [pl.BlockSpec(memory_space=pltpu.VMEM)] * len(flat),
        out_specs=pl.BlockSpec(memory_space=pltpu.VMEM),
        out_shape=jax.ShapeDtypeStruct((rows, columns), SHORT),
        compiler_params=kernel_params(0),
        cost_estimate=NO_COST,
    )(jnp.concatenate([row_places, block_places]).astype(jnp.int32), *flat)


def chunk_kernel(index_ref, in_ref, out_ref):
    out_ref[...] = in_ref[...]


def chunks_of(array, indices, count, waits=()):
    rows, width = array.shape
    chunk = width // count
    block = min(rows, 1024)
    if chunk % 128:
        return jnp.concatenate([lax.dynamic_slice_in_dim(array, i * chunk, chunk, 1) for i in indices], axis=1)
    return pl.pallas_call(
        waiting(chunk_kernel, len(waits)),
        grid_spec=pltpu.PrefetchScalarGridSpec(
            num_scalar_prefetch=1,
            grid=(rows // block, len(indices)),
            in_specs=[ANYWHERE] * len(waits) + [pl.BlockSpec((block, chunk), lambda r, c, index: (r, index[c]))],
            out_specs=pl.BlockSpec((block, chunk), lambda r, c, _: (r, c)),
        ),
        out_shape=jax.ShapeDtypeStruct((rows, len(indices) * chunk), array.dtype),
        compiler_params=kernel_params(2),
        cost_estimate=NO_COST,
    )(jnp.stack(indices).astype(jnp.int32), *waits, array)


def join_kernel(index_ref, *refs):
    size = refs[0].shape[0]
    for p, ref in enumerate(refs[:-1]):
        refs[-1][p * size : (p + 1) * size] = ref[...]


def join(parts, waits):
    size, width = parts[0].shape
    rows = len(parts) * size
    if size % 16:
        return jnp.concatenate(parts, axis=0)
    return pl.pallas_call(
        waiting(join_kernel, len(waits)),
        in_specs=[pl.BlockSpec(memory_space=pltpu.SMEM)]
        + [ANYWHERE] * len(waits)
        + [pl.BlockSpec(memory_space=pltpu.VMEM)] * len(parts),
        out_specs=pl.BlockSpec(memory_space=pltpu.VMEM),
        out_shape=jax.ShapeDtypeStruct((rows, width), parts[0].dtype),
        compiler_params=kernel_params(0),
        cost_estimate=NO_COST,
    )(jnp.zeros((1,), jnp.int32), *waits, *parts)


def product_kernel(dims, index_ref, *refs):
    inner, outer, pieces, depth, add = dims
    token_refs, weight_refs, (out_ref, joined_ref) = refs[:pieces], refs[pieces : pieces + inner], refs[-2:]
    size = token_refs[0].shape[0] // outer

    @pl.when(pl.program_id(0) == 0)
    def _():
        for p in range(pieces):
            for o in range(outer):
                rows = aligned(index_ref[2 + inner + o], size)
                place = (p * outer + o) * size
                joined_ref[place : place + size] = token_refs[p][rows]

    total = refs[-3][...].astype(WIDE) if add else 0.0
    for i in range(inner):
        columns = aligned(index_ref[2 + i], depth)
        total = total + wide_dot(joined_ref[:, columns], weight_refs[i][...])
    out_ref[...] = total.astype(SHORT).reshape(out_ref.shape)


def product(pieces, in_weight, chunk_index, received, inner_blocks, row_order, running, last, waits):
    inner = len(received) + 1
    outer = row_order.shape[0]
    depth, width = in_weight.shape
    chunk = width // outer
    channels = chunk // inner
    size, whole_depth = pieces[0].shape
    rows = len(pieces) * size
    at_inner = inner_blocks[0]
    if channels % 128:
        tokens = jnp.stack(pieces).reshape(len(pieces), outer, size // outer, whole_depth)
        tokens = jnp.concatenate([pick(tokens, row_order[s], 1)[:, None] for s in range(outer)], axis=1)
        tokens = tokens.reshape(rows, whole_depth)
        weights = [chunks_of(in_weight, [chunk_index], outer)]
        weights += [held[:, at * chunk : (at + 1) * chunk] for held, at in received]
        total = sum(
            wide_dot(lax.dynamic_slice_in_dim(tokens, inner_blocks[i] * depth, depth, 1), weights[i])
            for i in range(inner)
        )
        if running is not None:
            total = total + running.astype(WIDE)
        total = total.astype(SHORT)
        if last:
            total = total.reshape(rows, inner, channels)
            total = jnp.stack([pick(total, (at_inner + i) % inner, 1) for i in range(inner)])
        return total
    if last:
        out_spec = pl.BlockSpec((1, rows, channels), lambda g, index: ((g + inner - index[2]) % inner, 0, 0))
        out_shape = (inner, rows, channels)
    else:
        out_spec = pl.BlockSpec((rows, channels), lambda g, _: (0, g))
        out_shape = (rows, chunk)
    index = jnp.concatenate([chunk_index[None], at_inner[None], inner_blocks, row_order]).astype(jnp.int32)
    return pl.pallas_call(
        waiting(
            functools.partial(product_kernel, (inner, outer, len(pieces), depth, running is not None)), len(waits)
        ),
        grid_spec=pltpu.PrefetchScalarGridSpec(
            num_scalar_prefetch=1,
            grid=(inner,),
            in_specs=[ANYWHERE] * len(waits)
            + [pl.BlockSpec((size, whole_depth), lambda g, _: (0, 0)) for _ in pieces]
            + [pl.BlockSpec((depth, channels), lambda g, index: (0, index[0] * inner + g))]
            + [
                pl.BlockSpec((depth, channels), lambda g, _, at=at: (0, at * inner + g)) for _, at in received
            ]
            + ([] if running is None else [pl.BlockSpec((rows, channels), lambda g, _: (0, g))]),
            out_specs=out_spec,
            scratch_shapes=[pltpu.VMEM((rows, whole_depth), SHORT)],
        ),
        out_shape=jax.ShapeDtypeStruct(out_shape, SHORT),
        compiler_params=kernel_params(1),
        cost_estimate=NO_COST,
    )(index, *waits, *pieces, in_weight, *[held for held, _ in received], *([] if running is None else [running]))


def shares_kernel(dims, index_ref, grad_ref, *refs):
    outer, inner, near, chunk = dims
    own_ref, received_refs = refs[0], refs[1 : 1 + (inner - 1) * outer]
    out_refs, plain_ref = refs[1 + (inner - 1) * outer : -1], refs[-1]
    size = out_refs[0].shape[1]

    @pl.when(pl.program_id(0) == 0)
    def _():
        for o in range(outer):
            plain_ref[:, o * chunk : (o + 1) * chunk] = grad_ref[o]

    for i in range(inner):
        if i == 0:
            total = wide_dot_turned(plain_ref[...], own_ref[...])
        else:
            total = sum(
                wide_dot_turned(grad_ref[index_ref[s]], received_refs[(i - 1) * outer + s][...]) for s in range(outer)
            )
        total = total.astype(SHORT)
        for n in range(near):
            out_refs[n][i] = total[n * size : (n + 1) * size]


def shares(grad_values, in_weight, received, chunks, near, waits):
    outer, rows, chunk = grad_values.shape
    inner = len(received) + 1
    depth, width = in_weight.shape
    if chunk // inner % 128:
        plain = grad_values.swapaxes(0, 1).reshape(rows, width)
        totals = [wide_dot_turned(plain, in_weight)] + [
            sum(
                wide_dot_turned(pick(grad_values, chunks[s]), held[s][0][:, held[s][1] * chunk : (held[s][1] + 1) * chunk])
                for s in range(outer)
            )
            for held in received
        ]
        total = jnp.stack(totals).astype(SHORT).reshape(inner, near, rows // near, depth)
        return [total[:, n] for n in range(near)]
    block = min(depth, 256)
    flat = [w for held in received for w in held]
    out_spec = pl.BlockSpec((inner, rows // near, block), lambda k, _: (0, 0, k))
    return pl.pallas_call(
        waiting(functools.partial(shares_kernel, (outer, inner, near, chunk)), len(waits)),
        grid_spec=pltpu.PrefetchScalarGridSpec(
            num_scalar_prefetch=1,
            grid=(depth // block,),
            in_specs=[ANYWHERE] * len(waits)
            + [pl.BlockSpec((outer, rows, chunk), lambda k, _: (0, 0, 0))]
            + [pl.BlockSpec((block, width), lambda k, _: (k, 0))]
            + [pl.BlockSpec((block, chunk), lambda k, _, at=at: (k, at)) for _, at in flat],
            out_specs=[out_spec] * near,
            scratch_shapes=[pltpu.VMEM((rows, width), SHORT)],
        ),
        out_shape=[jax.ShapeDtypeStruct((inner, rows // near, depth), SHORT)] * near,
        compiler_params=kernel_params(1),
        cost_estimate=NO_COST,
    )(chunks.astype(jnp.int32), *waits, grad_values, in_weight, *[held for held, _ in flat])


def shifted(array, axis, shift):
    size = lax.axis_size(axis)
    return lax.ppermute(array, axis, [(at, (at + shift) % size) for at in range(size)])


def pick(array, index, axis=0):
    return lax.dynamic_index_in_dim(array, index, axis, keepdims=False)


def turned(parts, start):
    count = len(parts)
    backwards = jnp.stack(parts[::-1])
    doubled = jnp.concatenate([backwards, backwards], axis=0)
    return lax.dynamic_slice_in_dim(doubled, (count - 1 - start) % count, count, 0)


def per_device(tokens, in_weight, filters, gate, cotangent):
    outer, inner, far, near = (lax.axis_size(a) for a in ("outer", "inner", "far", "near"))
    at_outer, at_inner, at_far, at_near = (lax.axis_index(a) for a in ("outer", "inner", "far", "near"))
    tp = far * near
    at_tp = at_far * near + at_near
    rows, columns = tokens.shape
    fine_rows = rows // tp
    halves = 2 if fine_rows >= 32 else 1
    half_rows = fine_rows // halves
    ctx = ("outer", "inner")
    ctx_size = outer * inner
    cell = ("outer", "far", "near")
    split = tp // outer
    depth, width = in_weight.shape
    channels = width // ctx_size
    tile_blocks = columns // depth
    length = ctx_size * rows
    back_inner = [(at_inner - i) % inner for i in range(inner)]

    def destination(source_outer, source_tp, step):
        part = (source_outer * split + source_tp % split + step) % tp
        return (source_tp // split) * tp + part

    chunks = [(at_outer - s) % outer for s in range(outer)]
    order = [s % outer for s in range(1, outer + 1)]
    received = [[None] * outer for _ in range(1, inner)]
    arrivals = []

    def send_chunks(some, waits):
        sent = chunks_of(in_weight, [chunks[s] for s in some], outer, waits)
        arrivals.append([shifted(sent, "inner", i) for i in range(1, inner)])
        for i in range(1, inner):
            for at, s in enumerate(some):
                received[i - 1][s] = (arrivals[-1][i - 1], at)
        return sent

    moved = []
    if split == 1:
        by_far = tokens.reshape(far, near * fine_rows, columns)
        by_far = [pick(by_far, (at_far + f) % far) for f in range(far)]
        own_filters = prepare([filters], ctx_size, by_far[1:])
        all_filters = lax.all_to_all(own_filters, ctx, split_axis=0, concat_axis=0, tiled=True)
        sent = send_chunks(order[:2], [own_filters])
        prepared = prepare([cotangent, gate], ctx_size, [sent])
        held = [by_far[0]] + [shifted(by_far[f], "far", f) for f in range(1, far)]
        held = jnp.stack(held).reshape(far, near, fine_rows, columns)
        for step in range(tp):
            pairs = []
            for o in range(outer):
                for g in range(far):
                    for c in range(near):
                        tile, part = (o + step) % tp // near, (o + step) % tp % near
                        pairs.append(((o * far + g) * near + c, ((tile * near + c) * far + g) * near + part))
            number = (at_outer + step) % tp
            part = lax.dynamic_slice(
                held, ((at_far - number // near) % far, number % near, 0, 0), (1, 1, fine_rows, columns)
            )
            moved.append(lax.ppermute(part.reshape(fine_rows, columns), cell, pairs))
        token_part = join(moved, [prepared, all_filters, *arrivals[0]])
    else:
        own_filters = prepare([filters], ctx_size, [])
        all_filters = lax.all_to_all(own_filters, ctx, split_axis=0, concat_axis=0, tiled=True)
        sent = send_chunks(order[:2], [own_filters])
        prepared = prepare([cotangent, gate], ctx_size, [sent])
        row_parts = tokens.reshape(tp, fine_rows, columns)
        for step in range(tp):
            pairs = [(o * tp + t, destination(o, t, step)) for o in range(outer) for t in range(tp)]
            part = (at_outer * split + at_tp % split + step) % tp
            moved.append(lax.ppermute(pick(row_parts, part), cell, pairs))
        token_part = turned(moved, at_tp).reshape(outer, split, fine_rows, columns).swapaxes(1, 2)
        token_part = token_part.reshape(outer * fine_rows, split * columns)

    signal_rows = lax.all_to_all(release(prepared, [token_part]), ctx, split_axis=0, concat_axis=0, tiled=True)
    sent = token_part
    for s in order[2:]:
        sent = send_chunks([s], [sent, *arrivals[0]])
    table = transform_table(length)

    pieces = [token_part] + [shifted(token_part, "far", f) for f in range(1, far)]
    pieces = pieces + [shifted(piece, "near", n) for n in range(1, near) for piece in pieces]
    places = []
    for n in range(near):
        for f in range(far):
            source_near = (at_near - n) % near
            source = (at_far - f) % far * near + source_near
            for s in range(outer):
                source_outer = (source_near - s) % outer if split == 1 else s
                places.append(source_outer * (inner * tp) + source)
    places = jnp.stack(places).astype(jnp.int32)
    places = jnp.stack([places + back_inner[s] * tp for s in range(inner)])

    blocks = jnp.stack(back_inner)
    turn = at_outer // near * near if split == 1 else 0
    row_order = jnp.stack([(s + turn) % outer + at_outer * 0 for s in range(outer)])
    running = None
    waits = [sent]
    for s in order:
        if running is not None:
            running = shifted(running, "outer", 1)
        held = [chunk[s] for chunk in received]
        running = product(pieces, in_weight, chunks[s], held, blocks, row_order, running, s == 0, waits)
        waits = []
        if s == 1:
            grad_values, spectrum = correlate(table, rotation(length), all_filters, signal_rows, [running])
            by_inner = grad_values.reshape(outer, inner, rows, channels)
            grad_parts = [pick(by_inner, at_inner, 1)]
            for i in range(1, inner):
                grad_parts.append(shifted(pick(by_inner, (at_inner + i) % inner, 1), "inner", i))
            waits = [spectrum, *arrivals[1]]
        if s == 2:
            sources = [(at_far + f) % far * near + (at_near + n) % near for n in range(near) for f in range(far)]
            arranged = arrange(
                grad_parts, jnp.stack(back_inner), jnp.stack(sources), (outer, inner, far, near, halves, half_rows), [running]
            )
            gathered = [lax.all_gather(half, "outer", axis=0, tiled=False) for half in arranged]
            waits = list(arranged) + arrivals[-1]
        if s == outer - 1:
            first_shares = shares(gathered[0], in_weight, received, jnp.stack(chunks), near, [running])
            waits = [first_shares[0]]
    value_parts = [running[0]] + [shifted(running[i], "inner", i) for i in range(1, inner)]

    sent_back = []
    for at, half in enumerate(gathered):
        by_near = first_shares
        if at > 0:
            by_near = shares(half, in_weight, received, jnp.stack(chunks), near, waits)
        total = by_near[0].astype(WIDE) + sum(shifted(by_near[n], "near", n).astype(WIDE) for n in range(1, near))
        total = total.astype(SHORT).reshape(inner, far, outer * half_rows, depth)
        if at == 0:
            convolved = convolve(table, spectrum, value_parts, places, [total])
            convolved = convolved.reshape(ctx_size, rows, channels)
            exchanged = lax.all_to_all(convolved, ctx, split_axis=0, concat_axis=0, tiled=True)
        others = [shifted(total[:, f], "far", f) for f in range(1, far)]
        total = total[:, 0].astype(WIDE) + sum(other.astype(WIDE) for other in others)
        total = total.astype(SHORT).reshape(inner, outer, half_rows, depth)
        waits = [convolved, total]
        if split == 1:
            total = total.swapaxes(0, 1)
        else:
            total = turned(list(total), at_inner).reshape(split, tile_blocks, outer, half_rows, depth)
            total = total.transpose(2, 0, 1, 3, 4).reshape(tp, tile_blocks, half_rows, depth)
        back = []
        for step in range(tp):
            pairs = [(destination(o, t, step), o * tp + t) for o in range(outer) for t in range(tp)]
            back.append(lax.ppermute(pick(total, (at_tp - step) % tp), cell, pairs))
        sent_back.append(back)
    row_places = [(at_outer * split + at_tp % split + step) % tp for step in range(tp)]
    block_places = back_inner if split == 1 else [jnp.int32(b) for b in range(tile_blocks)]
    grad_tokens = assemble(sent_back, jnp.stack(row_places), jnp.stack(block_places), columns)

    gated_output, grad_gate = finish(exchanged, gate, cotangent)
    return (gated_output, grad_gate, grad_tokens)


def solution(mesh):
    ctx_size, tp_size = mesh.shape["ctx"], mesh.shape["tp"]
    inner, near = 1, 2
    while inner * inner * 4 <= ctx_size:
        inner *= 2
    fine_mesh = Mesh(
        np.asarray(mesh.devices).reshape(ctx_size // inner, inner, tp_size // near, near),
        ("outer", "inner", "far", "near"),
    )
    placed = P(("outer", "inner"), ("far", "near"))
    return jax.shard_map(
        per_device,
        mesh=fine_mesh,
        in_specs=(placed,) * 5,
        out_specs=(placed,) * 3,
        check_vma=False,
    )
```

```python
import functools
import math

import jax
import jax.numpy as jnp
import numpy as np
from jax import lax
from jax.experimental import pallas as pl
from jax.experimental.pallas import tpu as pltpu
from jax.sharding import Mesh, PartitionSpec as P

TWO_PI = 2.0 * math.pi
WIDE = jnp.float32
SHORT = jnp.bfloat16
LAST_TWO = (((1,), (1,)), ((), ()))


def transform_table(length):
    period = 16 * length
    if length > 2048:
        points = 4 * jnp.arange(length, dtype=jnp.int32) + 1
        angles = (points[:, None] * points[None, :] % period).astype(WIDE) * (TWO_PI / period)
        return [jnp.cos(angles).astype(SHORT), jnp.sin(angles).astype(SHORT)]
    points = 4 * np.arange(length, dtype=np.int64) + 1
    turns = points[:, None] * points[None, :] % period
    angles = np.arange(period) * (TWO_PI / period)
    return [jnp.asarray(wave(angles).astype(SHORT)[turns]) for wave in (np.cos, np.sin)]


def table_block(length):
    return min(512, length // 2)


def rotation(length):
    angle = (4 * jnp.arange(length, dtype=jnp.int32) + 1).astype(WIDE) * (TWO_PI / (16 * length))
    return jnp.stack([jnp.cos(angle), jnp.sin(angle)], axis=1)


def wide_dot(left, right):
    return jnp.dot(left, right, preferred_element_type=WIDE)


def wide_dot_turned(left, right):
    return lax.dot_general(left, right, LAST_TWO, preferred_element_type=WIDE)


def kernel_params(axes):
    return pltpu.CompilerParams(
        dimension_semantics=("arbitrary",) * axes, vmem_limit_bytes=48 * 1024 * 1024
    )


NO_COST = pl.CostEstimate(flops=0, bytes_accessed=0, transcendentals=0)


ANYWHERE = pl.BlockSpec(memory_space=pl.ANY)


def waiting(kernel, count):
    return lambda index_ref, *refs: kernel(index_ref, *refs[count:])


def release_kernel(index_ref, in_ref, out_ref):
    pass


def release(array, waits):
    return pl.pallas_call(
        waiting(release_kernel, len(waits)),
        in_specs=[pl.BlockSpec(memory_space=pltpu.SMEM)] + [ANYWHERE] * (len(waits) + 1),
        out_specs=ANYWHERE,
        out_shape=jax.ShapeDtypeStruct(array.shape, array.dtype),
        input_output_aliases={1 + len(waits): 0},
        compiler_params=kernel_params(0),
        cost_estimate=NO_COST,
    )(jnp.zeros((1,), jnp.int32), *waits, array)


def aligned(index, size):
    return pl.ds(pl.multiple_of(index * size, size), size)


def correlate_kernel(index_ref, cos_ref, sin_ref, turn_ref, both_ref, out_ref, spectrum_ref, signal_ref, mix_ref):
    phase, step = pl.program_id(0), pl.program_id(1)
    block = cos_ref.shape[0]
    length, channels = mix_ref.shape[1:]
    rows = aligned(step, block)

    @pl.when((phase == 0) & (step == 0))
    def _():
        for which in range(2):
            signal_ref[:, which * channels : (which + 1) * channels] = both_ref[:, which].reshape(length, channels)

    @pl.when(phase == 0)
    def _():
        turn_cos, turn_sin = turn_ref[:, 0:1], turn_ref[:, 1:2]
        cos_sums = wide_dot(cos_ref[...], signal_ref[...])
        sin_sums = wide_dot(sin_ref[...], signal_ref[...])
        raw_cos, signal_cos = cos_sums[:, :channels], cos_sums[:, channels:]
        raw_sin, signal_sin = sin_sums[:, :channels], sin_sums[:, channels:]
        filter_cos = raw_cos * turn_cos + raw_sin * turn_sin
        filter_sin = raw_sin * turn_cos - raw_cos * turn_sin
        spectrum_ref[0] = filter_cos.astype(SHORT)
        spectrum_ref[1] = filter_sin.astype(SHORT)
        mix_ref[0, rows] = (signal_cos * filter_cos + signal_sin * filter_sin).astype(SHORT)
        mix_ref[1, rows] = (signal_sin * filter_cos - signal_cos * filter_sin).astype(SHORT)

    @pl.when(phase == 1)
    def _():
        total = wide_dot(cos_ref[...], mix_ref[0]) + wide_dot(sin_ref[...], mix_ref[1])
        out_ref[...] = (total * (1.0 / length)).astype(out_ref.dtype)


def correlate(table, turn, both, waits):
    parts, _, rows, channels = both.shape
    length = parts * rows
    block = table_block(length)
    steps = length // block
    table_spec = pl.BlockSpec((block, length), lambda p, s: (s, 0))
    return pl.pallas_call(
        waiting(correlate_kernel, len(waits)),
        grid=(2, steps),
        in_specs=[
            pl.BlockSpec(memory_space=pltpu.SMEM),
            *[ANYWHERE] * len(waits),
            table_spec,
            table_spec,
            pl.BlockSpec((block, 2), lambda p, s: (s, 0)),
            pl.BlockSpec((parts, 2, rows, channels), lambda p, s: (0, 0, 0, 0)),
        ],
        out_specs=[
            pl.BlockSpec((block, channels), lambda p, s: (p * s, 0)),
            pl.BlockSpec((2, block, channels), lambda p, s: (0, s + p * (steps - 1 - s), 0)),
        ],
        out_shape=[
            jax.ShapeDtypeStruct((length, channels), SHORT),
            jax.ShapeDtypeStruct((2, length, channels), SHORT),
        ],
        scratch_shapes=[pltpu.VMEM((length, 2 * channels), SHORT), pltpu.VMEM((2, length, channels), SHORT)],
        compiler_params=kernel_params(2),
        cost_estimate=NO_COST,
    )(jnp.zeros((1,), jnp.int32), *waits, table[0], table[1], turn, both)


def convolve_kernel(inner, places_ref, cos_ref, sin_ref, spectrum_ref, *refs):
    part_refs, (out_ref, signal_ref, mix_ref) = refs[:inner], refs[inner:]
    phase, step = pl.program_id(0), pl.program_id(1)
    block = cos_ref.shape[0]
    length = signal_ref.shape[0]
    rows = aligned(step, block)
    pieces = places_ref.shape[1]
    size = part_refs[0].shape[0] // pieces

    @pl.when((phase == 0) & (step == 0))
    def _():
        for s in range(inner):
            for p in range(pieces):
                signal_ref[aligned(places_ref[s, p], size)] = part_refs[s][p * size : (p + 1) * size]

    @pl.when(phase == 0)
    def _():
        filter_cos, filter_sin = spectrum_ref[0].astype(WIDE), spectrum_ref[1].astype(WIDE)
        signal_cos = wide_dot(cos_ref[...], signal_ref[...])
        signal_sin = wide_dot(sin_ref[...], signal_ref[...])
        mix_ref[0, rows] = (signal_cos * filter_cos - signal_sin * filter_sin).astype(SHORT)
        mix_ref[1, rows] = (signal_cos * filter_sin + signal_sin * filter_cos).astype(SHORT)

    @pl.when(phase == 1)
    def _():
        total = wide_dot(cos_ref[...], mix_ref[0]) + wide_dot(sin_ref[...], mix_ref[1])
        out_ref[...] = (total * (1.0 / length)).astype(out_ref.dtype)


def convolve(table, spectrum, parts, places, waits):
    length, channels = spectrum.shape[1:]
    block = table_block(length)
    steps = length // block
    table_spec = pl.BlockSpec((block, length), lambda p, s, _: (s, 0))
    return pl.pallas_call(
        waiting(functools.partial(convolve_kernel, len(parts)), len(waits)),
        grid_spec=pltpu.PrefetchScalarGridSpec(
            num_scalar_prefetch=1,
            grid=(2, steps),
            in_specs=[
                *[ANYWHERE] * len(waits),
                table_spec,
                table_spec,
                pl.BlockSpec((2, block, channels), lambda p, s, _: (0, s + p * (steps - 1 - s), 0)),
            ]
            + [pl.BlockSpec(part.shape, lambda p, s, _: (0, 0)) for part in parts],
            out_specs=pl.BlockSpec((block, channels), lambda p, s, _: (p * s, 0)),
            scratch_shapes=[pltpu.VMEM((length, channels), SHORT), pltpu.VMEM((2, length, channels), SHORT)],
        ),
        out_shape=jax.ShapeDtypeStruct((length, channels), SHORT),
        compiler_params=kernel_params(2),
        cost_estimate=NO_COST,
    )(places, *waits, table[0], table[1], spectrum, *parts)


def prepare_kernel(index_ref, filters_ref, gate_ref, cotangent_ref, out_ref):
    out_ref[0, 0] = filters_ref[...].astype(SHORT)
    out_ref[0, 1] = (cotangent_ref[...].astype(WIDE) * gate_ref[...].astype(WIDE)).astype(SHORT)


def prepare(filters, gate, cotangent, groups, waits):
    rows, width = filters.shape
    channels = width // groups
    if channels % 128:
        both = jnp.stack([filters, cotangent.astype(WIDE) * gate.astype(WIDE)]).astype(SHORT)
        return both.reshape(2, rows, groups, channels).transpose(2, 0, 1, 3)
    spec = pl.BlockSpec((rows, channels), lambda g: (0, g))
    return pl.pallas_call(
        waiting(prepare_kernel, len(waits)),
        grid=(groups,),
        in_specs=[pl.BlockSpec(memory_space=pltpu.SMEM)] + [ANYWHERE] * len(waits) + [spec] * 3,
        out_specs=pl.BlockSpec((1, 2, rows, channels), lambda g: (g, 0, 0, 0)),
        out_shape=jax.ShapeDtypeStruct((groups, 2, rows, channels), SHORT),
        compiler_params=kernel_params(1),
        cost_estimate=NO_COST,
    )(jnp.zeros((1,), jnp.int32), *waits, filters, gate, cotangent)


def finish_kernel(convolved_ref, gate_ref, cotangent_ref, output_ref, grad_ref):
    convolved = convolved_ref[0].astype(WIDE)
    output_ref[...] = (gate_ref[...].astype(WIDE) * convolved).astype(SHORT)
    grad_ref[...] = (cotangent_ref[...].astype(WIDE) * convolved).astype(SHORT)


def finish(convolved, gate, cotangent):
    groups, rows, channels = convolved.shape
    width = groups * channels
    if channels % 128:
        wide = convolved.swapaxes(0, 1).reshape(rows, width).astype(WIDE)
        return [(other.astype(WIDE) * wide).astype(SHORT) for other in (gate, cotangent)]
    spec = pl.BlockSpec((rows, channels), lambda g: (0, g))
    return pl.pallas_call(
        finish_kernel,
        grid=(groups,),
        in_specs=[pl.BlockSpec((1, rows, channels), lambda g: (g, 0, 0)), spec, spec],
        out_specs=[spec, spec],
        out_shape=[jax.ShapeDtypeStruct((rows, width), SHORT)] * 2,
        compiler_params=kernel_params(1),
        cost_estimate=NO_COST,
    )(convolved, gate, cotangent)


def arrange_kernel(dims, index_ref, *refs):
    outer, inner, far, near, halves, half_rows = dims
    part_refs, out_ref = refs[:inner], refs[-1]
    channels = part_refs[0].shape[-1]
    tp = far * near
    for s in range(inner):
        lanes = aligned(index_ref[s], channels)
        for ahead in range(tp):
            source = index_ref[inner + ahead]
            for o in range(outer):
                for h in range(halves):
                    place = (ahead * outer + o) * half_rows
                    piece = part_refs[s][o, aligned(source * halves + h, half_rows)]
                    out_ref[h, place : place + half_rows, lanes] = piece


def arrange(parts, inner_places, sources, dims, waits):
    outer, inner, far, near, halves, half_rows = dims
    channels = parts[0].shape[-1]
    tp = far * near
    shape = (tp * outer * half_rows, inner * channels)
    if channels % 128:
        slots = jnp.zeros((inner, *parts[0].shape), SHORT)
        for s in range(inner):
            slots = lax.dynamic_update_index_in_dim(slots, parts[s], inner_places[s], 0)
        slots = slots.reshape(inner, outer, tp, halves, half_rows, channels).transpose(2, 3, 1, 4, 0, 5)
        slots = jnp.stack([pick(slots, sources[a]) for a in range(tp)])
        return jnp.stack([slots[:, h].reshape(shape) for h in range(halves)])
    index = jnp.concatenate([inner_places, sources]).astype(jnp.int32)
    size = math.prod(shape) * 2
    return pl.pallas_call(
        waiting(functools.partial(arrange_kernel, dims), len(waits)),
        in_specs=[pl.BlockSpec(memory_space=pltpu.SMEM)]
        + [ANYWHERE] * len(waits)
        + [pl.BlockSpec(memory_space=pltpu.VMEM)] * inner,
        out_specs=pl.BlockSpec(memory_space=pltpu.VMEM),
        out_shape=jax.ShapeDtypeStruct((halves, *shape), SHORT),
        compiler_params=kernel_params(0),
        cost_estimate=NO_COST,
    )(index, *waits, *parts)


def assemble_kernel(dims, index_ref, *refs):
    halves, steps, blocks, half_rows, depth = dims
    out_ref = refs[-1]
    for h in range(halves):
        for s in range(steps):
            rows = aligned(index_ref[s] * halves + h, half_rows)
            for b in range(blocks):
                out_ref[rows, aligned(index_ref[steps + b], depth)] = refs[h * steps + s][b]


def assemble(pieces, row_places, block_places, columns):
    halves, steps = len(pieces), len(pieces[0])
    blocks, half_rows, depth = pieces[0][0].shape
    flat = [piece for half in pieces for piece in half]
    rows = halves * steps * half_rows
    return pl.pallas_call(
        functools.partial(assemble_kernel, (halves, steps, blocks, half_rows, depth)),
        in_specs=[pl.BlockSpec(memory_space=pltpu.SMEM)] + [pl.BlockSpec(memory_space=pltpu.VMEM)] * len(flat),
        out_specs=pl.BlockSpec(memory_space=pltpu.VMEM),
        out_shape=jax.ShapeDtypeStruct((rows, columns), SHORT),
        compiler_params=kernel_params(0),
        cost_estimate=NO_COST,
    )(jnp.concatenate([row_places, block_places]).astype(jnp.int32), *flat)


def chunk_kernel(index_ref, in_ref, out_ref):
    out_ref[...] = in_ref[...]


def chunks_of(array, indices, count, waits=()):
    rows, width = array.shape
    chunk = width // count
    block = min(rows, 1024)
    if chunk % 128:
        return jnp.concatenate([lax.dynamic_slice_in_dim(array, i * chunk, chunk, 1) for i in indices], axis=1)
    return pl.pallas_call(
        waiting(chunk_kernel, len(waits)),
        grid_spec=pltpu.PrefetchScalarGridSpec(
            num_scalar_prefetch=1,
            grid=(rows // block, len(indices)),
            in_specs=[ANYWHERE] * len(waits) + [pl.BlockSpec((block, chunk), lambda r, c, index: (r, index[c]))],
            out_specs=pl.BlockSpec((block, chunk), lambda r, c, _: (r, c)),
        ),
        out_shape=jax.ShapeDtypeStruct((rows, len(indices) * chunk), array.dtype),
        compiler_params=kernel_params(2),
        cost_estimate=NO_COST,
    )(jnp.stack(indices).astype(jnp.int32), *waits, array)


def join_kernel(index_ref, *refs):
    size = refs[0].shape[0]
    for p, ref in enumerate(refs[:-1]):
        refs[-1][p * size : (p + 1) * size] = ref[...]


def join(parts, waits):
    size, width = parts[0].shape
    rows = len(parts) * size
    if size % 16:
        return jnp.concatenate(parts, axis=0)
    return pl.pallas_call(
        waiting(join_kernel, len(waits)),
        in_specs=[pl.BlockSpec(memory_space=pltpu.SMEM)]
        + [ANYWHERE] * len(waits)
        + [pl.BlockSpec(memory_space=pltpu.VMEM)] * len(parts),
        out_specs=pl.BlockSpec(memory_space=pltpu.VMEM),
        out_shape=jax.ShapeDtypeStruct((rows, width), parts[0].dtype),
        compiler_params=kernel_params(0),
        cost_estimate=NO_COST,
    )(jnp.zeros((1,), jnp.int32), *waits, *parts)


def product_kernel(dims, index_ref, *refs):
    inner, outer, pieces, depth, add = dims
    token_refs, weight_refs, (out_ref, joined_ref) = refs[:pieces], refs[pieces : pieces + inner], refs[-2:]
    size = token_refs[0].shape[0] // outer

    @pl.when(pl.program_id(0) == 0)
    def _():
        for p in range(pieces):
            for o in range(outer):
                rows = aligned(index_ref[2 + inner + o], size)
                place = (p * outer + o) * size
                joined_ref[place : place + size] = token_refs[p][rows]

    total = refs[-3][...].astype(WIDE) if add else 0.0
    for i in range(inner):
        columns = aligned(index_ref[2 + i], depth)
        total = total + wide_dot(joined_ref[:, columns], weight_refs[i][...])
    out_ref[...] = total.astype(SHORT).reshape(out_ref.shape)


def product(pieces, in_weight, chunk_index, received, inner_blocks, row_order, running, last, waits):
    inner = len(received) + 1
    outer = row_order.shape[0]
    depth, width = in_weight.shape
    chunk = width // outer
    channels = chunk // inner
    size, whole_depth = pieces[0].shape
    rows = len(pieces) * size
    at_inner = inner_blocks[0]
    if channels % 128:
        tokens = jnp.stack(pieces).reshape(len(pieces), outer, size // outer, whole_depth)
        tokens = jnp.concatenate([pick(tokens, row_order[s], 1)[:, None] for s in range(outer)], axis=1)
        tokens = tokens.reshape(rows, whole_depth)
        weights = [chunks_of(in_weight, [chunk_index], outer)]
        weights += [held[:, at * chunk : (at + 1) * chunk] for held, at in received]
        total = sum(
            wide_dot(lax.dynamic_slice_in_dim(tokens, inner_blocks[i] * depth, depth, 1), weights[i])
            for i in range(inner)
        )
        if running is not None:
            total = total + running.astype(WIDE)
        total = total.astype(SHORT)
        if last:
            total = total.reshape(rows, inner, channels)
            total = jnp.stack([pick(total, (at_inner + i) % inner, 1) for i in range(inner)])
        return total
    if last:
        out_spec = pl.BlockSpec((1, rows, channels), lambda g, index: ((g + inner - index[2]) % inner, 0, 0))
        out_shape = (inner, rows, channels)
    else:
        out_spec = pl.BlockSpec((rows, channels), lambda g, _: (0, g))
        out_shape = (rows, chunk)
    index = jnp.concatenate([chunk_index[None], at_inner[None], inner_blocks, row_order]).astype(jnp.int32)
    return pl.pallas_call(
        waiting(
            functools.partial(product_kernel, (inner, outer, len(pieces), depth, running is not None)), len(waits)
        ),
        grid_spec=pltpu.PrefetchScalarGridSpec(
            num_scalar_prefetch=1,
            grid=(inner,),
            in_specs=[ANYWHERE] * len(waits)
            + [pl.BlockSpec((size, whole_depth), lambda g, _: (0, 0)) for _ in pieces]
            + [pl.BlockSpec((depth, channels), lambda g, index: (0, index[0] * inner + g))]
            + [
                pl.BlockSpec((depth, channels), lambda g, _, at=at: (0, at * inner + g)) for _, at in received
            ]
            + ([] if running is None else [pl.BlockSpec((rows, channels), lambda g, _: (0, g))]),
            out_specs=out_spec,
            scratch_shapes=[pltpu.VMEM((rows, whole_depth), SHORT)],
        ),
        out_shape=jax.ShapeDtypeStruct(out_shape, SHORT),
        compiler_params=kernel_params(1),
        cost_estimate=NO_COST,
    )(index, *waits, *pieces, in_weight, *[held for held, _ in received], *([] if running is None else [running]))


def shares_kernel(dims, index_ref, grad_ref, *refs):
    outer, inner, near, chunk = dims
    own_ref, received_refs = refs[0], refs[1 : 1 + (inner - 1) * outer]
    out_refs, plain_ref = refs[1 + (inner - 1) * outer : -1], refs[-1]
    size = out_refs[0].shape[1]

    @pl.when(pl.program_id(0) == 0)
    def _():
        for o in range(outer):
            plain_ref[:, o * chunk : (o + 1) * chunk] = grad_ref[o, 0]

    for i in range(inner):
        if i == 0:
            total = wide_dot_turned(plain_ref[...], own_ref[...])
        else:
            total = sum(
                wide_dot_turned(grad_ref[index_ref[s], 0], received_refs[(i - 1) * outer + s][...]) for s in range(outer)
            )
        total = total.astype(SHORT)
        for n in range(near):
            out_refs[n][i] = total[n * size : (n + 1) * size]


def shares(grad_values, half, in_weight, received, chunks, near, waits):
    outer, _, rows, chunk = grad_values.shape
    inner = len(received) + 1
    depth, width = in_weight.shape
    if chunk // inner % 128:
        grad_values = grad_values[:, half]
        plain = grad_values.swapaxes(0, 1).reshape(rows, width)
        totals = [wide_dot_turned(plain, in_weight)] + [
            sum(
                wide_dot_turned(pick(grad_values, chunks[s]), held[s][0][:, held[s][1] * chunk : (held[s][1] + 1) * chunk])
                for s in range(outer)
            )
            for held in received
        ]
        total = jnp.stack(totals).astype(SHORT).reshape(inner, near, rows // near, depth)
        return [total[:, n] for n in range(near)]
    block = min(depth, 256)
    flat = [w for held in received for w in held]
    out_spec = pl.BlockSpec((inner, rows // near, block), lambda k, _: (0, 0, k))
    return pl.pallas_call(
        waiting(functools.partial(shares_kernel, (outer, inner, near, chunk)), len(waits)),
        grid_spec=pltpu.PrefetchScalarGridSpec(
            num_scalar_prefetch=1,
            grid=(depth // block,),
            in_specs=[ANYWHERE] * len(waits)
            + [pl.BlockSpec((outer, 1, rows, chunk), lambda k, _: (0, half, 0, 0))]
            + [pl.BlockSpec((block, width), lambda k, _: (k, 0))]
            + [pl.BlockSpec((block, chunk), lambda k, _, at=at: (k, at)) for _, at in flat],
            out_specs=[out_spec] * near,
            scratch_shapes=[pltpu.VMEM((rows, width), SHORT)],
        ),
        out_shape=[jax.ShapeDtypeStruct((inner, rows // near, depth), SHORT)] * near,
        compiler_params=kernel_params(1),
        cost_estimate=NO_COST,
    )(chunks.astype(jnp.int32), *waits, grad_values, in_weight, *[held for held, _ in flat])


def shifted(array, axis, shift):
    size = lax.axis_size(axis)
    return lax.ppermute(array, axis, [(at, (at + shift) % size) for at in range(size)])


def pick(array, index, axis=0):
    return lax.dynamic_index_in_dim(array, index, axis, keepdims=False)


def turned(parts, start):
    count = len(parts)
    backwards = jnp.stack(parts[::-1])
    doubled = jnp.concatenate([backwards, backwards], axis=0)
    return lax.dynamic_slice_in_dim(doubled, (count - 1 - start) % count, count, 0)


def per_device(tokens, in_weight, filters, gate, cotangent):
    outer, inner, far, near = (lax.axis_size(a) for a in ("outer", "inner", "far", "near"))
    at_outer, at_inner, at_far, at_near = (lax.axis_index(a) for a in ("outer", "inner", "far", "near"))
    tp = far * near
    at_tp = at_far * near + at_near
    rows, columns = tokens.shape
    fine_rows = rows // tp
    halves = 2 if fine_rows >= 32 else 1
    half_rows = fine_rows // halves
    ctx = ("outer", "inner")
    ctx_size = outer * inner
    cell = ("outer", "far", "near")
    split = tp // outer
    depth, width = in_weight.shape
    channels = width // ctx_size
    tile_blocks = columns // depth
    length = ctx_size * rows
    back_inner = [(at_inner - i) % inner for i in range(inner)]

    def destination(source_outer, source_tp, step):
        part = (source_outer * split + source_tp % split + step) % tp
        return (source_tp // split) * tp + part

    chunks = [(at_outer - s) % outer for s in range(outer)]
    order = [s % outer for s in range(1, outer + 1)]
    received = [[None] * outer for _ in range(1, inner)]
    arrivals = []

    def send_chunks(some, waits):
        sent = chunks_of(in_weight, [chunks[s] for s in some], outer, waits)
        arrivals.append([shifted(sent, "inner", i) for i in range(1, inner)])
        for i in range(1, inner):
            for at, s in enumerate(some):
                received[i - 1][s] = (arrivals[-1][i - 1], at)
        return sent

    moved = []
    if split == 1:
        by_far = tokens.reshape(far, near * fine_rows, columns)
        by_far = [pick(by_far, (at_far + f) % far) for f in range(far)]
        sent = send_chunks(order[:2], by_far[1:])
        prepared = prepare(filters, gate, cotangent, ctx_size, [sent])
        held = [by_far[0]] + [shifted(by_far[f], "far", f) for f in range(1, far)]
        held = jnp.stack(held).reshape(far, near, fine_rows, columns)
        for step in range(tp):
            pairs = []
            for o in range(outer):
                for g in range(far):
                    for c in range(near):
                        tile, part = (o + step) % tp // near, (o + step) % tp % near
                        pairs.append(((o * far + g) * near + c, ((tile * near + c) * far + g) * near + part))
            number = (at_outer + step) % tp
            part = lax.dynamic_slice(
                held, ((at_far - number // near) % far, number % near, 0, 0), (1, 1, fine_rows, columns)
            )
            moved.append(lax.ppermute(part.reshape(fine_rows, columns), cell, pairs))
        token_part = join(moved, [prepared, *arrivals[0]])
    else:
        sent = send_chunks(order[:2], [])
        prepared = prepare(filters, gate, cotangent, ctx_size, [sent])
        row_parts = tokens.reshape(tp, fine_rows, columns)
        for step in range(tp):
            pairs = [(o * tp + t, destination(o, t, step)) for o in range(outer) for t in range(tp)]
            part = (at_outer * split + at_tp % split + step) % tp
            moved.append(lax.ppermute(pick(row_parts, part), cell, pairs))
        token_part = turned(moved, at_tp).reshape(outer, split, fine_rows, columns).swapaxes(1, 2)
        token_part = token_part.reshape(outer * fine_rows, split * columns)

    channel_rows = lax.all_to_all(release(prepared, [token_part]), ctx, split_axis=0, concat_axis=0, tiled=True)
    sent = send_chunks(order[2:], [token_part, *arrivals[0]])
    table = transform_table(length)

    pieces = [token_part] + [shifted(token_part, "far", f) for f in range(1, far)]
    pieces = pieces + [shifted(piece, "near", n) for n in range(1, near) for piece in pieces]
    places = []
    for n in range(near):
        for f in range(far):
            source_near = (at_near - n) % near
            source = (at_far - f) % far * near + source_near
            for s in range(outer):
                source_outer = (source_near - s) % outer if split == 1 else s
                places.append(source_outer * (inner * tp) + source)
    places = jnp.stack(places).astype(jnp.int32)
    places = jnp.stack([places + back_inner[s] * tp for s in range(inner)])

    blocks = jnp.stack(back_inner)
    turn = at_outer // near * near if split == 1 else 0
    row_order = jnp.stack([(s + turn) % outer + at_outer * 0 for s in range(outer)])
    running = None
    waits = [sent]
    for s in order:
        if running is not None:
            running = shifted(running, "outer", 1)
        held = [chunk[s] for chunk in received]
        running = product(pieces, in_weight, chunks[s], held, blocks, row_order, running, s == 0, waits)
        waits = []
        if s == outer - 2:
            grad_values, spectrum = correlate(table, rotation(length), channel_rows, [running])
            by_inner = grad_values.reshape(outer, inner, rows, channels)
            grad_parts = [pick(by_inner, at_inner, 1)]
            for i in range(1, inner):
                grad_parts.append(shifted(pick(by_inner, (at_inner + i) % inner, 1), "inner", i))
            waits = [spectrum]
        if s == outer - 1:
            sources = [(at_far + f) % far * near + (at_near + n) % near for n in range(near) for f in range(far)]
            arranged = arrange(
                grad_parts, jnp.stack(back_inner), jnp.stack(sources), (outer, inner, far, near, halves, half_rows), [running]
            )
            gathered = lax.all_gather(arranged, "outer", axis=0, tiled=False)
            waits = [arranged]
    value_parts = [running[0]] + [shifted(running[i], "inner", i) for i in range(1, inner)]

    convolved = convolve(table, spectrum, value_parts, places, []).reshape(ctx_size, rows, channels)
    exchanged = lax.all_to_all(convolved, ctx, split_axis=0, concat_axis=0, tiled=True)

    sent_back = []
    waits = [convolved]
    for half in range(halves):
        by_near = shares(gathered, half, in_weight, received, jnp.stack(chunks), near, waits)
        waits = [by_near[0]]
        total = by_near[0].astype(WIDE) + sum(shifted(by_near[n], "near", n).astype(WIDE) for n in range(1, near))
        total = total.astype(SHORT).reshape(inner, far, outer * half_rows, depth)
        others = [shifted(total[:, f], "far", f) for f in range(1, far)]
        total = total[:, 0].astype(WIDE) + sum(other.astype(WIDE) for other in others)
        total = total.astype(SHORT).reshape(inner, outer, half_rows, depth)
        if split == 1:
            total = total.swapaxes(0, 1)
        else:
            total = turned(list(total), at_inner).reshape(split, tile_blocks, outer, half_rows, depth)
            total = total.transpose(2, 0, 1, 3, 4).reshape(tp, tile_blocks, half_rows, depth)
        back = []
        for step in range(tp):
            pairs = [(destination(o, t, step), o * tp + t) for o in range(outer) for t in range(tp)]
            back.append(lax.ppermute(pick(total, (at_tp - step) % tp), cell, pairs))
        sent_back.append(back)
    row_places = [(at_outer * split + at_tp % split + step) % tp for step in range(tp)]
    block_places = back_inner if split == 1 else [jnp.int32(b) for b in range(tile_blocks)]
    grad_tokens = assemble(sent_back, jnp.stack(row_places), jnp.stack(block_places), columns)

    gated_output, grad_gate = finish(exchanged, gate, cotangent)
    return (gated_output, grad_gate, grad_tokens)


def solution(mesh):
    ctx_size, tp_size = mesh.shape["ctx"], mesh.shape["tp"]
    inner, near = 1, 2
    while inner * inner * 4 <= ctx_size:
        inner *= 2
    fine_mesh = Mesh(
        np.asarray(mesh.devices).reshape(ctx_size // inner, inner, tp_size // near, near),
        ("outer", "inner", "far", "near"),
    )
    placed = P(("outer", "inner"), ("far", "near"))
    return jax.shard_map(
        per_device,
        mesh=fine_mesh,
        in_specs=(placed,) * 5,
        out_specs=(placed,) * 3,
        check_vma=False,
    )
```

```python
import functools
import math

import jax
import jax.numpy as jnp
import numpy as np
from jax import lax
from jax.experimental import pallas as pl
from jax.experimental.pallas import tpu as pltpu
from jax.sharding import Mesh, PartitionSpec as P

TWO_PI = 2.0 * math.pi
WIDE = jnp.float32
SHORT = jnp.bfloat16
LAST_TWO = (((1,), (1,)), ((), ()))


def transform_table(length):
    period = 16 * length
    if length > 2048:
        points = 4 * jnp.arange(length, dtype=jnp.int32) + 1
        angles = (points[:, None] * points[None, :] % period).astype(WIDE) * (TWO_PI / period)
        return [jnp.cos(angles).astype(SHORT), jnp.sin(angles).astype(SHORT)]
    points = 4 * np.arange(length, dtype=np.int64) + 1
    turns = points[:, None] * points[None, :] % period
    angles = np.arange(period) * (TWO_PI / period)
    return [jnp.asarray(wave(angles).astype(SHORT)[turns]) for wave in (np.cos, np.sin)]


def table_block(length):
    return min(512, length // 2)


def rotation(length):
    angle = (4 * jnp.arange(length, dtype=jnp.int32) + 1).astype(WIDE) * (TWO_PI / (16 * length))
    return jnp.stack([jnp.cos(angle), jnp.sin(angle)], axis=1)


def wide_dot(left, right):
    return jnp.dot(left, right, preferred_element_type=WIDE)


def wide_dot_turned(left, right):
    return lax.dot_general(left, right, LAST_TWO, preferred_element_type=WIDE)


def kernel_params(axes):
    return pltpu.CompilerParams(
        dimension_semantics=("arbitrary",) * axes, vmem_limit_bytes=48 * 1024 * 1024
    )


NO_COST = pl.CostEstimate(flops=0, bytes_accessed=0, transcendentals=0)


ANYWHERE = pl.BlockSpec(memory_space=pl.ANY)


def waiting(kernel, count):
    return lambda index_ref, *refs: kernel(index_ref, *refs[count:])


def release_kernel(index_ref, in_ref, out_ref):
    pass


def release(array, waits):
    return pl.pallas_call(
        waiting(release_kernel, len(waits)),
        in_specs=[pl.BlockSpec(memory_space=pltpu.SMEM)] + [ANYWHERE] * (len(waits) + 1),
        out_specs=ANYWHERE,
        out_shape=jax.ShapeDtypeStruct(array.shape, array.dtype),
        input_output_aliases={1 + len(waits): 0},
        compiler_params=kernel_params(0),
        cost_estimate=NO_COST,
    )(jnp.zeros((1,), jnp.int32), *waits, array)


def aligned(index, size):
    return pl.ds(pl.multiple_of(index * size, size), size)


def correlate_kernel(index_ref, cos_ref, sin_ref, turn_ref, both_ref, out_ref, spectrum_ref, signal_ref, mix_ref):
    phase, step = pl.program_id(0), pl.program_id(1)
    block = cos_ref.shape[0]
    length, channels = mix_ref.shape[1:]
    rows = aligned(step, block)

    @pl.when((phase == 0) & (step == 0))
    def _():
        for which in range(2):
            signal_ref[:, which * channels : (which + 1) * channels] = both_ref[:, which].reshape(length, channels)

    @pl.when(phase == 0)
    def _():
        turn_cos, turn_sin = turn_ref[:, 0:1], turn_ref[:, 1:2]
        cos_sums = wide_dot(cos_ref[...], signal_ref[...])
        sin_sums = wide_dot(sin_ref[...], signal_ref[...])
        raw_cos, signal_cos = cos_sums[:, :channels], cos_sums[:, channels:]
        raw_sin, signal_sin = sin_sums[:, :channels], sin_sums[:, channels:]
        filter_cos = raw_cos * turn_cos + raw_sin * turn_sin
        filter_sin = raw_sin * turn_cos - raw_cos * turn_sin
        spectrum_ref[0] = filter_cos.astype(SHORT)
        spectrum_ref[1] = filter_sin.astype(SHORT)
        mix_ref[0, rows] = (signal_cos * filter_cos + signal_sin * filter_sin).astype(SHORT)
        mix_ref[1, rows] = (signal_sin * filter_cos - signal_cos * filter_sin).astype(SHORT)

    @pl.when(phase == 1)
    def _():
        total = wide_dot(cos_ref[...], mix_ref[0]) + wide_dot(sin_ref[...], mix_ref[1])
        out_ref[...] = (total * (1.0 / length)).astype(out_ref.dtype)


def correlate(table, turn, both, waits):
    parts, _, rows, channels = both.shape
    length = parts * rows
    block = table_block(length)
    steps = length // block
    table_spec = pl.BlockSpec((block, length), lambda p, s: (s, 0))
    return pl.pallas_call(
        waiting(correlate_kernel, len(waits)),
        grid=(2, steps),
        in_specs=[
            pl.BlockSpec(memory_space=pltpu.SMEM),
            *[ANYWHERE] * len(waits),
            table_spec,
            table_spec,
            pl.BlockSpec((block, 2), lambda p, s: (s, 0)),
            pl.BlockSpec((parts, 2, rows, channels), lambda p, s: (0, 0, 0, 0)),
        ],
        out_specs=[
            pl.BlockSpec((block, channels), lambda p, s: (p * s, 0)),
            pl.BlockSpec((2, block, channels), lambda p, s: (0, s + p * (steps - 1 - s), 0)),
        ],
        out_shape=[
            jax.ShapeDtypeStruct((length, channels), SHORT),
            jax.ShapeDtypeStruct((2, length, channels), SHORT),
        ],
        scratch_shapes=[pltpu.VMEM((length, 2 * channels), SHORT), pltpu.VMEM((2, length, channels), SHORT)],
        compiler_params=kernel_params(2),
        cost_estimate=NO_COST,
    )(jnp.zeros((1,), jnp.int32), *waits, table[0], table[1], turn, both)


def convolve_kernel(inner, places_ref, cos_ref, sin_ref, spectrum_ref, *refs):
    part_refs, (out_ref, signal_ref, mix_ref) = refs[:inner], refs[inner:]
    phase, step = pl.program_id(0), pl.program_id(1)
    block = cos_ref.shape[0]
    length = signal_ref.shape[0]
    rows = aligned(step, block)
    pieces = places_ref.shape[1]
    size = part_refs[0].shape[0] // pieces

    @pl.when((phase == 0) & (step == 0))
    def _():
        for s in range(inner):
            for p in range(pieces):
                signal_ref[aligned(places_ref[s, p], size)] = part_refs[s][p * size : (p + 1) * size]

    @pl.when(phase == 0)
    def _():
        filter_cos, filter_sin = spectrum_ref[0].astype(WIDE), spectrum_ref[1].astype(WIDE)
        signal_cos = wide_dot(cos_ref[...], signal_ref[...])
        signal_sin = wide_dot(sin_ref[...], signal_ref[...])
        mix_ref[0, rows] = (signal_cos * filter_cos - signal_sin * filter_sin).astype(SHORT)
        mix_ref[1, rows] = (signal_cos * filter_sin + signal_sin * filter_cos).astype(SHORT)

    @pl.when(phase == 1)
    def _():
        total = wide_dot(cos_ref[...], mix_ref[0]) + wide_dot(sin_ref[...], mix_ref[1])
        out_ref[...] = (total * (1.0 / length)).astype(out_ref.dtype)


def convolve(table, spectrum, parts, places, waits):
    length, channels = spectrum.shape[1:]
    block = table_block(length)
    steps = length // block
    table_spec = pl.BlockSpec((block, length), lambda p, s, _: (s, 0))
    return pl.pallas_call(
        waiting(functools.partial(convolve_kernel, len(parts)), len(waits)),
        grid_spec=pltpu.PrefetchScalarGridSpec(
            num_scalar_prefetch=1,
            grid=(2, steps),
            in_specs=[
                *[ANYWHERE] * len(waits),
                table_spec,
                table_spec,
                pl.BlockSpec((2, block, channels), lambda p, s, _: (0, s + p * (steps - 1 - s), 0)),
            ]
            + [pl.BlockSpec(part.shape, lambda p, s, _: (0, 0)) for part in parts],
            out_specs=pl.BlockSpec((block, channels), lambda p, s, _: (p * s, 0)),
            scratch_shapes=[pltpu.VMEM((length, channels), SHORT), pltpu.VMEM((2, length, channels), SHORT)],
        ),
        out_shape=jax.ShapeDtypeStruct((length, channels), SHORT),
        compiler_params=kernel_params(2),
        cost_estimate=NO_COST,
    )(places, *waits, table[0], table[1], spectrum, *parts)


def prepare_kernel(index_ref, filters_ref, gate_ref, cotangent_ref, out_ref):
    out_ref[0, 0] = filters_ref[...].astype(SHORT)
    out_ref[0, 1] = (cotangent_ref[...].astype(WIDE) * gate_ref[...].astype(WIDE)).astype(SHORT)


def prepare(filters, gate, cotangent, groups, waits):
    rows, width = filters.shape
    channels = width // groups
    if channels % 128:
        both = jnp.stack([filters, cotangent.astype(WIDE) * gate.astype(WIDE)]).astype(SHORT)
        return both.reshape(2, rows, groups, channels).transpose(2, 0, 1, 3)
    spec = pl.BlockSpec((rows, channels), lambda g: (0, g))
    return pl.pallas_call(
        waiting(prepare_kernel, len(waits)),
        grid=(groups,),
        in_specs=[pl.BlockSpec(memory_space=pltpu.SMEM)] + [ANYWHERE] * len(waits) + [spec] * 3,
        out_specs=pl.BlockSpec((1, 2, rows, channels), lambda g: (g, 0, 0, 0)),
        out_shape=jax.ShapeDtypeStruct((groups, 2, rows, channels), SHORT),
        compiler_params=kernel_params(1),
        cost_estimate=NO_COST,
    )(jnp.zeros((1,), jnp.int32), *waits, filters, gate, cotangent)


def finish_kernel(convolved_ref, gate_ref, cotangent_ref, output_ref, grad_ref):
    convolved = convolved_ref[0].astype(WIDE)
    output_ref[...] = (gate_ref[...].astype(WIDE) * convolved).astype(SHORT)
    grad_ref[...] = (cotangent_ref[...].astype(WIDE) * convolved).astype(SHORT)


def finish(convolved, gate, cotangent):
    groups, rows, channels = convolved.shape
    width = groups * channels
    if channels % 128:
        wide = convolved.swapaxes(0, 1).reshape(rows, width).astype(WIDE)
        return [(other.astype(WIDE) * wide).astype(SHORT) for other in (gate, cotangent)]
    spec = pl.BlockSpec((rows, channels), lambda g: (0, g))
    return pl.pallas_call(
        finish_kernel,
        grid=(groups,),
        in_specs=[pl.BlockSpec((1, rows, channels), lambda g: (g, 0, 0)), spec, spec],
        out_specs=[spec, spec],
        out_shape=[jax.ShapeDtypeStruct((rows, width), SHORT)] * 2,
        compiler_params=kernel_params(1),
        cost_estimate=NO_COST,
    )(convolved, gate, cotangent)


def arrange_kernel(dims, index_ref, *refs):
    outer, inner, far, near, halves, half_rows = dims
    part_refs, out_ref = refs[:inner], refs[-1]
    channels = part_refs[0].shape[-1]
    tp = far * near
    for s in range(inner):
        lanes = aligned(index_ref[s], channels)
        for ahead in range(tp):
            source = index_ref[inner + ahead]
            for o in range(outer):
                for h in range(halves):
                    place = (ahead * outer + o) * half_rows
                    piece = part_refs[s][o, aligned(source * halves + h, half_rows)]
                    out_ref[h, place : place + half_rows, lanes] = piece


def arrange(parts, inner_places, sources, dims, waits):
    outer, inner, far, near, halves, half_rows = dims
    channels = parts[0].shape[-1]
    tp = far * near
    shape = (tp * outer * half_rows, inner * channels)
    if channels % 128:
        slots = jnp.zeros((inner, *parts[0].shape), SHORT)
        for s in range(inner):
            slots = lax.dynamic_update_index_in_dim(slots, parts[s], inner_places[s], 0)
        slots = slots.reshape(inner, outer, tp, halves, half_rows, channels).transpose(2, 3, 1, 4, 0, 5)
        slots = jnp.stack([pick(slots, sources[a]) for a in range(tp)])
        return jnp.stack([slots[:, h].reshape(shape) for h in range(halves)])
    index = jnp.concatenate([inner_places, sources]).astype(jnp.int32)
    size = math.prod(shape) * 2
    return pl.pallas_call(
        waiting(functools.partial(arrange_kernel, dims), len(waits)),
        in_specs=[pl.BlockSpec(memory_space=pltpu.SMEM)]
        + [ANYWHERE] * len(waits)
        + [pl.BlockSpec(memory_space=pltpu.VMEM)] * inner,
        out_specs=pl.BlockSpec(memory_space=pltpu.VMEM),
        out_shape=jax.ShapeDtypeStruct((halves, *shape), SHORT),
        compiler_params=kernel_params(0),
        cost_estimate=NO_COST,
    )(index, *waits, *parts)


def assemble_kernel(dims, index_ref, *refs):
    halves, steps, blocks, half_rows, depth = dims
    out_ref = refs[-1]
    for h in range(halves):
        for s in range(steps):
            rows = aligned(index_ref[s] * halves + h, half_rows)
            for b in range(blocks):
                out_ref[rows, aligned(index_ref[steps + b], depth)] = refs[h * steps + s][b]


def assemble(pieces, row_places, block_places, columns):
    halves, steps = len(pieces), len(pieces[0])
    blocks, half_rows, depth = pieces[0][0].shape
    flat = [piece for half in pieces for piece in half]
    rows = halves * steps * half_rows
    return pl.pallas_call(
        functools.partial(assemble_kernel, (halves, steps, blocks, half_rows, depth)),
        in_specs=[pl.BlockSpec(memory_space=pltpu.SMEM)] + [pl.BlockSpec(memory_space=pltpu.VMEM)] * len(flat),
        out_specs=pl.BlockSpec(memory_space=pltpu.VMEM),
        out_shape=jax.ShapeDtypeStruct((rows, columns), SHORT),
        compiler_params=kernel_params(0),
        cost_estimate=NO_COST,
    )(jnp.concatenate([row_places, block_places]).astype(jnp.int32), *flat)


def chunk_kernel(index_ref, in_ref, out_ref):
    out_ref[...] = in_ref[...]


def chunks_of(array, indices, count, waits=()):
    rows, width = array.shape
    chunk = width // count
    block = min(rows, 1024)
    if chunk % 128:
        return jnp.concatenate([lax.dynamic_slice_in_dim(array, i * chunk, chunk, 1) for i in indices], axis=1)
    return pl.pallas_call(
        waiting(chunk_kernel, len(waits)),
        grid_spec=pltpu.PrefetchScalarGridSpec(
            num_scalar_prefetch=1,
            grid=(rows // block, len(indices)),
            in_specs=[ANYWHERE] * len(waits) + [pl.BlockSpec((block, chunk), lambda r, c, index: (r, index[c]))],
            out_specs=pl.BlockSpec((block, chunk), lambda r, c, _: (r, c)),
        ),
        out_shape=jax.ShapeDtypeStruct((rows, len(indices) * chunk), array.dtype),
        compiler_params=kernel_params(2),
        cost_estimate=NO_COST,
    )(jnp.stack(indices).astype(jnp.int32), *waits, array)


def join_kernel(index_ref, *refs):
    size = refs[0].shape[0]
    for p, ref in enumerate(refs[:-1]):
        refs[-1][p * size : (p + 1) * size] = ref[...]


def join(parts, waits):
    size, width = parts[0].shape
    rows = len(parts) * size
    if size % 16:
        return jnp.concatenate(parts, axis=0)
    return pl.pallas_call(
        waiting(join_kernel, len(waits)),
        in_specs=[pl.BlockSpec(memory_space=pltpu.SMEM)]
        + [ANYWHERE] * len(waits)
        + [pl.BlockSpec(memory_space=pltpu.VMEM)] * len(parts),
        out_specs=pl.BlockSpec(memory_space=pltpu.VMEM),
        out_shape=jax.ShapeDtypeStruct((rows, width), parts[0].dtype),
        compiler_params=kernel_params(0),
        cost_estimate=NO_COST,
    )(jnp.zeros((1,), jnp.int32), *waits, *parts)


def product_kernel(dims, index_ref, *refs):
    inner, outer, pieces, depth, add = dims
    token_refs, weight_refs, (out_ref, joined_ref) = refs[:pieces], refs[pieces : pieces + inner], refs[-2:]
    size = token_refs[0].shape[0] // outer

    @pl.when(pl.program_id(0) == 0)
    def _():
        for p in range(pieces):
            for o in range(outer):
                rows = aligned(index_ref[2 + inner + o], size)
                place = (p * outer + o) * size
                joined_ref[place : place + size] = token_refs[p][rows]

    total = refs[-3][...].astype(WIDE) if add else 0.0
    for i in range(inner):
        columns = aligned(index_ref[2 + i], depth)
        total = total + wide_dot(joined_ref[:, columns], weight_refs[i][...])
    out_ref[...] = total.astype(SHORT).reshape(out_ref.shape)


def product(pieces, in_weight, chunk_index, received, inner_blocks, row_order, running, last, waits):
    inner = len(received) + 1
    outer = row_order.shape[0]
    depth, width = in_weight.shape
    chunk = width // outer
    channels = chunk // inner
    size, whole_depth = pieces[0].shape
    rows = len(pieces) * size
    at_inner = inner_blocks[0]
    if channels % 128:
        tokens = jnp.stack(pieces).reshape(len(pieces), outer, size // outer, whole_depth)
        tokens = jnp.concatenate([pick(tokens, row_order[s], 1)[:, None] for s in range(outer)], axis=1)
        tokens = tokens.reshape(rows, whole_depth)
        weights = [chunks_of(in_weight, [chunk_index], outer)]
        weights += [held[:, at * chunk : (at + 1) * chunk] for held, at in received]
        total = sum(
            wide_dot(lax.dynamic_slice_in_dim(tokens, inner_blocks[i] * depth, depth, 1), weights[i])
            for i in range(inner)
        )
        if running is not None:
            total = total + running.astype(WIDE)
        total = total.astype(SHORT)
        if last:
            total = total.reshape(rows, inner, channels)
            total = jnp.stack([pick(total, (at_inner + i) % inner, 1) for i in range(inner)])
        return total
    if last:
        out_spec = pl.BlockSpec((1, rows, channels), lambda g, index: ((g + inner - index[2]) % inner, 0, 0))
        out_shape = (inner, rows, channels)
    else:
        out_spec = pl.BlockSpec((rows, channels), lambda g, _: (0, g))
        out_shape = (rows, chunk)
    index = jnp.concatenate([chunk_index[None], at_inner[None], inner_blocks, row_order]).astype(jnp.int32)
    return pl.pallas_call(
        waiting(
            functools.partial(product_kernel, (inner, outer, len(pieces), depth, running is not None)), len(waits)
        ),
        grid_spec=pltpu.PrefetchScalarGridSpec(
            num_scalar_prefetch=1,
            grid=(inner,),
            in_specs=[ANYWHERE] * len(waits)
            + [pl.BlockSpec((size, whole_depth), lambda g, _: (0, 0)) for _ in pieces]
            + [pl.BlockSpec((depth, channels), lambda g, index: (0, index[0] * inner + g))]
            + [
                pl.BlockSpec((depth, channels), lambda g, _, at=at: (0, at * inner + g)) for _, at in received
            ]
            + ([] if running is None else [pl.BlockSpec((rows, channels), lambda g, _: (0, g))]),
            out_specs=out_spec,
            scratch_shapes=[pltpu.VMEM((rows, whole_depth), SHORT)],
        ),
        out_shape=jax.ShapeDtypeStruct(out_shape, SHORT),
        compiler_params=kernel_params(1),
        cost_estimate=NO_COST,
    )(index, *waits, *pieces, in_weight, *[held for held, _ in received], *([] if running is None else [running]))


def shares_kernel(dims, index_ref, grad_ref, *refs):
    outer, inner, near, chunk = dims
    own_ref, received_refs = refs[0], refs[1 : 1 + (inner - 1) * outer]
    out_refs, plain_ref = refs[1 + (inner - 1) * outer : -1], refs[-1]
    size = out_refs[0].shape[1]

    @pl.when(pl.program_id(0) == 0)
    def _():
        for o in range(outer):
            plain_ref[:, o * chunk : (o + 1) * chunk] = grad_ref[o, 0]

    for i in range(inner):
        if i == 0:
            total = wide_dot_turned(plain_ref[...], own_ref[...])
        else:
            total = sum(
                wide_dot_turned(grad_ref[index_ref[s], 0], received_refs[(i - 1) * outer + s][...]) for s in range(outer)
            )
        total = total.astype(SHORT)
        for n in range(near):
            out_refs[n][i] = total[n * size : (n + 1) * size]


def shares(grad_values, half, in_weight, received, chunks, near, waits):
    outer, _, rows, chunk = grad_values.shape
    inner = len(received) + 1
    depth, width = in_weight.shape
    if chunk // inner % 128:
        grad_values = grad_values[:, half]
        plain = grad_values.swapaxes(0, 1).reshape(rows, width)
        totals = [wide_dot_turned(plain, in_weight)] + [
            sum(
                wide_dot_turned(pick(grad_values, chunks[s]), held[s][0][:, held[s][1] * chunk : (held[s][1] + 1) * chunk])
                for s in range(outer)
            )
            for held in received
        ]
        total = jnp.stack(totals).astype(SHORT).reshape(inner, near, rows // near, depth)
        return [total[:, n] for n in range(near)]
    block = min(depth, 256)
    flat = [w for held in received for w in held]
    out_spec = pl.BlockSpec((inner, rows // near, block), lambda k, _: (0, 0, k))
    return pl.pallas_call(
        waiting(functools.partial(shares_kernel, (outer, inner, near, chunk)), len(waits)),
        grid_spec=pltpu.PrefetchScalarGridSpec(
            num_scalar_prefetch=1,
            grid=(depth // block,),
            in_specs=[ANYWHERE] * len(waits)
            + [pl.BlockSpec((outer, 1, rows, chunk), lambda k, _: (0, half, 0, 0))]
            + [pl.BlockSpec((block, width), lambda k, _: (k, 0))]
            + [pl.BlockSpec((block, chunk), lambda k, _, at=at: (k, at)) for _, at in flat],
            out_specs=[out_spec] * near,
            scratch_shapes=[pltpu.VMEM((rows, width), SHORT)],
        ),
        out_shape=[jax.ShapeDtypeStruct((inner, rows // near, depth), SHORT)] * near,
        compiler_params=kernel_params(1),
        cost_estimate=NO_COST,
    )(chunks.astype(jnp.int32), *waits, grad_values, in_weight, *[held for held, _ in flat])


def shifted(array, axis, shift):
    size = lax.axis_size(axis)
    return lax.ppermute(array, axis, [(at, (at + shift) % size) for at in range(size)])


def pick(array, index, axis=0):
    return lax.dynamic_index_in_dim(array, index, axis, keepdims=False)


def turned(parts, start):
    count = len(parts)
    backwards = jnp.stack(parts[::-1])
    doubled = jnp.concatenate([backwards, backwards], axis=0)
    return lax.dynamic_slice_in_dim(doubled, (count - 1 - start) % count, count, 0)


def per_device(tokens, in_weight, filters, gate, cotangent):
    outer, inner, far, near = (lax.axis_size(a) for a in ("outer", "inner", "far", "near"))
    at_outer, at_inner, at_far, at_near = (lax.axis_index(a) for a in ("outer", "inner", "far", "near"))
    tp = far * near
    at_tp = at_far * near + at_near
    rows, columns = tokens.shape
    fine_rows = rows // tp
    halves = 2 if fine_rows >= 32 else 1
    half_rows = fine_rows // halves
    ctx = ("outer", "inner")
    ctx_size = outer * inner
    cell = ("outer", "far", "near")
    split = tp // outer
    depth, width = in_weight.shape
    channels = width // ctx_size
    tile_blocks = columns // depth
    length = ctx_size * rows
    back_inner = [(at_inner - i) % inner for i in range(inner)]

    def destination(source_outer, source_tp, step):
        part = (source_outer * split + source_tp % split + step) % tp
        return (source_tp // split) * tp + part

    chunks = [(at_outer - s) % outer for s in range(outer)]
    order = [s % outer for s in range(1, outer + 1)]
    received = [[None] * outer for _ in range(1, inner)]
    arrivals = []

    def send_chunks(some, waits):
        sent = chunks_of(in_weight, [chunks[s] for s in some], outer, waits)
        arrivals.append([shifted(sent, "inner", i) for i in range(1, inner)])
        for i in range(1, inner):
            for at, s in enumerate(some):
                received[i - 1][s] = (arrivals[-1][i - 1], at)
        return sent

    moved = []
    if split == 1:
        by_far = tokens.reshape(far, near * fine_rows, columns)
        by_far = [pick(by_far, (at_far + f) % far) for f in range(far)]
        sent = send_chunks(order[:2], by_far[1:])
        prepared = prepare(filters, gate, cotangent, ctx_size, [sent])
        held = [by_far[0]] + [shifted(by_far[f], "far", f) for f in range(1, far)]
        held = jnp.stack(held).reshape(far, near, fine_rows, columns)
        for step in range(tp):
            pairs = []
            for o in range(outer):
                for g in range(far):
                    for c in range(near):
                        tile, part = (o + step) % tp // near, (o + step) % tp % near
                        pairs.append(((o * far + g) * near + c, ((tile * near + c) * far + g) * near + part))
            number = (at_outer + step) % tp
            part = lax.dynamic_slice(
                held, ((at_far - number // near) % far, number % near, 0, 0), (1, 1, fine_rows, columns)
            )
            moved.append(lax.ppermute(part.reshape(fine_rows, columns), cell, pairs))
        token_part = join(moved, [prepared, *arrivals[0]])
    else:
        sent = send_chunks(order[:2], [])
        prepared = prepare(filters, gate, cotangent, ctx_size, [sent])
        row_parts = tokens.reshape(tp, fine_rows, columns)
        for step in range(tp):
            pairs = [(o * tp + t, destination(o, t, step)) for o in range(outer) for t in range(tp)]
            part = (at_outer * split + at_tp % split + step) % tp
            moved.append(lax.ppermute(pick(row_parts, part), cell, pairs))
        token_part = turned(moved, at_tp).reshape(outer, split, fine_rows, columns).swapaxes(1, 2)
        token_part = token_part.reshape(outer * fine_rows, split * columns)

    channel_rows = lax.all_to_all(release(prepared, [token_part]), ctx, split_axis=0, concat_axis=0, tiled=True)
    sent = send_chunks(order[2:], [token_part, *arrivals[0]])
    table = transform_table(length)

    pieces = [token_part] + [shifted(token_part, "far", f) for f in range(1, far)]
    pieces = pieces + [shifted(piece, "near", n) for n in range(1, near) for piece in pieces]
    places = []
    for n in range(near):
        for f in range(far):
            source_near = (at_near - n) % near
            source = (at_far - f) % far * near + source_near
            for s in range(outer):
                source_outer = (source_near - s) % outer if split == 1 else s
                places.append(source_outer * (inner * tp) + source)
    places = jnp.stack(places).astype(jnp.int32)
    places = jnp.stack([places + back_inner[s] * tp for s in range(inner)])

    blocks = jnp.stack(back_inner)
    turn = at_outer // near * near if split == 1 else 0
    row_order = jnp.stack([(s + turn) % outer + at_outer * 0 for s in range(outer)])
    running = None
    waits = [sent]
    for s in order:
        if running is not None:
            running = shifted(running, "outer", 1)
        held = [chunk[s] for chunk in received]
        running = product(pieces, in_weight, chunks[s], held, blocks, row_order, running, s == 0, waits)
        waits = []
        if s == outer - 2:
            grad_values, spectrum = correlate(table, rotation(length), channel_rows, [running])
            by_inner = grad_values.reshape(outer, inner, rows, channels)
            grad_parts = [pick(by_inner, at_inner, 1)]
            for i in range(1, inner):
                grad_parts.append(shifted(pick(by_inner, (at_inner + i) % inner, 1), "inner", i))
            waits = [spectrum]
        if s == outer - 1:
            sources = [(at_far + f) % far * near + (at_near + n) % near for n in range(near) for f in range(far)]
            arranged = arrange(
                grad_parts, jnp.stack(back_inner), jnp.stack(sources), (outer, inner, far, near, halves, half_rows), [running]
            )
            gathered = lax.all_gather(arranged, "outer", axis=0, tiled=False)
            waits = [arranged]
    value_parts = [running[0]] + [shifted(running[i], "inner", i) for i in range(1, inner)]

    convolved = convolve(table, spectrum, value_parts, places, []).reshape(ctx_size, rows, channels)
    exchanged = lax.all_to_all(convolved, ctx, split_axis=0, concat_axis=0, tiled=True)

    sent_back = []
    waits = [convolved]
    for half in range(halves):
        by_near = shares(gathered, half, in_weight, received, jnp.stack(chunks), near, waits)
        total = by_near[0].astype(WIDE) + sum(shifted(by_near[n], "near", n).astype(WIDE) for n in range(1, near))
        total = total.astype(SHORT).reshape(inner, far, outer * half_rows, depth)
        waits = [total]
        others = [shifted(total[:, f], "far", f) for f in range(1, far)]
        total = total[:, 0].astype(WIDE) + sum(other.astype(WIDE) for other in others)
        total = total.astype(SHORT).reshape(inner, outer, half_rows, depth)
        if split == 1:
            total = total.swapaxes(0, 1)
        else:
            total = turned(list(total), at_inner).reshape(split, tile_blocks, outer, half_rows, depth)
            total = total.transpose(2, 0, 1, 3, 4).reshape(tp, tile_blocks, half_rows, depth)
        back = []
        for step in range(tp):
            pairs = [(destination(o, t, step), o * tp + t) for o in range(outer) for t in range(tp)]
            back.append(lax.ppermute(pick(total, (at_tp - step) % tp), cell, pairs))
        sent_back.append(back)
    row_places = [(at_outer * split + at_tp % split + step) % tp for step in range(tp)]
    block_places = back_inner if split == 1 else [jnp.int32(b) for b in range(tile_blocks)]
    grad_tokens = assemble(sent_back, jnp.stack(row_places), jnp.stack(block_places), columns)

    gated_output, grad_gate = finish(exchanged, gate, cotangent)
    return (gated_output, grad_gate, grad_tokens)


def solution(mesh):
    ctx_size, tp_size = mesh.shape["ctx"], mesh.shape["tp"]
    inner, near = 1, 2
    while inner * inner * 4 <= ctx_size:
        inner *= 2
    fine_mesh = Mesh(
        np.asarray(mesh.devices).reshape(ctx_size // inner, inner, tp_size // near, near),
        ("outer", "inner", "far", "near"),
    )
    placed = P(("outer", "inner"), ("far", "near"))
    return jax.shard_map(
        per_device,
        mesh=fine_mesh,
        in_specs=(placed,) * 5,
        out_specs=(placed,) * 3,
        check_vma=False,
    )
```
